32 devices in a mesh: dp: 8 (over y, x, core), tensor: 4 (over z).
Axes of the slice: x: 2, y: 2, z: 4, core: 2. Of those that a mesh axis runs over, the one named last changes fastest.
Arguments:
- tokens_in: bfloat16 [8192, 768], P('dp'), may hold values from -6 to 6
- patch_mask: int32 [8192], P('dp'), may hold values 0 or 1
- image_ids: int32 [8192], P('dp'), may hold values from 0 to 10, as said below
- mask_token: float32 [768], replicated, may hold values from -6 to 6
- norm1_gain: float32 [2, 768], replicated, may hold values from 0.5 to 1.5
- norm1_bias: float32 [2, 768], replicated, may hold values from -1.75 to 1.75
- qkv_weight: bfloat16 [2, 768, 3, 768], P(None, None, None, 'tensor'), may hold values from -0.21875 to 0.21875
- qv_bias: float32 [2, 2, 768], P(None, None, 'tensor'), may hold values from -1.75 to 1.75
- out_weight: bfloat16 [2, 768, 768], P(None, 'tensor'), may hold values from -0.625 to 0.625
- out_bias: float32 [2, 768], replicated, may hold values from -1.75 to 1.75
- norm2_gain: float32 [2, 768], replicated, may hold values from 0.5 to 1.5
- norm2_bias: float32 [2, 768], replicated, may hold values from -1.75 to 1.75
- up_weight: bfloat16 [2, 768, 3072], P(None, None, 'tensor'), may hold values from -0.21875 to 0.21875
- up_bias: float32 [2, 3072], P(None, 'tensor'), may hold values from -1.75 to 1.75
- down_weight: bfloat16 [2, 3072, 768], P(None, 'tensor'), may hold values from -0.109375 to 0.109375
- down_bias: float32 [2, 768], replicated, may hold values from -1.75 to 1.75
- out_grad: float32 [8192, 768], P('dp'), may hold values from -6 to 6
Outputs:
- activations: float32 [8192, 768], P('dp')
- tokens_grad: float32 [8192, 768], P('dp')
- mask_token_grad: float32 [768], replicated
- norm1_gain_grad: float32 [2, 768], replicated
- norm1_bias_grad: float32 [2, 768], replicated
- qkv_weight_grad: float32 [2, 768, 3, 768], P(None, None, None, 'tensor')
- qv_bias_grad: float32 [2, 2, 768], P(None, None, 'tensor')
- out_weight_grad: float32 [2, 768, 768], P(None, 'tensor')
- out_bias_grad: float32 [2, 768], replicated
- norm2_gain_grad: float32 [2, 768], replicated
- norm2_bias_grad: float32 [2, 768], replicated
- up_weight_grad: float32 [2, 768, 3072], P(None, None, 'tensor')
- up_bias_grad: float32 [2, 3072], P(None, 'tensor')
- down_weight_grad: float32 [2, 3072, 768], P(None, 'tensor')
- down_bias_grad: float32 [2, 768], replicated
The draws below stay inside these ranges and needn't reach their ends.
Inputs may be any that keep to these rules, and one draw needn't show every extreme that they name: `image_ids`: on each dp index the rows hold whole images of 100, 196 or 400 patches one after another, numbered 0, 1, 2 and so on; the rows left after the last whole image carry the next number and form one group of their own. On some dp index every image has 100 patches.
All inputs are finite; a program needn't handle non-finite values. No bound on the sum of `patch_mask` on one device may be relied on, other than what follows from the above.
Results may differ from the reference program's by a relative error of at most 0.033.
Values may be sent and summed in bfloat16 or wider, within the bound.
No kernel may reach another device: no remote copies, remote signals or barrier semaphores. Data moves between devices by JAX's collectives and lax.ppermute only.
A program may use at most 128 MiB of HBM per device.

```python
import jax
import jax.numpy as jnp
from jax import lax

D = 768
FF = 3072
HD = 64
LAYERS = 2
TOK_DEV = 1024
P_SMALL = 100
P_MID = 196
P_BIG = 400
TOKENS = 8192


def draw_image_ids(key, part):
    key = jax.random.fold_in(key, 17)
    packs = TOKENS // TOK_DEV
    most_images = TOK_DEV // P_SMALL + 1
    chosen_pack = jax.random.randint(jax.random.fold_in(key, 23), (), 0, packs).astype(jnp.int32)

    def one_pack(pack_key, pack_number):
        picked = jax.random.randint(pack_key, (most_images,), 0, 3)
        picked = jnp.where(pack_number == chosen_pack, 0, picked)
        image_sizes = jnp.where(picked == 0, P_SMALL, jnp.where(picked == 1, P_MID, P_BIG)).astype(jnp.int32)
        image_ends = jnp.cumsum(image_sizes).astype(jnp.int32)
        image_ends = jnp.where(image_ends <= TOK_DEV, image_ends, TOK_DEV + 1)
        row_index = jnp.arange(TOK_DEV, dtype=jnp.int32)
        return jnp.sum((image_ends[None, :] <= row_index[:, None]).astype(jnp.int32), axis=1)
    pack_keys = jax.random.split(key, packs)
    pack_numbers = jnp.arange(packs, dtype=jnp.int32)
    return jax.vmap(one_pack)(pack_keys, pack_numbers).reshape(TOKENS).astype(jnp.int32)


def place_ends(array, key, low, largest):
    index_at = [jax.random.randint(jax.random.fold_in(key, axis), (), 0, length) for axis, length in enumerate(array.shape)]
    longest = array.shape.index(max(array.shape))
    next_to = index_at[:longest] + [(index_at[longest] + 1) % array.shape[longest]] + index_at[longest + 1:]
    return array.at[tuple(index_at)].set(low).at[tuple(next_to)].set(largest)


def block_scale(rng, shape, pieces, low, top_value):
    def one(axis_at, shards_of):
        draws = jax.random.uniform(jax.random.fold_in(jax.random.fold_in(rng, 6), axis_at), (shards_of,), jnp.float32, low / len(pieces), top_value / len(pieces))
        return jnp.repeat(jnp.exp(draws), shape[axis_at] // shards_of).reshape((-1,) + (1,) * (len(shape) - axis_at - 1))

    level = one(*pieces[0])
    for cut in pieces[1:]:
        level = level * one(*cut)
    return level


def normal_values(stream_key, shape, width, limit, cuts=(), kind=jnp.bfloat16):
    array = width * jax.random.normal(stream_key, shape, jnp.float32)
    if cuts:
        array = array * block_scale(stream_key, shape, cuts, -0.22, 0.18)
    return jnp.clip(array, -limit, limit).astype(kind)


def setup_inputs(seed: int = 0) -> dict:
    streams_of = jax.random.split(jax.random.key(seed), 18)
    return {
        "tokens_in": normal_values(streams_of[0], (TOKENS, D), 1.0, 6.0, ((0, 8),)),
        "patch_mask": place_ends((jax.random.randint(streams_of[1], (TOKENS,), 0, 5) < 2).astype(jnp.int32), jax.random.fold_in(streams_of[1], 1), 0, 1),
        "image_ids": draw_image_ids(jax.random.fold_in(streams_of[17], 71), 0),
        "mask_token": normal_values(streams_of[3], (D,), 1.0, 6.0, (), jnp.float32),
        "norm1_gain": jnp.clip(1.0 + 0.1 * jax.random.normal(streams_of[4], (LAYERS, D), jnp.float32), 0.5, 1.5),
        "norm1_bias": normal_values(streams_of[5], (LAYERS, D), 0.3, 1.75, (), jnp.float32),
        "qkv_weight": normal_values(streams_of[6], (LAYERS, D, 3, D), D ** -0.5, 0.21875, ((3, 4),)),
        "qv_bias": normal_values(streams_of[7], (LAYERS, 2, D), 0.3, 1.75, ((2, 4),), jnp.float32),
        "out_weight": normal_values(streams_of[8], (LAYERS, D, D), (D // 8) ** -0.5, 0.625, ((1, 4),)),
        "out_bias": normal_values(streams_of[9], (LAYERS, D), 0.3, 1.75, (), jnp.float32),
        "norm2_gain": jnp.clip(1.0 + 0.1 * jax.random.normal(streams_of[10], (LAYERS, D), jnp.float32), 0.5, 1.5),
        "norm2_bias": normal_values(streams_of[11], (LAYERS, D), 0.3, 1.75, (), jnp.float32),
        "up_weight": normal_values(streams_of[12], (LAYERS, D, FF), D ** -0.5, 0.21875, ((2, 4),)),
        "up_bias": normal_values(streams_of[13], (LAYERS, FF), 0.3, 1.75, ((1, 4),), jnp.float32),
        "down_weight": normal_values(streams_of[14], (LAYERS, FF, D), FF ** -0.5, 0.109375, ((1, 4),)),
        "down_bias": normal_values(streams_of[15], (LAYERS, D), 0.3, 1.75, (), jnp.float32),
        "out_grad": normal_values(streams_of[16], (TOKENS, D), 1.0, 6.0, ((0, 8),), jnp.float32),
    }


@jax.custom_vjp
def low(v):
    return lax.optimization_barrier(v.astype(jnp.bfloat16)).astype(jnp.float32)

@jax.custom_vjp
def low_back(v):
    return v

def low_keep(v):
    return (low(v), None)

def low_pass(kept, grad):
    return (grad,)

def back_keep(v):
    return (v, None)

def back_low(kept, grad):
    return (low(grad),)
low.defvjp(low_keep, low_pass)
low_back.defvjp(back_keep, back_low)
HIGH = lax.Precision.HIGHEST
EPSILON = 1e-06
MASKED = -1e+30

def both_round(value_in):
    return low(low_back(value_in))

def layer_norm(rows_in, gain_row, shift_row):
    centre = rows_in - lax.optimization_barrier(jnp.mean(rows_in, axis=-1, keepdims=True))
    spread = lax.optimization_barrier(jnp.mean(centre * centre, axis=-1, keepdims=True))
    return centre * lax.rsqrt(spread + EPSILON) * gain_row + shift_row

def attention(queries, key_rows, value_rows, same_image):
    score_scale = HD ** (-0.5)
    scores = low_back(jnp.einsum('qhd,khd->hqk', queries, key_rows, precision=HIGH) * score_scale)
    scores = jnp.where(same_image[None], scores, MASKED)
    row_max = lax.optimization_barrier(jnp.max(scores, axis=-1, keepdims=True))
    expo_scores = jnp.exp(scores - row_max)
    probs_all = expo_scores / lax.optimization_barrier(jnp.sum(expo_scores, axis=-1, keepdims=True))
    return jnp.einsum('hqk,khd->qhd', low(probs_all), value_rows, precision=HIGH)

def block_layer(rows_in, params, same_image):
    gain1, shift1, w_qkv, bias_qv, w_out, bias_out, gain2, shift2, w_up, bias_up, w_down, bias_down = params
    row_count = rows_in.shape[0]
    head_count = D // HD
    normed = low(layer_norm(rows_in, gain1, shift1))
    projected = jnp.einsum('rd,dcf->rcf', normed, w_qkv, precision=HIGH)
    queries = both_round(projected[:, 0] + bias_qv[0]).reshape(row_count, head_count, HD)
    key_rows = both_round(projected[:, 1]).reshape(row_count, head_count, HD)
    value_rows = both_round(projected[:, 2] + bias_qv[1]).reshape(row_count, head_count, HD)
    attended = both_round(attention(queries, key_rows, value_rows, same_image).reshape(row_count, D))
    middle = rows_in + low_back(jnp.dot(attended, w_out, precision=HIGH)) + bias_out
    normed_mid = low(layer_norm(middle, gain2, shift2))
    before_act = low_back(jnp.dot(normed_mid, w_up, precision=HIGH) + bias_up)
    hidden = low(jax.nn.gelu(before_act, approximate=False))
    return middle + low_back(jnp.dot(hidden, w_down, precision=HIGH)) + bias_down

def forward(token_rows, token_fill, params, masked_rows, same_image):
    residual = jnp.where(masked_rows[:, None], token_fill[None, :], token_rows)
    for layer_at in range(LAYERS):
        residual = block_layer(residual, tuple((weight[layer_at] for weight in params)), same_image)
    return residual

def reference(tokens_in, patch_mask, image_ids, mask_token, norm1_gain, norm1_bias, qkv_weight, qv_bias, out_weight, out_bias, norm2_gain, norm2_bias, up_weight, up_bias, down_weight, down_bias, out_grad):
    params = tuple((weight.astype(jnp.float32) for weight in (norm1_gain, norm1_bias, qkv_weight, qv_bias, out_weight, out_bias, norm2_gain, norm2_bias, up_weight, up_bias, down_weight, down_bias)))
    packs = TOKENS // TOK_DEV
    token_packs = tokens_in.astype(jnp.float32).reshape(packs, TOK_DEV, D)
    mask_packs = (patch_mask == 1).reshape(packs, TOK_DEV)
    id_packs = image_ids.reshape(packs, TOK_DEV)
    cotangent_packs = out_grad.reshape(packs, TOK_DEV, D)
    token_fill = mask_token.astype(jnp.float32)
    start_totals = (jnp.zeros_like(token_fill), tuple((jnp.zeros_like(weight) for weight in params)))

    def one_pack(running, pack_item):
        token_rows, masked_rows, pack_ids, cotangent = pack_item
        same_image = pack_ids[:, None] == pack_ids[None, :]

        def local_forward(rows_value, fill_value, param_value):
            return forward(rows_value, fill_value, param_value, masked_rows, same_image)
        result, pull_back = jax.vjp(local_forward, token_rows, token_fill, params)
        grad_rows, grad_fill, grad_params = pull_back(cotangent)
        running = (running[0] + grad_fill, jax.tree.map(jnp.add, running[1], grad_params))
        return (running, (result, grad_rows))
    grad_totals, (results, grad_tokens) = lax.scan(one_pack, start_totals, (token_packs, mask_packs, id_packs, cotangent_packs))
    weight_grads = grad_totals[1]
    return (results.reshape(TOKENS, D), grad_tokens.reshape(TOKENS, D), grad_totals[0], weight_grads[0], weight_grads[1], weight_grads[2], weight_grads[3], weight_grads[4], weight_grads[5], weight_grads[6], weight_grads[7], weight_grads[8], weight_grads[9], weight_grads[10], weight_grads[11])
```

```python
from functools import partial

import jax
import jax.numpy as jnp
from jax import lax
from jax.experimental import pallas as pl
from jax.experimental.pallas import tpu as pltpu
from jax.sharding import PartitionSpec as P

AXES = ("dp", "tensor")
HD = 64
WIDE = jnp.float32
NARROW = jnp.bfloat16
EPSILON = 1e-06
MASKED = -1e30
NN = ((1,), (0,))
NT = ((1,), (1,))
TN = ((0,), (0,))


def dot(a, b, dims=NN):
    return lax.dot_general(a, b, (dims, ((), ())), preferred_element_type=WIDE)


def call(kernel, outs, *args, scratch=(), flops=0, exps=0):
    size = lambda x: x.size * x.dtype.itemsize
    moved = sum(size(x) for x in args) + sum(size(x) for x in outs)
    return pl.pallas_call(
        kernel,
        out_shape=outs,
        in_specs=[pl.BlockSpec(memory_space=pltpu.VMEM)] * len(args),
        out_specs=[pl.BlockSpec(memory_space=pltpu.VMEM)] * len(outs),
        scratch_shapes=list(scratch),
        compiler_params=pltpu.CompilerParams(vmem_limit_bytes=48 * 2**20),
        cost_estimate=pl.CostEstimate(flops=flops, bytes_accessed=moved, transcendentals=exps),
    )(*args)


def shape(s, kind=NARROW):
    return jax.ShapeDtypeStruct(s, kind)


def attend_rows(qkv_ref, at, ids_col, ids_row, q_rows, width):
    same = ids_col == ids_row
    bias = jnp.where(same, 0.0, MASKED)
    outs, lses = [], []
    for head in range(width // HD):
        cols = slice(head * HD, head * HD + HD)
        q = qkv_ref[pl.ds(at, q_rows), cols]
        k = qkv_ref[:, width + head * HD : width + head * HD + HD]
        v = qkv_ref[:, 2 * width + head * HD : 2 * width + head * HD + HD]
        s = dot(k, q * jnp.asarray(HD**-0.5, NARROW), NT) + bias
        top = jnp.max(s, axis=0, keepdims=True)
        e = jnp.exp(s - top)
        total = jnp.sum(e, axis=0, keepdims=True)
        o = dot(e.astype(NARROW), v, TN)
        o = o * jnp.transpose(1.0 / total)
        outs.append(o)
        lses.append(top + jnp.log(total))
    return jnp.concatenate(outs, axis=1), jnp.concatenate(lses, axis=0)


def qkv_kernel(mine_ref, other_ref, w_ref, b_ref, out_ref):
    half = mine_ref.shape[0]
    for ref, at in ((mine_ref, 0), (other_ref, half)):
        for r in range(0, half, 256):
            y = dot(ref[r : r + 256, :], w_ref[...]) + b_ref[...]
            out_ref[at + r : at + r + 256, :] = y.astype(NARROW)


def make_attn_fwd(q0, q1, width, block):
    def kernel(qkv_ref, idc_ref, idr_ref, w_ref, att_ref, lse_ref, part_ref):
        def step(i, _):
            at = pl.multiple_of(q0 + i * block, block)
            o, lse = attend_rows(
                qkv_ref, at, idc_ref[...], idr_ref[:, pl.ds(at, block)], block, width
            )
            low = o.astype(NARROW)
            r = pl.multiple_of(i * block, block)
            att_ref[pl.ds(r, block), :] = low
            lse_ref[:, pl.ds(r, block)] = lse
            part_ref[pl.ds(r, block), :] = dot(low, w_ref[...], NT).astype(NARROW)
            return 0

        lax.fori_loop(0, (q1 - q0) // block, step, 0)

    return kernel


def stats(x):
    mean = jnp.mean(x, axis=-1, keepdims=True)
    centre = x - mean
    spread = jnp.mean(centre * centre, axis=-1, keepdims=True)
    return centre, lax.rsqrt(spread + EPSILON)


def norm_kernel(x_ref, a_ref, b_ref, bias_ref, gain_ref, shift_ref, h_ref, n_ref):
    for r in range(0, x_ref.shape[0], 128):
        rows = slice(r, r + 128)
        h = x_ref[rows, :] + (a_ref[rows, :].astype(WIDE) + b_ref[rows, :].astype(WIDE)) + bias_ref[...]
        h_ref[rows, :] = h
        centre, inv = stats(h)
        n_ref[rows, :] = (centre * inv * gain_ref[...] + shift_ref[...]).astype(NARROW)


def fold(x):
    return jnp.sum(x.reshape(x.shape[0] // 8, 8, x.shape[1]), axis=0)


def make_norm_back(last):
    def kernel(g_ref, a_ref, b_ref, x_ref, gain_ref, *refs):
        if last:
            mask_ref, low_ref, sums_ref = refs
        else:
            out_ref, low_ref, sums_ref = refs
        half, d = x_ref.shape
        gain_sum = jnp.zeros((8, d), WIDE)
        shift_sum = jnp.zeros((8, d), WIDE)
        out_sum = jnp.zeros((8, d), WIDE)
        for r in range(0, half, 64):
            rows = slice(r, r + 64)
            gn = a_ref[rows, :].astype(WIDE) + b_ref[rows, :].astype(WIDE)
            centre, inv = stats(x_ref[rows, :])
            xhat = centre * inv
            e = gn * gain_ref[...]
            mean_e = jnp.mean(e, axis=-1, keepdims=True)
            mean_ex = jnp.mean(e * xhat, axis=-1, keepdims=True)
            out = g_ref[rows, :] + inv * (e - mean_e - xhat * mean_ex)
            if last:
                masked = mask_ref[rows, :] == 1
                low_ref[rows, :] = jnp.where(masked, 0.0, out).astype(NARROW)
                out = jnp.where(masked, out, 0.0)
            else:
                out_ref[rows, :] = out
                low_ref[rows, :] = out.astype(NARROW)
            gain_sum += fold(gn * xhat)
            shift_sum += fold(gn)
            out_sum += fold(out)
        total = lambda x: jnp.sum(x, axis=0, keepdims=True)
        sums = [total(gain_sum), total(shift_sum), total(out_sum)]
        if last:
            sums_ref[...] = jnp.concatenate(sums + [jnp.zeros((5, d), WIDE)], axis=0)
        else:
            sums_ref[...] = jnp.concatenate(sums + [jnp.zeros((5, d), WIDE)], axis=0)
            low_ref[half:, :] = jnp.concatenate(sums + [jnp.zeros((13, d), WIDE)], axis=0).astype(NARROW)

    return kernel


def cast_kernel(g_ref, low_ref):
    half, d = g_ref.shape
    total = jnp.zeros((8, d), WIDE)
    for r in range(0, half, 64):
        g = g_ref[r : r + 64, :]
        low_ref[r : r + 64, :] = g.astype(NARROW)
        total += fold(g)
    zero = jnp.zeros((1, d), WIDE)
    sums = [zero, zero, jnp.sum(total, axis=0, keepdims=True), jnp.zeros((13, d), WIDE)]
    low_ref[half:, :] = jnp.concatenate(sums, axis=0).astype(NARROW)


def first_kernel(x_ref, mask_ref, fill_ref, gain_ref, shift_ref, h_ref, n_ref):
    for r in range(0, x_ref.shape[0], 128):
        rows = slice(r, r + 128)
        h = jnp.where(mask_ref[rows, :] == 1, fill_ref[...], x_ref[rows, :].astype(WIDE))
        h_ref[rows, :] = h
        centre, inv = stats(h)
        n_ref[rows, :] = (centre * inv * gain_ref[...] + shift_ref[...]).astype(NARROW)


ERF = (0.254829592, -0.284496736, 1.421413741, -1.453152027, 1.061405429)


def gelu_and_slope(x):
    bell = jnp.exp(x * x * -0.5)
    t = 1.0 / (1.0 + (0.3275911 * 0.7071067811865476) * jnp.abs(x))
    tail = t * (ERF[0] + t * (ERF[1] + t * (ERF[2] + t * (ERF[3] + t * ERF[4]))))
    tail = 0.5 * (tail * bell)
    phi = jnp.where(x < 0.0, tail, 1.0 - tail)
    return x * phi, phi + x * (0.3989422804014327 * bell)


def mlp_kernel(n_ref, up_ref, bias_ref, down_ref, hid_ref, slope_ref, part_ref):
    for r in range(0, n_ref.shape[0], 256):
        rows = slice(r, r + 256)
        for f in range(0, up_ref.shape[1], 256):
            cols = slice(f, f + 256)
            x = dot(n_ref[rows, :], up_ref[:, cols]) + bias_ref[:, cols]
            y, slope = gelu_and_slope(x)
            hid_ref[rows, cols] = y.astype(NARROW)
            slope_ref[rows, cols] = slope.astype(NARROW)
        part_ref[rows, :] = dot(hid_ref[rows, :], down_ref[...]).astype(NARROW)


def mlp_back_kernel(g_ref, down_ref, slope_ref, up_ref, gb_ref, part_ref, sum_ref):
    total = jnp.zeros((8, down_ref.shape[0]), WIDE)
    for r in range(0, gb_ref.shape[0], 256):
        rows = slice(r, r + 256)
        dh = dot(g_ref[rows, :], down_ref[...], NT)
        gb = (dh * slope_ref[rows, :].astype(WIDE)).astype(NARROW)
        gb_ref[rows, :] = gb
        total += fold(gb.astype(WIDE))
        part_ref[rows, :] = dot(gb, up_ref[...], NT).astype(NARROW)
    sum_ref[...] = jnp.broadcast_to(jnp.sum(total, axis=0, keepdims=True), sum_ref.shape)


def pair_grad_kernel(am_ref, ao_ref, bm_ref, bo_ref, out_ref):
    for f in range(0, out_ref.shape[0], 192):
        cols = slice(f, f + 192)
        half = am_ref.shape[0]
        y = dot(am_ref[:, cols], bm_ref[0:half, :], TN) + dot(ao_ref[:, cols], bo_ref[0:half, :], TN)
        out_ref[cols, :] = y.astype(NARROW)


def make_attn_back(width, block):
    heads = width // HD

    def kernel(gm_ref, go_ref, w_ref, qkv_ref, att_m_ref, att_o_ref, lse_m_ref, lse_o_ref, idc_ref, idr_ref,
               wq_ref, d_ref, sum_ref, part_m_ref, part_o_ref, ga_ref, dqt_ref, dd_ref):
        rows = qkv_ref.shape[0]
        half = rows // 2
        for ref, att, at in ((gm_ref, att_m_ref, 0), (go_ref, att_o_ref, half)):
            ga = dot(ref[0:half, :], w_ref[...]).astype(NARROW)
            ga_ref[at : at + half, :] = ga
            x = ga.astype(WIDE) * att[...].astype(WIDE)
            per = [jnp.sum(x[:, HD * i : HD * i + HD], axis=1, keepdims=True) for i in range(heads)]
            per = jnp.concatenate(per + [jnp.zeros((half, 128 - heads), WIDE)], axis=1)
            dd_ref[:, at : at + half] = jnp.transpose(per)[0:8]
        dqt_ref[...] = jnp.zeros_like(dqt_ref)
        lse = jnp.concatenate([lse_m_ref[...], lse_o_ref[...]], axis=1)

        def step(i, _):
            at = pl.multiple_of(i * block, block)
            bias = jnp.where(idc_ref[pl.ds(at, block), :] == idr_ref[...], 0.0, MASKED)
            dks, dvs = [], []
            for head in range(heads):
                cols = slice(head * HD, head * HD + HD)
                q = qkv_ref[:, cols]
                k = qkv_ref[pl.ds(at, block), width + head * HD : width + head * HD + HD]
                v = qkv_ref[pl.ds(at, block), 2 * width + head * HD : 2 * width + head * HD + HD]
                ga = ga_ref[:, cols]
                scaled = k * jnp.asarray(HD**-0.5, NARROW)
                p = jnp.exp(dot(scaled, q, NT) + bias - lse[head : head + 1, :])
                dvs.append(dot(p.astype(NARROW), ga))
                ds = (p * (dot(v, ga, NT) - dd_ref[head : head + 1, :])).astype(NARROW)
                dks.append(dot(ds, q) * HD**-0.5)
                dqt_ref[cols, :] += dot(scaled, ds, TN)
            d_ref[pl.ds(at, block), width : 2 * width] = jnp.concatenate(dks, axis=1).astype(NARROW)
            d_ref[pl.ds(at, block), 2 * width :] = jnp.concatenate(dvs, axis=1).astype(NARROW)
            return 0

        lax.fori_loop(0, rows // block, step, 0)
        d_ref[:, :width] = jnp.transpose(dqt_ref[...]).astype(NARROW)
        sum_ref[...] = jnp.broadcast_to(jnp.sum(d_ref[...].astype(WIDE), axis=0, keepdims=True), sum_ref.shape)
        for ref, at in ((part_o_ref, half), (part_m_ref, 0)):
            ref[...] = dot(d_ref[at : at + half, :], wq_ref[...], NT).astype(NARROW)

    return kernel


class Layout:
    def __init__(self, mesh):
        self.pairs = mesh.shape["dp"] // 2
        self.tensor = mesh.shape["tensor"]
        self.lowers = self.tensor // 2
        self.everyone = [
            (k, c, h, l)
            for k in range(self.pairs)
            for c in range(2)
            for h in range(2)
            for l in range(self.lowers)
        ]
        self.same = [a for a in self.everyone if a[1] == a[2]]
        self.cross = [a for a in self.everyone if a[1] != a[2]]

    def place(self, k, c, h, l):
        return (2 * k + c) * self.tensor + self.lowers * h + l

    def send(self, value, among, where):
        perm = [(self.place(*a), self.place(*where(*a))) for a in among]
        return lax.ppermute(value, AXES, perm)

    def to_core(self, value):
        return self.send(value, self.everyone, lambda k, c, h, l: (k, 1 - c, h, l))

    def to_lower(self, value):
        return self.send(value, self.everyone, lambda k, c, h, l: (k, c, h, 1 - l))


def here(lay):
    at = lax.axis_index("dp")
    z = lax.axis_index("tensor")
    return at // 2, at % 2, z // lay.lowers, z % lay.lowers


def in_order(pieces, number):
    pieces = list(pieces)
    bit = 1
    while bit < len(pieces):
        swap = (number & bit) != 0
        pieces = [jnp.where(swap, pieces[i ^ bit], pieces[i]) for i in range(len(pieces))]
        bit *= 2
    return pieces


def block(value, number, count):
    size = value.shape[0] // count
    return lax.dynamic_slice_in_dim(value, number * size, size, 0)


def among_pairs(lay, piece, among):
    k = here(lay)[0]
    pieces = [piece] + [
        lay.send(piece, among, lambda k, c, h, l, j=j: (k ^ j, c, h, l))
        for j in range(1, lay.pairs)
    ]
    return in_order(pieces, k)


def fetch(lay, natives):
    k, c, h, l = here(lay)
    mine = jnp.concatenate([block(w, k, lay.pairs) for w in natives], axis=1)
    got = lay.send(mine, lay.cross, lambda k, c, h, l: (k, 1 - c, 1 - h, l))
    pieces = among_pairs(lay, got, lay.cross)
    out, at = [], 0
    for w in natives:
        width = w.shape[1]
        whole = jnp.concatenate([p[:, at : at + width] for p in pieces], axis=0)
        out.append(jnp.where(c == h, w, whole))
        at += width
    return out


def total_grads(lay, grads):
    k, c, h, l = here(lay)
    cut = lambda number: jnp.concatenate([block(x, number, lay.pairs) for x in grads], axis=0)
    mine = cut(k).astype(WIDE)
    for j in range(1, lay.pairs):
        mine = mine + lay.send(
            cut(k ^ j), lay.everyone, lambda k, c, h, l, j=j: (k ^ j, c, h, l)
        ).astype(WIDE)
    mine = mine.astype(NARROW)
    got = lay.send(mine, lay.cross, lambda k, c, h, l: (k, c, 1 - h, l))
    mine = (mine.astype(WIDE) + got.astype(WIDE)).astype(NARROW)
    whole = jnp.stack(among_pairs(lay, mine, lay.same))
    other = lay.send(whole, lay.same, lambda k, c, h, l: (k, 1 - c, h, l))
    whole = jnp.where(c == h, whole, other)
    out, at = [], 0
    for x in grads:
        size = x.shape[0] // lay.pairs
        out.append(whole[:, at : at + size].reshape(x.shape))
        at += size
    return out


def total_small(lay, value):
    bits = [lambda k, c, h, l, j=1 << b: (k ^ j, c, h, l) for b in range(lay.pairs.bit_length() - 1)]
    bits += [lambda k, c, h, l: (k, c, 1 - h, l), lambda k, c, h, l: (k, 1 - c, h, l)]
    for where in bits:
        value = value + lay.send(value, lay.everyone, where)
    return value


def spread(lay, rows):
    k, c, h, l = here(lay)
    part = block(rows, l, lay.lowers)
    halves = [
        lay.send(
            part,
            [a for a in lay.everyone if a[1] == side],
            lambda k, c, h, l: (k, h, 1 - h, l),
        )
        for side in range(2)
    ]
    both = jnp.stack(halves)
    beside = lay.send(both, lay.cross, lambda k, c, h, l: (k, c, h, 1 - l))
    first = jnp.where(l == 0, both, beside)
    second = jnp.where(l == 0, beside, both)
    far = jnp.stack([first, second], axis=1).reshape(2 * rows.shape[0], rows.shape[1])
    other = lay.send(rows, lay.cross, lambda k, c, h, l: (k, 1 - c, h, l))
    near = jnp.concatenate(
        [jnp.where(c == 0, rows, other), jnp.where(c == 0, other, rows)], axis=0
    )
    return jnp.where(c == h, near, far)


def add(a, b):
    return (a.astype(WIDE) + b.astype(WIDE)).astype(NARROW)


def body(
    lay,
    tokens_in,
    patch_mask,
    image_ids,
    mask_token,
    norm1_gain,
    norm1_bias,
    qkv_weight,
    qv_bias,
    out_weight,
    out_bias,
    norm2_gain,
    norm2_bias,
    up_weight,
    up_bias,
    down_weight,
    down_bias,
    out_grad,
):
    k, c, h, l = here(lay)
    near = c == h
    layers, d, _, width = qkv_weight.shape
    hidden_units = up_weight.shape[2]
    rows_all = tokens_in.shape[0]
    half = rows_all // 2
    heads = width // HD
    block_rows = 256

    def swap_rows(native):
        mine = block(native, c, 2)
        got = lay.send(block(native, 1 - c, 2), lay.same, lambda k, c, h, l: (k, 1 - c, h, l))
        return jnp.where(near, mine, got)

    tokens = swap_rows(tokens_in)
    whole = jnp.concatenate([block(patch_mask, 1 - c, 2), image_ids])
    got = lay.send(whole, lay.same, lambda k, c, h, l: (k, 1 - c, h, l))
    masked = jnp.where(near, block(patch_mask, c, 2), got[:half])[:, None]
    ids = jnp.where(near, image_ids, got[half:])
    ids = jnp.concatenate([block(ids, c, 2), block(ids, 1 - c, 2)])
    idc, idr = ids[:, None], ids[None, :]

    natives = [
        (
            qkv_weight[i].reshape(d, 3 * width),
            up_weight[i],
            down_weight[i],
            jnp.transpose(out_weight[i]),
        )
        for i in range(layers)
    ]
    fetched = []
    for i in range(layers):
        if i == 0:
            fetched.append(fetch(lay, natives[i][:1]) + fetch(lay, natives[i][1:]))
        else:
            fetched.append(fetch(lay, natives[i]))
    biases = jnp.concatenate([up_bias, qv_bias.reshape(layers, 2 * width)], axis=1)
    got = lay.send(biases, lay.cross, lambda k, c, h, l: (k, 1 - c, 1 - h, l))
    biases = jnp.where(near, biases, got)
    b_up = [biases[i : i + 1, :hidden_units] for i in range(layers)]
    nothing = jnp.zeros((1, width), WIDE)
    b_qkv = [
        jnp.concatenate(
            [
                biases[i : i + 1, hidden_units : hidden_units + width],
                nothing,
                biases[i : i + 1, hidden_units + width :],
            ],
            axis=1,
        )
        for i in range(layers)
    ]

    rows_f = shape((half, d), WIDE)
    rows_b = shape((half, d))
    rows_u = shape((half, hidden_units))
    h_rows, n1m = call(
        first_kernel, [rows_f, rows_b], tokens, masked, mask_token[None], norm1_gain[:1], norm1_bias[:1]
    )
    kept = []
    activations = None
    for i in range(layers):
        w_qkv, w_up, w_down, w_out = fetched[i]
        n1o = lay.to_core(n1m)
        (qkv,) = call(
            qkv_kernel, [shape((rows_all, 3 * width))], n1m, n1o, w_qkv, b_qkv[i], flops=2 * rows_all * d * 3 * width
        )
        att, lse, part = [None] * 2, [None] * 2, [None] * 2
        for s in (1, 0):
            att[s], lse[s], part[s] = call(
                make_attn_fwd(s * half, s * half + half, width, block_rows),
                [shape((half, width)), shape((heads, half), WIDE), rows_b],
                qkv,
                idc,
                idr,
                w_out,
                flops=4 * half * rows_all * width * 4,
                exps=half * rows_all * heads,
            )
        mine = add(part[0], lay.to_core(part[1]))
        middle, n2m = call(
            norm_kernel,
            [rows_f, rows_b],
            h_rows,
            mine,
            lay.to_lower(mine),
            out_bias[i : i + 1],
            norm2_gain[i : i + 1],
            norm2_bias[i : i + 1],
        )
        n2 = [n2m, lay.to_core(n2m)]
        hid, slope = [None] * 2, [None] * 2
        for s in (1, 0):
            hid[s], slope[s], part[s] = call(
                mlp_kernel,
                [rows_u, rows_u, rows_b],
                n2[s],
                w_up,
                b_up[i],
                w_down,
                flops=4 * half * d * hidden_units,
                exps=2 * half * hidden_units,
            )
        mine = add(part[0], lay.to_core(part[1]))
        kept.append((h_rows, n1m, n1o, qkv, att, lse, middle, n2, hid, slope))
        j = min(i + 1, layers - 1)
        h_rows, n1m = call(
            norm_kernel,
            [rows_f, rows_b],
            middle,
            mine,
            lay.to_lower(mine),
            down_bias[i : i + 1],
            norm1_gain[j : j + 1],
            norm1_bias[j : j + 1],
        )
    activations = spread(lay, h_rows.astype(NARROW)).astype(WIDE)

    g = swap_rows(out_grad)
    rows_s = shape((half + 16, d))
    small_f = shape((8, d), WIDE)
    (glm,) = call(cast_kernel, [rows_s], g)
    big = [None] * layers
    vectors = [[None] * 8 for _ in range(layers)]

    def vector_rows(rows):
        rows = [jnp.pad(r, ((0, 0), (0, d - r.shape[1]))).astype(NARROW) for r in rows]
        return jnp.concatenate(rows + [jnp.zeros((max(16, lay.pairs) - len(rows), d), NARROW)], axis=0)

    waiting = []
    for i in reversed(range(layers)):
        h_rows, n1m, n1o, qkv, att, lse, middle, n2, hid, slope = kept[i]
        w_qkv, w_up, w_down, w_out = fetched[i]
        gl = [glm, lay.to_core(glm)]
        sums_g = gl[0][half:].astype(WIDE) + gl[1][half:].astype(WIDE)
        gb, part, sums = [None] * 2, [None] * 2, [None] * 2
        for s in (1, 0):
            gb[s], part[s], sums[s] = call(
                mlp_back_kernel,
                [rows_u, rows_b, shape((8, hidden_units), WIDE)],
                gl[s],
                w_down,
                slope[s],
                w_up,
                flops=4 * half * d * hidden_units,
            )
        mine = add(part[0], lay.to_core(part[1]))
        got = lay.to_lower(mine)
        (d_down,) = call(
            pair_grad_kernel, [shape((hidden_units, d))], hid[0], hid[1], gl[0], gl[1], flops=2 * rows_all * d * hidden_units
        )
        (d_up,) = call(
            pair_grad_kernel, [shape((d, hidden_units))], n2[0], n2[1], gb[0], gb[1], flops=2 * rows_all * d * hidden_units
        )
        mlp_rows = [sums_g[0:1], sums_g[1:2], sums_g[2:3], sums[0][:1] + sums[1][:1]]
        gm, gmm, _ = call(
            make_norm_back(False), [rows_f, rows_s, small_f], g, mine, got, middle, norm2_gain[i : i + 1]
        )
        gm2 = [gmm, lay.to_core(gmm)]
        sums_m = gm2[0][half:].astype(WIDE) + gm2[1][half:].astype(WIDE)
        dqkv, qkv_sum, part_m, part_o = call(
            make_attn_back(width, block_rows),
            [shape((rows_all, 3 * width)), shape((8, 3 * width), WIDE), rows_b, rows_b],
            gm2[0],
            gm2[1],
            w_out,
            qkv,
            att[0],
            att[1],
            lse[0],
            lse[1],
            idc,
            idr,
            w_qkv,
            scratch=[
                pltpu.VMEM((rows_all, width), NARROW),
                pltpu.VMEM((width, rows_all), WIDE),
                pltpu.VMEM((8, rows_all), WIDE),
            ],
            flops=10 * rows_all * rows_all * width * 4,
            exps=rows_all * rows_all * heads,
        )
        mine = add(part_m, lay.to_core(part_o))
        got = lay.to_lower(mine)
        (d_out,) = call(
            pair_grad_kernel, [shape((width, d))], att[0], att[1], gm2[0], gm2[1], flops=2 * rows_all * d * width
        )
        (d_qkv,) = call(
            pair_grad_kernel,
            [shape((3 * width, d))],
            dqkv[:half],
            dqkv[half:],
            n1m,
            n1o,
            flops=2 * rows_all * d * 3 * width,
        )
        att_rows = [
            sums_m[0:1],
            sums_m[1:2],
            sums_m[2:3],
            jnp.concatenate([qkv_sum[:1, :width], qkv_sum[:1, 2 * width :]], axis=1),
        ]
        if i:
            big[i] = total_grads(lay, [d_down, d_up, d_out, d_qkv, vector_rows(mlp_rows + att_rows)])
            vectors[i] = big[i].pop()
            g, glm, _ = call(
                make_norm_back(False), [rows_f, rows_s, small_f], gm, mine, got, h_rows, norm1_gain[i : i + 1]
            )
        else:
            one = total_grads(lay, [d_down, d_up, vector_rows(mlp_rows)])
            two = total_grads(lay, [d_out, d_qkv, vector_rows(att_rows)])
            vectors[i] = jnp.concatenate([one.pop()[:4], two.pop()[:4]], axis=0)
            big[i] = one + two
            tok, last = call(
                make_norm_back(True), [rows_b, small_f], gm, mine, got, h_rows, norm1_gain[:1], masked
            )
    tokens_grad = spread(lay, tok).astype(WIDE)
    last = total_small(lay, last)

    vec = [v.astype(WIDE) for v in vectors]
    after = [last[0:2]] + [vec[i][0:2] for i in range(layers)]
    d_gain1 = jnp.stack([after[0][0]] + [vec[i][0] for i in range(layers - 1)])
    d_shift1 = jnp.stack([after[0][1]] + [vec[i][1] for i in range(layers - 1)])
    every = jnp.stack([v[:8] for v in vec])
    full = [jnp.stack([big[i][n] for i in range(layers)]).astype(WIDE) for n in range(4)]
    d_qkv = jnp.stack([jnp.transpose(big[i][3]).astype(WIDE) for i in range(layers)])
    return (
        activations,
        tokens_grad,
        last[2],
        d_gain1,
        d_shift1,
        d_qkv.reshape(layers, d, 3, width),
        every[:, 7, : 2 * width].reshape(layers, 2, width),
        full[2],
        every[:, 6],
        every[:, 4],
        every[:, 5],
        full[1],
        every[:, 3, :hidden_units],
        full[0],
        every[:, 2],
    )


def solution(mesh):
    lay = Layout(mesh)
    placed = (
        P("dp", None),
        P("dp"),
        P("dp"),
        P(),
        P(),
        P(),
        P(None, None, None, "tensor"),
        P(None, None, "tensor"),
        P(None, "tensor", None),
        P(),
        P(),
        P(),
        P(None, None, "tensor"),
        P(None, "tensor"),
        P(None, "tensor", None),
        P(),
        P("dp", None),
    )
    return jax.shard_map(
        partial(body, lay),
        mesh=mesh,
        in_specs=placed,
        out_specs=(
            P("dp", None),
            P("dp", None),
            P(),
            P(),
            P(),
            P(None, None, None, "tensor"),
            P(None, None, "tensor"),
            P(None, "tensor", None),
            P(),
            P(),
            P(),
            P(None, None, "tensor"),
            P(None, "tensor"),
            P(None, "tensor", None),
            P(),
        ),
        check_vma=False,
    )
```

```python
from functools import partial

import jax
import jax.numpy as jnp
from jax import lax
from jax.experimental import pallas as pl
from jax.experimental.pallas import tpu as pltpu
from jax.sharding import PartitionSpec as P

AXES = ("dp", "tensor")
VMEM_LIMIT = 16 * 2**20
COST = 1.0e10
HD = 64
WIDE = jnp.float32
NARROW = jnp.bfloat16
EPSILON = 1e-06
MASKED = -1e30
NN = ((1,), (0,))
NT = ((1,), (1,))
TN = ((0,), (0,))


def dot(a, b, dims=NN):
    return lax.dot_general(a, b, (dims, ((), ())), preferred_element_type=WIDE)


class Clock:
    def __init__(self):
        self.last = None

    def __call__(self, us, kernel, outs, *args, scratch=()):
        outs = call(us, kernel, outs, self.after(args[0]), *args[1:], scratch=scratch)
        self.last = outs[-1]
        return outs

    def after(self, value):
        return value if self.last is None else lax.optimization_barrier((value, self.last))[0]


def call(us, kernel, outs, *args, scratch=()):
    return pl.pallas_call(
        kernel,
        out_shape=outs,
        in_specs=[pl.BlockSpec(memory_space=pltpu.SMEM if x.ndim == 1 else pltpu.VMEM) for x in args],
        out_specs=[pl.BlockSpec(memory_space=pltpu.VMEM)] * len(outs),
        scratch_shapes=list(scratch),
        compiler_params=pltpu.CompilerParams(vmem_limit_bytes=VMEM_LIMIT),
        cost_estimate=pl.CostEstimate(flops=int(us * COST), bytes_accessed=int(us * COST // 300), transcendentals=0),
    )(*args)


def shape(s, kind=NARROW):
    return jax.ShapeDtypeStruct(s, kind)


def first_kernel(at_ref, own_ref, got_ref, ids_ref, ids_got_ref, fill_ref, gain_ref, shift_ref,
                 ha_ref, hb_ref, na_ref, nb_ref, idr_ref, idc_ref, mask_ref):
    core, near = at_ref[1], at_ref[4] == 1
    half = own_ref.shape[1]
    both = jnp.where(near, ids_ref[...], ids_got_ref[...]).astype(WIDE)
    swapped = jnp.concatenate([both[:, half:], both[:, :half]], axis=1)
    both = jnp.where(core == 0, both, swapped)
    idr_ref[...] = both
    column = jnp.transpose(jnp.concatenate([both, jnp.zeros((6, 2 * half), WIDE)], axis=0))
    idc_ref[...] = column
    mask_ref[...] = column[:half, 1:2] + jnp.zeros((half, 8), WIDE)
    chunk = ha_ref.shape[0]
    for h_ref, n_ref, at in ((ha_ref, na_ref, 0), (hb_ref, nb_ref, chunk)):
        for r in range(0, chunk, 128):
            rows = slice(at + r, at + r + 128)
            x = jnp.where(near, own_ref[core, rows, :].astype(WIDE), got_ref[core, rows, :].astype(WIDE))
            h = jnp.where(mask_ref[rows, 0:1] == 1.0, fill_ref[...], x)
            h_ref[r : r + 128, :] = h
            centre, inv = stats(h)
            n_ref[r : r + 128, :] = (centre * inv * gain_ref[0:1, :] + shift_ref[0:1, :]).astype(NARROW)


def grad_kernel(at_ref, own_ref, got_ref, ga_ref, gb_ref, la_ref, lb_ref, sa_ref, sb_ref):
    core, near = at_ref[1], at_ref[4] == 1
    chunk, d = ga_ref.shape
    zero = jnp.zeros((1, d), WIDE)
    for g_ref, l_ref, s_ref, at in ((ga_ref, la_ref, sa_ref, 0), (gb_ref, lb_ref, sb_ref, chunk)):
        total = jnp.zeros((8, d), WIDE)
        for r in range(0, chunk, 64):
            rows = slice(at + r, at + r + 64)
            g = jnp.where(near, own_ref[core, rows, :], got_ref[core, rows, :])
            g_ref[r : r + 64, :] = g
            l_ref[r : r + 64, :] = g.astype(NARROW)
            total += fold(g)
        total = jnp.sum(total, axis=0, keepdims=True)
        s_ref[...] = jnp.concatenate([zero, zero, total, jnp.zeros((5, d), WIDE)], axis=0)


def stats(x):
    mean = jnp.mean(x, axis=-1, keepdims=True)
    centre = x - mean
    spread = jnp.mean(centre * centre, axis=-1, keepdims=True)
    return centre, lax.rsqrt(spread + EPSILON)


def fold(x):
    return jnp.sum(x.reshape(x.shape[0] // 8, 8, x.shape[1]), axis=0)


def make_norm(i, j):
    def kernel(x_ref, a_ref, b_ref, bias_ref, gain_ref, shift_ref, h_ref, n_ref):
        for r in range(0, x_ref.shape[0], 128):
            rows = slice(r, r + 128)
            h = x_ref[rows, :] + (a_ref[rows, :].astype(WIDE) + b_ref[rows, :].astype(WIDE)) + bias_ref[i : i + 1, :]
            h_ref[rows, :] = h
            centre, inv = stats(h)
            n_ref[rows, :] = (centre * inv * gain_ref[j : j + 1, :] + shift_ref[j : j + 1, :]).astype(NARROW)

    return kernel


def make_last_rows(i):
    def kernel(at_ref, xa_ref, xb_ref, pa_ref, pb_ref, got_ref, bias_ref, out_ref):
        lower = at_ref[3] == 0
        x = jnp.where(lower, xa_ref[...], xb_ref[...])
        p = jnp.where(lower, pa_ref[...].astype(WIDE), pb_ref[...].astype(WIDE))
        out_ref[...] = (x + (p + got_ref[...].astype(WIDE)) + bias_ref[i : i + 1, :]).astype(NARROW)

    return kernel


def pick_kernel(at_ref, a_ref, b_ref, out_ref):
    out_ref[...] = jnp.where(at_ref[3] == 0, b_ref[...].astype(WIDE), a_ref[...].astype(WIDE)).astype(NARROW)


def norm_back(rows, gn, x, g, gain):
    centre, inv = stats(x)
    xhat = centre * inv
    e = gn * gain
    mean_e = jnp.mean(e, axis=-1, keepdims=True)
    mean_ex = jnp.mean(e * xhat, axis=-1, keepdims=True)
    return g + inv * (e - mean_e - xhat * mean_ex), gn * xhat


def put_sums(sums_ref, sums):
    d = sums_ref.shape[1]
    sums = [jnp.sum(x, axis=0, keepdims=True) for x in sums]
    sums_ref[...] = jnp.concatenate(sums + [jnp.zeros((8 - len(sums), d), WIDE)], axis=0)


def make_norm_back(i):
    def kernel(g_ref, a_ref, b_ref, x_ref, gain_ref, out_ref, low_ref, sums_ref):
        chunk, d = x_ref.shape
        sums = [jnp.zeros((8, d), WIDE)] * 3
        for r in range(0, chunk, 64):
            rows = slice(r, r + 64)
            gn = a_ref[rows, :].astype(WIDE) + b_ref[rows, :].astype(WIDE)
            out, scaled = norm_back(rows, gn, x_ref[rows, :], g_ref[rows, :], gain_ref[i : i + 1, :])
            out_ref[rows, :] = out
            low_ref[rows, :] = out.astype(NARROW)
            sums = [s + fold(y) for s, y in zip(sums, (scaled, gn, out))]
        put_sums(sums_ref, sums)

    return kernel


def last_back_kernel(at_ref, ga_ref, gb_ref, pa_ref, pb_ref, got_ref, xa_ref, xb_ref, mask_ref, gain_ref, low_ref, sums_ref):
    lower = at_ref[3]
    first = lower == 0
    chunk, d = xa_ref.shape
    sums = [jnp.zeros((8, d), WIDE)] * 3
    pick = lambda a, b, rows: jnp.where(first, a[rows, :].astype(WIDE), b[rows, :].astype(WIDE))
    for r in range(0, chunk, 64):
        rows = slice(r, r + 64)
        gn = pick(pa_ref, pb_ref, rows) + got_ref[rows, :].astype(WIDE)
        out, scaled = norm_back(
            rows, gn, pick(xa_ref, xb_ref, rows), pick(ga_ref, gb_ref, rows), gain_ref[0:1, :]
        )
        masked = mask_ref[pl.ds(pl.multiple_of(lower * chunk, chunk) + r, 64), 0:1] == 1.0
        low_ref[rows, :] = jnp.where(masked, 0.0, out).astype(NARROW)
        sums = [s + fold(y) for s, y in zip(sums, (scaled, gn, jnp.where(masked, out, 0.0)))]
    put_sums(sums_ref, sums)


def make_qkv(i, j):
    def kernel(na_ref, nb_ref, wq_ref, wkv_ref, b_ref, q_ref, kv_ref):
        chunk = na_ref.shape[0]
        width = wq_ref.shape[2]
        zero = jnp.zeros((1, width), WIDE)
        for n_ref, at in ((na_ref, 0), (nb_ref, chunk)):
            rows = slice(at, at + chunk)
            n = n_ref[...]
            q_ref[rows, :] = (dot(n, wq_ref[j]) + b_ref[2 * i : 2 * i + 1, :]).astype(NARROW)
            bias = jnp.concatenate([zero, b_ref[2 * i + 1 : 2 * i + 2, :]], axis=1)
            kv_ref[rows, :] = (dot(n, wkv_ref[j]) + bias).astype(NARROW)

    return kernel


def make_attn(width, chunk, chunks):
    heads = width // HD

    def kernel(q_ref, kvm_ref, kvo_ref, idc_ref, idr_ref, *refs):
        half = q_ref.shape[0]
        for n, number in enumerate(chunks):
            att_ref, lse_ref = refs[2 * n : 2 * n + 2]
            rows = slice(number * chunk, number * chunk + chunk)
            idr = idr_ref[0:1, rows]
            bias = [jnp.where(idc_ref[x : x + half, 0:1] == idr, 0.0, MASKED) for x in (0, half)]
            outs, lses = [], []
            for head in range(heads):
                cols = slice(head * HD, head * HD + HD)
                late = slice(width + head * HD, width + head * HD + HD)
                q = q_ref[rows, cols] * jnp.asarray(HD**-0.5, NARROW)
                s = [dot(ref[:, cols], q, NT) + b for ref, b in zip((kvm_ref, kvo_ref), bias)]
                top = jnp.max(jnp.maximum(s[0], s[1]), axis=0, keepdims=True)
                e = [jnp.exp(x - top) for x in s]
                total = jnp.sum(e[0] + e[1], axis=0, keepdims=True)
                o = dot(kvm_ref[:, late], e[0].astype(NARROW), TN)
                o = o + dot(kvo_ref[:, late], e[1].astype(NARROW), TN)
                outs.append(o * (1.0 / total))
                lses.append(top + jnp.log(total))
            att_ref[...] = jnp.transpose(jnp.concatenate(outs, axis=0)).astype(NARROW)
            lse_ref[0:heads, :] = jnp.concatenate(lses, axis=0)

    return kernel


def make_out(i):
    def kernel(a_ref, b_ref, wa_ref, wb_ref, part_ref):
        part_ref[...] = (dot(a_ref[...], wa_ref[i], NT) + dot(b_ref[...], wb_ref[0], NT)).astype(NARROW)

    return kernel


ERF = (0.254829592, -0.284496736, 1.421413741, -1.453152027, 1.061405429)


def gelu_and_slope(x):
    bell = jnp.exp(x * x * -0.5)
    t = 1.0 / (1.0 + (0.3275911 * 0.7071067811865476) * jnp.abs(x))
    tail = t * (ERF[0] + t * (ERF[1] + t * (ERF[2] + t * (ERF[3] + t * ERF[4]))))
    tail = 0.5 * (tail * bell)
    phi = jnp.where(x < 0.0, tail, 1.0 - tail)
    return x * phi, phi + x * (0.3989422804014327 * bell)


def make_mlp(i):
    def kernel(n_ref, up_a_ref, up_b_ref, bias_a_ref, bias_b_ref, down_a_ref, down_b_ref, hid_ref, slope_ref, part_ref):
        y = None
        for slot, j, up_ref, bias_ref, down_ref in (
            (0, i, up_a_ref, bias_a_ref, down_a_ref),
            (1, 0, up_b_ref, bias_b_ref, down_b_ref),
        ):
            for f in range(0, up_ref.shape[2], 256):
                cols = slice(f, f + 256)
                x = dot(n_ref[...], up_ref[j, :, cols]) + bias_ref[i : i + 1, cols]
                hid, slope = gelu_and_slope(x)
                hid_ref[slot, :, cols] = hid.astype(NARROW)
                slope_ref[slot, :, cols] = slope.astype(NARROW)
            z = dot(hid_ref[slot], down_ref[j])
            y = z if y is None else y + z
        part_ref[...] = y.astype(NARROW)

    return kernel


def make_mlp_back(i):
    def kernel(g_ref, down_a_ref, down_b_ref, slope_ref, up_a_ref, up_b_ref, gb_ref, part_ref):
        y = None
        for slot, j, down_ref, up_ref in ((0, i, down_a_ref, up_a_ref), (1, 0, down_b_ref, up_b_ref)):
            dh = dot(g_ref[...], down_ref[j], NT)
            gb = (dh * slope_ref[slot].astype(WIDE)).astype(NARROW)
            gb_ref[slot] = gb
            z = dot(gb, up_ref[j], NT)
            y = z if y is None else y + z
        part_ref[...] = y.astype(NARROW)

    return kernel


def row_sum(x):
    return jnp.sum(fold(x.astype(WIDE)), axis=0, keepdims=True)


def wide_row(x, d):
    return x if x.shape[1] == d else jnp.concatenate([x, jnp.zeros((1, d - x.shape[1]), WIDE)], axis=1)


def put_rows(out_ref, at, rows):
    d = out_ref.shape[1]
    rows = [wide_row(r, d) for r in rows]
    out_ref[at : at + 16, :] = jnp.concatenate(rows + [jnp.zeros((16 - len(rows), d), WIDE)], axis=0).astype(NARROW)
    if out_ref.shape[0] > at + 16:
        out_ref[at + 16 :, :] = jnp.zeros((out_ref.shape[0] - at - 16, d), NARROW)


def mlp_grad_kernel(core_ref, *refs):
    *refs, keep_ref, send_ref = refs
    hid, gl, n, gb = (refs[2 * i : 2 * i + 2] for i in range(4))
    units = hid[0].shape[2]
    d = n[0].shape[1]
    for out_ref, slot in ((send_ref, 1 - core_ref[1]), (keep_ref, core_ref[1])):
        for f in range(0, units, 256):
            y = sum(dot(x[slot, :, f : f + 256], y[...], TN) for x, y in zip(hid, gl))
            out_ref[f : f + 256, :] = y.astype(NARROW)
        for f in range(0, d, 256):
            y = sum(dot(x[:, f : f + 256], y[slot], TN) for x, y in zip(n, gb))
            out_ref[units + f : units + f + 256, :] = y.astype(NARROW)
        put_rows(out_ref, units + d, [sum(row_sum(x[slot]) for x in gb)])


def make_attn_back(width, block, i):
    heads = width // HD

    def kernel(ga_in, gb_in, w_ref, q_ref, kvm_ref, kvo_ref, atta_ref, attb_ref, lsea_ref, lseb_ref, idc_ref, idr_ref,
               dq_ref, dkvm_ref, dkvo_ref, ga_ref, dqt_ref, dd_ref, lse_ref):
        half = q_ref.shape[0]
        at = 0
        for g_in, att_ref, l_ref in ((ga_in, atta_ref, lsea_ref), (gb_in, attb_ref, lseb_ref)):
            size = g_in.shape[0]
            rows = slice(at, at + size)
            ga = dot(g_in[...], w_ref[i]).astype(NARROW)
            ga_ref[rows, :] = ga
            x = ga.astype(WIDE) * att_ref[...].astype(WIDE)
            per = [jnp.sum(x[:, HD * i : HD * i + HD], axis=1, keepdims=True) for i in range(heads)]
            per = jnp.concatenate(per + [jnp.zeros((size, 128 - heads), WIDE)], axis=1)
            dd_ref[:, rows] = jnp.transpose(per)[0:8]
            lse_ref[:, rows] = l_ref[...]
            at += size
        for kv_ref, d_ref, base in ((kvo_ref, dkvo_ref, half), (kvm_ref, dkvm_ref, 0)):
            for at in range(0, half, block):
                keys = slice(at, at + block)
                bias = jnp.where(idc_ref[base + at : base + at + block, 0:1] == idr_ref[0:1, :half], 0.0, MASKED)
                dks, dvs = [], []
                for head in range(heads):
                    cols = slice(head * HD, head * HD + HD)
                    late = slice(width + head * HD, width + head * HD + HD)
                    q = q_ref[:, cols]
                    ga = ga_ref[:, cols]
                    v = kv_ref[keys, late]
                    scaled = kv_ref[keys, cols] * jnp.asarray(HD**-0.5, NARROW)
                    p = jnp.exp(dot(scaled, q, NT) + bias - lse_ref[head : head + 1, :])
                    dvs.append(dot(p.astype(NARROW), ga))
                    ds = (p * (dot(v, ga, NT) - dd_ref[head : head + 1, :])).astype(NARROW)
                    dks.append(dot(ds, q) * HD**-0.5)
                    y = dot(scaled, ds, TN)
                    if base and not at:
                        dqt_ref[cols, :] = y
                    else:
                        dqt_ref[cols, :] += y
                d_ref[keys, :] = jnp.concatenate(dks + dvs, axis=1).astype(NARROW)
        dq_ref[...] = jnp.transpose(dqt_ref[...]).astype(NARROW)

    return kernel


def make_attn_join(number, i):
    def kernel(dqa_ref, dkva_ref, ra_ref, atta_ref, dqb_ref, dkvb_ref, rb_ref, attb_ref,
               wqa_ref, wkva_ref, wqb_ref, wkvb_ref, dq_ref, dkv_ref, att_ref, part_ref):
        size = part_ref.shape[0]
        rows = slice(number * size, number * size + size)
        y = None
        for slot, j, dq1_ref, own_ref, got_ref, a_ref, wq_ref, wkv_ref in (
            (0, i, dqa_ref, dkva_ref, ra_ref, atta_ref, wqa_ref, wkva_ref),
            (1, 0, dqb_ref, dkvb_ref, rb_ref, attb_ref, wqb_ref, wkvb_ref),
        ):
            dq = dq1_ref[rows, :]
            dq_ref[slot] = dq
            att_ref[slot] = a_ref[...]
            dkv = (own_ref[rows, :].astype(WIDE) + got_ref[rows, :].astype(WIDE)).astype(NARROW)
            dkv_ref[slot] = dkv
            z = dot(dq, wq_ref[j], NT) + dot(dkv, wkv_ref[j], NT)
            y = z if y is None else y + z
        part_ref[...] = y.astype(NARROW)

    return kernel


def attn_grad_kernel(core_ref, *refs):
    *refs, keep_ref, send_ref = refs
    dq, dkv, att, n, g = (refs[2 * i : 2 * i + 2] for i in range(5))
    width = dq[0].shape[2]
    for out_ref, slot in ((send_ref, 1 - core_ref[1]), (keep_ref, core_ref[1])):
        many = lambda x, y: sum(dot(a[slot], b[...], TN) for a, b in zip(x, y)).astype(NARROW)
        out_ref[0:width, :] = many(dq, n)
        out_ref[width : 3 * width, :] = many(dkv, n)
        out_ref[3 * width : 4 * width, :] = many(att, g)
        put_rows(
            out_ref,
            4 * width,
            [sum(row_sum(x[slot]) for x in dq), sum(row_sum(x[slot]) for x in dkv)[:, width:]],
        )


def vector_kernel(at_ref, *refs):
    *refs, last_ref, out_ref = refs
    once = jnp.where(at_ref[3] == 0, 1.0, 0.0)
    rows = [refs[0][2:3, :] + refs[1][2:3, :]]
    for a_ref, b_ref in zip(refs[2::2], refs[3::2]):
        rows.append(a_ref[0:3, :] + b_ref[0:3, :])
    rows = jnp.concatenate(rows, axis=0) * once
    last = last_ref[0:3, :]
    count = rows.shape[0] + last.shape[0]
    out_ref[...] = jnp.concatenate([rows, last, jnp.zeros((16 - count, rows.shape[1]), WIDE)], axis=0)


def make_pack(layers):
    def kernel(at_ref, *refs):
        n = len(refs) - len(layers)
        size = refs[n].shape[0]
        rows = pl.ds(pl.multiple_of((2 * at_ref[0] + at_ref[1]) * size, size), size)
        for i, out_ref in zip(layers, refs[n:]):
            at = 0
            for ref in refs[:n]:
                width = ref.shape[2]
                out_ref[:, at : at + width] = ref[i, rows, :]
                at += width

    return kernel


def pair_bits(pairs, core):
    count = pairs.bit_length() - 1
    return [(i + core) % count for i in range(count)]


def by_steps(number, pairs, core):
    return sum(((number >> i) & 1) << bit for i, bit in enumerate(pair_bits(pairs, core)))


def block_of(at_ref, pairs, number, other=0):
    core = at_ref[1] if not other else 1 - at_ref[1]
    return at_ref[0] ^ jnp.where(core == 0, by_steps(number, pairs, 0), by_steps(number, pairs, 1))


def stack_kernel(*refs):
    *refs, out_ref = refs
    at = 0
    for ref in refs:
        count = ref.shape[0]
        out_ref[at : at + count] = ref[...]
        at += count


def place_kernel(at_ref, own_ref, other_ref, *outs):
    pairs, size, _ = own_ref.shape
    for p in range(pairs):
        for ref, which in ((own_ref, 0), (other_ref, 1)):
            core = at_ref[1] if not which else 1 - at_ref[1]
            row = pl.multiple_of((2 * block_of(at_ref, pairs, p, which) + core) * size, size)
            at = 0
            for out_ref in outs:
                width = out_ref.shape[2]
                out_ref[0, pl.ds(row, size), :] = ref[p, :, at : at + width]
                at += width


def make_cut(pairs):
    def kernel(at_ref, keep_ref, got_ref, kept_ref, sent_ref):
        count, size, _ = kept_ref.shape
        for p in range(count):
            number = sum(((p >> (count.bit_length() - 2 - i)) & 1) << (i + 1) for i in range(count.bit_length() - 1))
            for ref, last in ((kept_ref, 0), (sent_ref, 1)):
                rows = pl.ds(pl.multiple_of(block_of(at_ref, pairs, number + last) * size, size), size)
                ref[p] = (keep_ref[rows, :].astype(WIDE) + got_ref[rows, :].astype(WIDE)).astype(NARROW)

    return kernel


def split_kernel(kept_ref, got_ref, out_ref, sent_ref):
    count = out_ref.shape[0]
    for p in range(count):
        out_ref[p] = (kept_ref[p].astype(WIDE) + got_ref[p].astype(WIDE)).astype(NARROW)
        sent_ref[p] = (kept_ref[count + p].astype(WIDE) + got_ref[count + p].astype(WIDE)).astype(NARROW)


def sum_kernel(*refs):
    *refs, out_ref = refs
    out_ref[...] = sum(r[...].astype(WIDE) for r in refs).astype(out_ref.dtype)


def choose_kernel(at_ref, own_ref, got_ref, out_ref):
    out_ref[...] = jnp.where(at_ref[1] == 0, own_ref[...].astype(WIDE), got_ref[...].astype(WIDE)).astype(NARROW)


def order_kernel(at_ref, own_ref, got_ref, out_ref):
    count = own_ref.shape[0]
    for p in range(count):
        out_ref[block_of(at_ref, 2 * count, p)] = own_ref[p]
        out_ref[block_of(at_ref, 2 * count, count + p)] = got_ref[p]


def pair_kernel(at_ref, own_ref, got_ref, out_ref):
    out_ref[at_ref[1]] = own_ref[...]
    out_ref[1 - at_ref[1]] = got_ref[...]


def rows_kernel(at_ref, near_ref, near_got_ref, far_ref, far_got_ref, out_ref):
    near, lower = at_ref[4] == 1, at_ref[3]
    size = near_ref.shape[1]
    pick = lambda a, b: jnp.where(near, a[0].astype(WIDE), b[0].astype(WIDE))
    out_ref[pl.ds(pl.multiple_of(lower * size, size), size), :] = pick(near_ref, far_ref)
    out_ref[pl.ds(pl.multiple_of((1 - lower) * size, size), size), :] = pick(near_got_ref, far_got_ref)


class Layout:
    def __init__(self, mesh):
        self.pairs = mesh.shape["dp"] // 2
        self.tensor = mesh.shape["tensor"]
        self.lowers = self.tensor // 2
        self.everyone = [
            (k, c, h, l)
            for k in range(self.pairs)
            for c in range(2)
            for h in range(2)
            for l in range(self.lowers)
        ]
        self.same = [a for a in self.everyone if a[1] == a[2]]
        self.cross = [a for a in self.everyone if a[1] != a[2]]
        self.core0 = [a for a in self.everyone if a[1] == 0]
        self.core1 = [a for a in self.everyone if a[1] == 1]

    def place(self, k, c, h, l):
        return (2 * k + c) * self.tensor + self.lowers * h + l

    def send(self, value, among, where):
        perm = [(self.place(*a), self.place(*where(*a))) for a in among]
        return lax.ppermute(value, AXES, perm)

    def to_core(self, value, among=None):
        return self.send(value, among or self.everyone, lambda k, c, h, l: (k, 1 - c, h, l))

    def to_lower(self, value, among=None):
        return self.send(value, among or self.everyone, lambda k, c, h, l: (k, c, h, 1 - l))

    def to_upper(self, value):
        return self.send(value, self.everyone, lambda k, c, h, l: (k, c, 1 - h, l))

    def exchange(self, value, step):
        return self.send(
            value, self.everyone, lambda k, c, h, l: (k ^ (1 << pair_bits(self.pairs, c)[step]), c, h, l)
        )


def tie(value, *others):
    return lax.optimization_barrier((value, *others))[0]


def block(value, number, count):
    size = value.shape[0] // count
    return lax.dynamic_slice_in_dim(value, number * size, size, 0)


def pack(run, lay, at, weights, layers):
    size = weights[0].shape[1] // (2 * lay.pairs)
    total = sum(w.shape[2] for w in weights)
    if size % 16 == 0:
        return run(1.5, make_pack(layers), [shape((size, total))] * len(layers), at, *weights)
    part = 2 * at[0] + at[1]
    return [jnp.concatenate([block(w[i], part, 2 * lay.pairs) for w in weights], axis=1) for i in layers]


class Gather:
    def __init__(self, run, lay, piece):
        self.run, self.lay, self.step = run, lay, 0
        self.value = piece[None]
        self.got = lay.exchange(self.value, 0)

    def next(self):
        self.step += 1
        n, *rest = self.value.shape
        (self.value,) = self.run(0.7, stack_kernel, [shape((2 * n, *rest))], self.value, self.got)
        if 1 << self.step < self.lay.pairs:
            self.got = self.lay.exchange(self.value, self.step)

    def all(self):
        while self.value.shape[0] < self.lay.pairs:
            self.next()
        return self.value

    def ordered(self, at):
        while 2 * self.value.shape[0] < self.lay.pairs:
            self.next()
        _, rows, d = self.value.shape
        (out,) = self.run(0.8, order_kernel, [shape((self.lay.pairs, rows, d))], at, self.value, self.got)
        return out.reshape(-1, d)


def unpack(run, lay, at, own, other, widths):
    size = own.shape[1]
    rows = 2 * lay.pairs * size
    if size % 16 == 0:
        return run(2.0, place_kernel, [shape((1, rows, w)) for w in widths], at, own, other)
    places = [
        (2 * block_of(at, lay.pairs, p, e) + (at[1] ^ e), x[p]) for p in range(lay.pairs) for e, x in ((0, own), (1, other))
    ]
    whole = jnp.zeros((rows, own.shape[2]), own.dtype)
    for place, part in places:
        whole = lax.dynamic_update_slice_in_dim(whole, part, place * size, 0)
    out, start = [], 0
    for w in widths:
        out.append(whole[None, :, start : start + w])
        start += w
    return out


class Scatter:
    def __init__(self, run, lay, at, keep, got):
        self.run, self.lay, self.step = run, lay, 0
        size, d = keep.shape
        parts = [shape((lay.pairs // 2, size // lay.pairs, d))] * 2
        self.kept, sent = run(1.2, make_cut(lay.pairs), parts, at, keep, got)
        self.got = lay.exchange(sent, 0)

    def next(self):
        self.step += 1
        n, *rest = self.kept.shape
        self.kept, sent = self.run(0.7, split_kernel, [shape((n // 2, *rest))] * 2, self.kept, self.got)
        self.got = self.lay.exchange(sent, self.step)

    def across(self):
        while self.kept.shape[0] > 1:
            self.next()
        self.mine = total(self.run, self.kept, self.got)
        self.got = self.lay.send(self.mine, self.lay.core1, lambda k, c, h, l: (k, 0, 1 - h, l))

    def to_core(self):
        self.mine = total(self.run, self.mine, self.got)
        self.got = self.lay.to_core(self.mine, self.lay.core0)

    def gather(self, at):
        (piece,) = self.run(0.4, choose_kernel, [shape(self.mine.shape)], at, self.mine, self.got)
        return Gather(self.run, self.lay, piece[0])


def total(run, *parts):
    return run(0.4, sum_kernel, [shape(parts[0].shape, parts[0].dtype)], *parts)[0]


def both_halves(run, at, piece, got):
    return run(0.5, pair_kernel, [shape((2, *piece.shape))], at, piece, got)[0]


def to_holders(lay, both):
    near = lay.to_lower(both, lay.same)
    far = lay.send(both, lay.same, lambda k, c, h, l: (k, c, 1 - h, l))
    return near, far


def whole_rows(run, at, near, near_got, far, far_got):
    _, size, d = near.shape
    spec = lambda: pl.BlockSpec((1, size, d), lambda i, *_: (i, 0, 0))
    run.last = pl.pallas_call(
        rows_kernel,
        grid_spec=pltpu.PrefetchScalarGridSpec(
            num_scalar_prefetch=1,
            grid=(2,),
            in_specs=[spec() for _ in range(4)],
            out_specs=pl.BlockSpec((2 * size, d), lambda i, *_: (i, 0)),
        ),
        out_shape=shape((4 * size, d), WIDE),
        compiler_params=pltpu.CompilerParams(vmem_limit_bytes=VMEM_LIMIT),
        cost_estimate=pl.CostEstimate(flops=int(2 * COST), bytes_accessed=int(2 * COST // 300), transcendentals=0),
    )(run.after(at), near, near_got, far, far_got)
    return run.last


def body(
    lay,
    tokens_in,
    patch_mask,
    image_ids,
    mask_token,
    norm1_gain,
    norm1_bias,
    qkv_weight,
    qv_bias,
    out_weight,
    out_bias,
    norm2_gain,
    norm2_bias,
    up_weight,
    up_bias,
    down_weight,
    down_bias,
    out_grad,
):
    dp, tensor = lax.axis_index("dp"), lax.axis_index("tensor")
    c, h = dp % 2, tensor // lay.lowers
    at = jnp.stack([dp // 2, c, h, tensor % lay.lowers, c == h]).astype(jnp.int32)
    layers, d, _, width = qkv_weight.shape
    units = up_weight.shape[2]
    half = tokens_in.shape[0] // 2
    chunk = half // 2
    both = range(2)
    by_half = lambda x: x.reshape(2, half, d)

    part_f = shape((chunk, d), WIDE)
    part_b = shape((chunk, d))
    part_q = shape((chunk, width))
    part_l = shape((8, chunk), WIDE)
    part_u = shape((2, chunk, units))
    sums_f = shape((8, d), WIDE)
    rows_q = shape((half, width))
    rows_kv = shape((half, 2 * width))

    run = Clock()
    tok_got = lay.to_core(tokens_in, lay.same)
    ids = jnp.stack([image_ids, patch_mask])
    ids_got = lay.to_core(ids, lay.same)
    native = (
        qkv_weight[:, :, 0],
        qkv_weight[:, :, 1:].reshape(layers, d, 2 * width),
        jnp.swapaxes(out_weight, 1, 2),
        up_weight,
        down_weight,
    )
    widths = [w.shape[2] for w in native]
    qv = qv_bias.reshape(2 * layers, width)
    b_qv = [qv, lay.to_upper(qv)]
    b_up = [up_bias, lay.to_upper(up_bias)]
    (piece,) = pack(run, lay, at, native[:3], (0,))
    first = lay.to_upper(piece)
    at = tie(at, b_qv[1], b_up[1])
    *rows, idr, idc, mask = run(
        2.5,
        first_kernel,
        [part_f, part_f, part_b, part_b, shape((2, 2 * half), WIDE), shape((2 * half, 8), WIDE), shape((half, 8), WIDE)],
        at,
        by_half(tokens_in),
        by_half(tok_got),
        ids,
        ids_got,
        mask_token[None],
        norm1_gain,
        norm1_bias,
    )
    h_rows, n1 = rows[:2], rows[2:]

    def project(i, s, w, j):
        q, kv = run(0.8, make_qkv(i, j), [rows_q, rows_kv], *n1, w[0], w[1], b_qv[s])
        return q, kv, lay.to_core(kv)

    def attend(s, chunks):
        return run(
            2.0 * len(chunks),
            make_attn(width, chunk, chunks),
            [part_q, part_l] * len(chunks),
            q[s],
            kvm[s],
            kvo[s],
            idc,
            idr,
        )

    fetched = [None] * layers
    kept = []
    for i in range(layers):
        f_w = fetched[i]
        q, kvm, kvo, mine, got = ([None] * 2 for _ in range(5))
        att, lse = ([[None] * 2 for _ in both] for _ in range(2))
        q[0], kvm[0], kvo[0] = project(i, 0, native, i)
        if i == 0:
            (piece,) = pack(run, lay, at, native[3:], (0,))
            late = lay.to_upper(piece)
        else:
            f_w = fetched[i] = unpack(run, lay, at, own, other, widths)
            q[1], kvm[1], kvo[1] = project(i, 1, f_w, 0)
        att[0][0], lse[0][0], att[0][1], lse[0][1] = attend(0, (0, 1))
        if i == 0:
            first = Gather(run, lay, tie(first, att[0][0]))
            first.next()
            late = Gather(run, lay, tie(late, first.value))
            own = first.all()
            other = lay.to_core(own)
            (piece,) = pack(run, lay, at, native, (1,))
            following = lay.to_upper(tie(piece, late.value))
            late.next()
            f_w = unpack(run, lay, at, own, other, widths[:3])
            q[1], kvm[1], kvo[1] = project(i, 1, f_w, 0)
            own = late.all()
            other = lay.to_core(own)
        for a in both:
            att[1][a], lse[1][a] = attend(1, (a,))
            (mine[a],) = run(0.9, make_out(i), [part_b], att[0][a], att[1][a], native[2], f_w[2])
            got[a] = lay.to_lower(mine[a])
        if i == 0:
            f_w = fetched[0] = [*f_w, *unpack(run, lay, at, own, other, widths[3:])]
        middle, n2, hid, slope, part, got2 = ([None] * 2 for _ in range(6))
        for a in both:
            middle[a], n2[a] = run(
                0.8, make_norm(i, i), [part_f, part_b], h_rows[a], mine[a], got[a], out_bias, norm2_gain, norm2_bias
            )
            hid[a], slope[a], part[a] = run(
                2.9,
                make_mlp(i),
                [part_u, part_u, part_b],
                n2[a],
                native[3],
                f_w[3],
                b_up[0],
                b_up[1],
                native[4],
                f_w[4],
            )
            if i + 1 < layers:
                got2[a] = lay.to_lower(part[a])
                if a == 0:
                    following = Gather(run, lay, tie(following, part[0]))
        kept.append((h_rows, n1, q, kvm, kvo, att, lse, middle, n2, hid, slope))
        if i + 1 < layers:
            g_got = lay.to_core(tie(out_grad, part[1]), lay.same)
            following.next()
            h_rows, n1 = [None] * 2, [None] * 2
            for a in both:
                h_rows[a], n1[a] = run(
                    0.8,
                    make_norm(i, i + 1),
                    [part_f, part_b],
                    middle[a],
                    part[a],
                    got2[a],
                    down_bias,
                    norm1_gain,
                    norm1_bias,
                )
            own = following.all()
            other = lay.to_core(own)
    *g, = run(1.5, grad_kernel, [part_f] * 2 + [part_b] * 2 + [sums_f] * 2, at, by_half(out_grad), by_half(g_got))
    g, low, sums = g[:2], g[2:4], g[4:]

    extra = 16 * max(lay.pairs, 4)
    done = {}

    def back_mlp(i):
        for a in both:
            gb[a], mine[a] = run(
                2.0, make_mlp_back(i), [part_u, part_b], low[a], native[4], f_w[4], slope[a], native[3], f_w[3]
            )
            got[a] = lay.to_lower(mine[a])

    def mlp_grads():
        size = units + d + extra
        keep, sent = run(4.2, mlp_grad_kernel, [shape((size, d))] * 2, at, *hid, *low, *n2, *gb)
        return keep, lay.to_core(sent)

    def back_norm(i, a, x, gain):
        return run(1.4, make_norm_back(i), [part_f, part_b, sums_f], g[a], mine[a], got[a], x[a], gain)

    def back_attn(i, s):
        w, j = (native, i) if s == 0 else (f_w, 0)
        dq[s], dkvm[s], dkvo[s] = run(
            4.9,
            make_attn_back(width, half, j),
            [rows_q, rows_kv, rows_kv],
            *gml,
            w[2],
            q[s],
            kvm[s],
            kvo[s],
            *att[s],
            *lse[s],
            idc,
            idr,
            scratch=[
                pltpu.VMEM((half, width), NARROW),
                pltpu.VMEM((width, half), WIDE),
                pltpu.VMEM((8, half), WIDE),
                pltpu.VMEM((8, half), WIDE),
            ],
        )
        dkvr[s] = lay.to_core(dkvo[s])

    def join(i, a):
        dqs[a], dkvs[a], atts[a], mine[a] = run(
            1.7,
            make_attn_join(a, i),
            [shape((2, chunk, width)), shape((2, chunk, 2 * width)), shape((2, chunk, width)), part_b],
            dq[0],
            dkvm[0],
            dkvr[0],
            att[0][a],
            dq[1],
            dkvm[1],
            dkvr[1],
            att[1][a],
            native[0],
            native[1],
            f_w[0],
            f_w[1],
        )

    def attn_grads():
        size = 4 * width + extra
        keep, sent = run(2.5, attn_grad_kernel, [shape((size, d))] * 2, at, *dqs, *dkvs, *atts, *n1, *gml)
        return keep, lay.to_core(sent)

    i = layers - 1
    h_rows, n1, q, kvm, kvo, att, lse, middle, n2, hid, slope = kept[i]
    f_w = fetched[i]
    gb, mine, got, gm, gml, dq, dkvm, dkvo, dkvr, dqs, dkvs, atts = ([None] * 2 for _ in range(12))
    back_mlp(i)
    (sent,) = run(0.4, pick_kernel, [part_b], at, *part)
    last_got = lay.to_lower(sent)
    mlp1 = mlp_grads()
    vectors = [*sums]
    for a in both:
        gm[a], gml[a], sums[a] = back_norm(i, a, middle, norm2_gain)
    vectors += sums
    back_attn(i, 0)
    (rows,) = run(0.5, make_last_rows(i), [part_b], at, *middle, *part, last_got, down_bias)
    rows_got = lay.to_core(rows)
    mlp1 = Scatter(run, lay, at, *mlp1)
    back_attn(i, 1)
    act = both_halves(run, at, rows, rows_got)
    act_near, act_far = to_holders(lay, act)
    for a in both:
        join(i, a)
        got[a] = lay.to_lower(mine[a])
    attn1 = attn_grads()
    g, new_g, low, sums = gm, [None] * 2, [None] * 2, [None] * 2
    for a in both:
        new_g[a], low[a], sums[a] = back_norm(i, a, h_rows, norm1_gain)
        if a == 0:
            mlp1.next()
    g = new_g
    vectors += sums

    i = 0
    h_rows, n1, q, kvm, kvo, att, lse, middle, n2, hid, slope = kept[i]
    f_w = fetched[i]
    gb, mine, got, gm, gml, dq, dkvm, dkvo, dkvr, dqs, dkvs, atts = ([None] * 2 for _ in range(12))
    back_mlp(i)
    mlp1.across()
    attn1 = Scatter(run, lay, at, *attn1)
    mlp0 = mlp_grads()
    sums = [None] * 2
    for a in both:
        gm[a], gml[a], sums[a] = back_norm(i, a, middle, norm2_gain)
        if a == 0:
            mlp1.to_core()
    vectors += sums
    back_attn(i, 0)
    attn1.next()
    mlp0 = Scatter(run, lay, at, *mlp0)
    mlp1 = mlp1.gather(at)
    act_far_got = lay.to_lower(tie(act_far, mlp1.value), lay.cross)
    back_attn(i, 1)
    attn1.across()
    mlp1.next()
    for a in both:
        join(i, a)
    (sent,) = run(0.4, pick_kernel, [part_b], at, *mine)
    got = lay.to_lower(sent)
    attn0 = attn_grads()
    mlp0.next()
    activations = whole_rows(run, at, act, act_near, act_far, act_far_got)
    attn1.to_core()
    mlp1 = mlp1.ordered(at)
    tok, last = run(1.4, last_back_kernel, [part_b, sums_f], at, *gm, *mine, got, *h_rows, mask, norm1_gain)
    tok_got = lay.to_core(tok)
    (last,) = run(0.4, vector_kernel, [shape((16, d), WIDE)], at, *vectors, last)
    small = lay.to_core(last)
    attn0 = Scatter(run, lay, at, *attn0)
    tok = both_halves(run, at, tok, tok_got)
    tok_near, tok_far = to_holders(lay, tok)
    mlp0.across()
    last = total(run, last, small)
    attn1 = attn1.gather(at)

    def flip(step):
        return lay.send(last, lay.everyone, lambda k, c, h, l: (k ^ (1 << step), c, h, l))

    small = flip(0)
    attn0.next()
    last = total(run, last, small)
    small = flip(1)
    mlp0.to_core()
    attn1.next()
    attn0.across()
    last = total(run, last, small)
    for step in range(2, lay.pairs.bit_length() - 1):
        last = total(run, last, flip(step))
    small = lay.to_upper(last)
    mlp0 = mlp0.gather(at)
    attn1 = attn1.ordered(at)
    attn0.to_core()
    tok_far_got = lay.to_lower(tok_far, lay.cross)
    last = total(run, last, small)
    small = lay.to_lower(last)
    mlp0.next()
    attn0 = attn0.gather(at)
    last = total(run, last, small)
    mlp0 = mlp0.ordered(at)
    attn0.next()
    tokens_grad = whole_rows(run, at, tok, tok_near, tok_far, tok_far_got)
    attn0 = attn0.ordered(at)

    mlp, attn = [mlp0, mlp1], [attn0, attn1]
    stack = lambda packs, a, b: jnp.stack([x[a:b] for x in packs]).astype(WIDE)
    d_qkv = jnp.stack([jnp.transpose(x[: 3 * width]) for x in attn]).astype(WIDE)
    def by_layer(row1, row0):
        return jnp.concatenate([last[row0 : row0 + 1], last[row1 : row1 + 1]], axis=0)

    return (
        activations,
        tokens_grad,
        last[12],
        by_layer(4, 10),
        by_layer(5, 11),
        d_qkv.reshape(layers, d, 3, width),
        stack(attn, 4 * width, 4 * width + 2)[:, :, :width],
        stack(attn, 3 * width, 4 * width),
        by_layer(3, 9),
        by_layer(1, 7),
        by_layer(2, 8),
        stack(mlp, units, units + d),
        stack(mlp, units + d, units + d + 1)[:, 0, :units],
        stack(mlp, 0, units),
        by_layer(0, 6),
    )


def solution(mesh):
    lay = Layout(mesh)
    placed = (
        P("dp", None),
        P("dp"),
        P("dp"),
        P(),
        P(),
        P(),
        P(None, None, None, "tensor"),
        P(None, None, "tensor"),
        P(None, "tensor", None),
        P(),
        P(),
        P(),
        P(None, None, "tensor"),
        P(None, "tensor"),
        P(None, "tensor", None),
        P(),
        P("dp", None),
    )
    return jax.shard_map(
        partial(body, lay),
        mesh=mesh,
        in_specs=placed,
        out_specs=(
            P("dp", None),
            P("dp", None),
            P(),
            P(),
            P(),
            P(None, None, None, "tensor"),
            P(None, None, "tensor"),
            P(None, "tensor", None),
            P(),
            P(),
            P(),
            P(None, None, "tensor"),
            P(None, "tensor"),
            P(None, "tensor", None),
            P(),
        ),
        check_vma=False,
    )
```

```python
from functools import partial

import jax
import jax.numpy as jnp
from jax import lax
from jax.experimental import pallas as pl
from jax.experimental.pallas import tpu as pltpu
from jax.sharding import PartitionSpec as P

AXES = ("dp", "tensor")
VMEM_LIMIT = 16 * 2**20
COST = 1.0e10
EARLY = 0.001
SHORT = 0.001
HD = 64
WIDE = jnp.float32
NARROW = jnp.bfloat16
EPSILON = 1e-06
MASKED = -1e30
NN = ((1,), (0,))
NT = ((1,), (1,))
TN = ((0,), (0,))


def dot(a, b, dims=NN):
    return lax.dot_general(a, b, (dims, ((), ())), preferred_element_type=WIDE)


class Clock:
    def __init__(self):
        self.last = None
        self.scale = 1.0

    def __call__(self, us, kernel, outs, *args, scratch=()):
        outs = call(us * self.scale, kernel, outs, self.after(args[0]), *args[1:], scratch=scratch)
        self.last = outs[-1]
        return outs

    def after(self, value):
        return value if self.last is None else lax.optimization_barrier((value, self.last))[0]


def call(us, kernel, outs, *args, scratch=()):
    return pl.pallas_call(
        kernel,
        out_shape=outs,
        in_specs=[pl.BlockSpec(memory_space=pltpu.SMEM if x.ndim == 1 else pltpu.VMEM) for x in args],
        out_specs=[pl.BlockSpec(memory_space=pltpu.VMEM)] * len(outs),
        scratch_shapes=list(scratch),
        compiler_params=pltpu.CompilerParams(vmem_limit_bytes=VMEM_LIMIT),
        cost_estimate=pl.CostEstimate(flops=int(us * COST), bytes_accessed=int(us * COST // 300), transcendentals=0),
    )(*args)


def shape(s, kind=NARROW):
    return jax.ShapeDtypeStruct(s, kind)


def first_kernel(at_ref, own_ref, got_ref, ids_ref, ids_got_ref, fill_ref, gain_ref, shift_ref,
                 ha_ref, hb_ref, na_ref, nb_ref, idr_ref, idc_ref, mask_ref):
    core, near = at_ref[1], at_ref[4] == 1
    half = own_ref.shape[1]
    both = jnp.where(near, ids_ref[...], ids_got_ref[...]).astype(WIDE)
    swapped = jnp.concatenate([both[:, half:], both[:, :half]], axis=1)
    both = jnp.where(core == 0, both, swapped)
    idr_ref[...] = both
    column = jnp.transpose(jnp.concatenate([both, jnp.zeros((6, 2 * half), WIDE)], axis=0))
    idc_ref[...] = column
    mask_ref[...] = column[:half, 1:2] + jnp.zeros((half, 8), WIDE)
    chunk = ha_ref.shape[0]
    for h_ref, n_ref, at in ((ha_ref, na_ref, 0), (hb_ref, nb_ref, chunk)):
        for r in range(0, chunk, 128):
            rows = slice(at + r, at + r + 128)
            x = jnp.where(near, own_ref[core, rows, :].astype(WIDE), got_ref[core, rows, :].astype(WIDE))
            h = jnp.where(mask_ref[rows, 0:1] == 1.0, fill_ref[...], x)
            h_ref[r : r + 128, :] = h
            centre, inv = stats(h)
            n_ref[r : r + 128, :] = (centre * inv * gain_ref[0:1, :] + shift_ref[0:1, :]).astype(NARROW)


def grad_kernel(at_ref, own_ref, got_ref, ga_ref, gb_ref, la_ref, lb_ref, sa_ref, sb_ref):
    core, near = at_ref[1], at_ref[4] == 1
    chunk, d = ga_ref.shape
    zero = jnp.zeros((1, d), WIDE)
    for g_ref, l_ref, s_ref, at in ((ga_ref, la_ref, sa_ref, 0), (gb_ref, lb_ref, sb_ref, chunk)):
        total = jnp.zeros((8, d), WIDE)
        for r in range(0, chunk, 64):
            rows = slice(at + r, at + r + 64)
            g = jnp.where(near, own_ref[core, rows, :], got_ref[core, rows, :])
            g_ref[r : r + 64, :] = g
            l_ref[r : r + 64, :] = g.astype(NARROW)
            total += fold(g)
        total = jnp.sum(total, axis=0, keepdims=True)
        s_ref[...] = jnp.concatenate([zero, zero, total, jnp.zeros((5, d), WIDE)], axis=0)


def stats(x):
    mean = jnp.mean(x, axis=-1, keepdims=True)
    centre = x - mean
    spread = jnp.mean(centre * centre, axis=-1, keepdims=True)
    return centre, lax.rsqrt(spread + EPSILON)


def fold(x):
    return jnp.sum(x.reshape(x.shape[0] // 8, 8, x.shape[1]), axis=0)


def make_norm(i, j):
    def kernel(x_ref, a_ref, b_ref, bias_ref, gain_ref, shift_ref, h_ref, n_ref):
        for r in range(0, x_ref.shape[0], 128):
            rows = slice(r, r + 128)
            h = x_ref[rows, :] + (a_ref[rows, :].astype(WIDE) + b_ref[rows, :].astype(WIDE)) + bias_ref[i : i + 1, :]
            h_ref[rows, :] = h
            centre, inv = stats(h)
            n_ref[rows, :] = (centre * inv * gain_ref[j : j + 1, :] + shift_ref[j : j + 1, :]).astype(NARROW)

    return kernel


def make_last_rows(i):
    def kernel(at_ref, xa_ref, xb_ref, pa_ref, pb_ref, got_ref, bias_ref, out_ref):
        lower = at_ref[3] == 0
        x = jnp.where(lower, xa_ref[...], xb_ref[...])
        p = jnp.where(lower, pa_ref[...].astype(WIDE), pb_ref[...].astype(WIDE))
        out_ref[...] = (x + (p + got_ref[...].astype(WIDE)) + bias_ref[i : i + 1, :]).astype(NARROW)

    return kernel


def pick_kernel(at_ref, a_ref, b_ref, out_ref):
    out_ref[...] = jnp.where(at_ref[3] == 0, b_ref[...].astype(WIDE), a_ref[...].astype(WIDE)).astype(NARROW)


def norm_back(rows, gn, x, g, gain):
    centre, inv = stats(x)
    xhat = centre * inv
    e = gn * gain
    mean_e = jnp.mean(e, axis=-1, keepdims=True)
    mean_ex = jnp.mean(e * xhat, axis=-1, keepdims=True)
    return g + inv * (e - mean_e - xhat * mean_ex), gn * xhat


def put_sums(sums_ref, sums):
    d = sums_ref.shape[1]
    sums = [jnp.sum(x, axis=0, keepdims=True) for x in sums]
    sums_ref[...] = jnp.concatenate(sums + [jnp.zeros((8 - len(sums), d), WIDE)], axis=0)


def make_norm_back(i):
    def kernel(g_ref, a_ref, b_ref, x_ref, gain_ref, out_ref, low_ref, sums_ref):
        chunk, d = x_ref.shape
        sums = [jnp.zeros((8, d), WIDE)] * 3
        for r in range(0, chunk, 64):
            rows = slice(r, r + 64)
            gn = a_ref[rows, :].astype(WIDE) + b_ref[rows, :].astype(WIDE)
            out, scaled = norm_back(rows, gn, x_ref[rows, :], g_ref[rows, :], gain_ref[i : i + 1, :])
            out_ref[rows, :] = out
            low_ref[rows, :] = out.astype(NARROW)
            sums = [s + fold(y) for s, y in zip(sums, (scaled, gn, out))]
        put_sums(sums_ref, sums)

    return kernel


def last_back_kernel(at_ref, ga_ref, gb_ref, pa_ref, pb_ref, got_ref, xa_ref, xb_ref, mask_ref, gain_ref, low_ref, sums_ref):
    lower = at_ref[3]
    first = lower == 0
    chunk, d = xa_ref.shape
    sums = [jnp.zeros((8, d), WIDE)] * 3
    pick = lambda a, b, rows: jnp.where(first, a[rows, :].astype(WIDE), b[rows, :].astype(WIDE))
    for r in range(0, chunk, 64):
        rows = slice(r, r + 64)
        gn = pick(pa_ref, pb_ref, rows) + got_ref[rows, :].astype(WIDE)
        out, scaled = norm_back(
            rows, gn, pick(xa_ref, xb_ref, rows), pick(ga_ref, gb_ref, rows), gain_ref[0:1, :]
        )
        masked = mask_ref[pl.ds(pl.multiple_of(lower * chunk, chunk) + r, 64), 0:1] == 1.0
        low_ref[rows, :] = jnp.where(masked, 0.0, out).astype(NARROW)
        sums = [s + fold(y) for s, y in zip(sums, (scaled, gn, jnp.where(masked, out, 0.0)))]
    put_sums(sums_ref, sums)


def make_qkv(i, j):
    def kernel(na_ref, nb_ref, wq_ref, wkv_ref, b_ref, q_ref, kv_ref):
        chunk = na_ref.shape[0]
        width = wq_ref.shape[2]
        zero = jnp.zeros((1, width), WIDE)
        for n_ref, at in ((na_ref, 0), (nb_ref, chunk)):
            rows = slice(at, at + chunk)
            n = n_ref[...]
            q_ref[rows, :] = (dot(n, wq_ref[j]) + b_ref[2 * i : 2 * i + 1, :]).astype(NARROW)
            bias = jnp.concatenate([zero, b_ref[2 * i + 1 : 2 * i + 2, :]], axis=1)
            kv_ref[rows, :] = (dot(n, wkv_ref[j]) + bias).astype(NARROW)

    return kernel


def make_attn(width, chunk, chunks):
    heads = width // HD

    def kernel(q_ref, kvm_ref, kvo_ref, idc_ref, idr_ref, *refs):
        half = q_ref.shape[0]
        for n, number in enumerate(chunks):
            att_ref, lse_ref = refs[2 * n : 2 * n + 2]
            rows = slice(number * chunk, number * chunk + chunk)
            idr = idr_ref[0:1, rows]
            bias = [jnp.where(idc_ref[x : x + half, 0:1] == idr, 0.0, MASKED) for x in (0, half)]
            outs, lses = [], []
            for head in range(heads):
                cols = slice(head * HD, head * HD + HD)
                late = slice(width + head * HD, width + head * HD + HD)
                q = q_ref[rows, cols] * jnp.asarray(HD**-0.5, NARROW)
                s = [dot(ref[:, cols], q, NT) + b for ref, b in zip((kvm_ref, kvo_ref), bias)]
                top = jnp.max(jnp.maximum(s[0], s[1]), axis=0, keepdims=True)
                e = [jnp.exp(x - top) for x in s]
                total = jnp.sum(e[0] + e[1], axis=0, keepdims=True)
                o = dot(kvm_ref[:, late], e[0].astype(NARROW), TN)
                o = o + dot(kvo_ref[:, late], e[1].astype(NARROW), TN)
                outs.append(o * (1.0 / total))
                lses.append(top + jnp.log(total))
            att_ref[...] = jnp.transpose(jnp.concatenate(outs, axis=0)).astype(NARROW)
            lse_ref[0:heads, :] = jnp.concatenate(lses, axis=0)

    return kernel


def make_out(i):
    def kernel(a_ref, b_ref, wa_ref, wb_ref, part_ref):
        part_ref[...] = (dot(a_ref[...], wa_ref[i], NT) + dot(b_ref[...], wb_ref[0], NT)).astype(NARROW)

    return kernel


ERF = (0.254829592, -0.284496736, 1.421413741, -1.453152027, 1.061405429)


def gelu_and_slope(x):
    bell = jnp.exp(x * x * -0.5)
    t = 1.0 / (1.0 + (0.3275911 * 0.7071067811865476) * jnp.abs(x))
    tail = t * (ERF[0] + t * (ERF[1] + t * (ERF[2] + t * (ERF[3] + t * ERF[4]))))
    tail = 0.5 * (tail * bell)
    phi = jnp.where(x < 0.0, tail, 1.0 - tail)
    return x * phi, phi + x * (0.3989422804014327 * bell)


def make_mlp(i):
    def kernel(n_ref, up_a_ref, up_b_ref, bias_a_ref, bias_b_ref, down_a_ref, down_b_ref, hid_ref, slope_ref, part_ref):
        y = None
        for slot, j, up_ref, bias_ref, down_ref in (
            (0, i, up_a_ref, bias_a_ref, down_a_ref),
            (1, 0, up_b_ref, bias_b_ref, down_b_ref),
        ):
            for f in range(0, up_ref.shape[2], 256):
                cols = slice(f, f + 256)
                x = dot(n_ref[...], up_ref[j, :, cols]) + bias_ref[i : i + 1, cols]
                hid, slope = gelu_and_slope(x)
                hid_ref[slot, :, cols] = hid.astype(NARROW)
                slope_ref[slot, :, cols] = slope.astype(NARROW)
            z = dot(hid_ref[slot], down_ref[j])
            y = z if y is None else y + z
        part_ref[...] = y.astype(NARROW)

    return kernel


def make_mlp_back(i):
    def kernel(g_ref, down_a_ref, down_b_ref, slope_ref, up_a_ref, up_b_ref, gb_ref, part_ref):
        y = None
        for slot, j, down_ref, up_ref in ((0, i, down_a_ref, up_a_ref), (1, 0, down_b_ref, up_b_ref)):
            dh = dot(g_ref[...], down_ref[j], NT)
            gb = (dh * slope_ref[slot].astype(WIDE)).astype(NARROW)
            gb_ref[slot] = gb
            z = dot(gb, up_ref[j], NT)
            y = z if y is None else y + z
        part_ref[...] = y.astype(NARROW)

    return kernel


def row_sum(x):
    return jnp.sum(fold(x.astype(WIDE)), axis=0, keepdims=True)


def wide_row(x, d):
    return x if x.shape[1] == d else jnp.concatenate([x, jnp.zeros((1, d - x.shape[1]), WIDE)], axis=1)


def put_rows(out_ref, at, rows):
    d = out_ref.shape[1]
    rows = [wide_row(r, d) for r in rows]
    out_ref[at : at + 16, :] = jnp.concatenate(rows + [jnp.zeros((16 - len(rows), d), WIDE)], axis=0).astype(NARROW)
    if out_ref.shape[0] > at + 16:
        out_ref[at + 16 :, :] = jnp.zeros((out_ref.shape[0] - at - 16, d), NARROW)


def mlp_grad_kernel(core_ref, *refs):
    *refs, keep_ref, send_ref = refs
    hid, gl, n, gb = (refs[2 * i : 2 * i + 2] for i in range(4))
    units = hid[0].shape[2]
    d = n[0].shape[1]
    for out_ref, slot in ((send_ref, 1 - core_ref[1]), (keep_ref, core_ref[1])):
        for f in range(0, units, 256):
            y = sum(dot(x[slot, :, f : f + 256], y[...], TN) for x, y in zip(hid, gl))
            out_ref[f : f + 256, :] = y.astype(NARROW)
        for f in range(0, d, 256):
            y = sum(dot(x[:, f : f + 256], y[slot], TN) for x, y in zip(n, gb))
            out_ref[units + f : units + f + 256, :] = y.astype(NARROW)
        put_rows(out_ref, units + d, [sum(row_sum(x[slot]) for x in gb)])


def make_attn_back(width, block, i):
    heads = width // HD

    def kernel(ga_in, gb_in, w_ref, q_ref, kvm_ref, kvo_ref, atta_ref, attb_ref, lsea_ref, lseb_ref, idc_ref, idr_ref,
               dq_ref, dkvm_ref, dkvo_ref, ga_ref, dqt_ref, dd_ref, lse_ref):
        half = q_ref.shape[0]
        at = 0
        for g_in, att_ref, l_ref in ((ga_in, atta_ref, lsea_ref), (gb_in, attb_ref, lseb_ref)):
            size = g_in.shape[0]
            rows = slice(at, at + size)
            ga = dot(g_in[...], w_ref[i]).astype(NARROW)
            ga_ref[rows, :] = ga
            x = ga.astype(WIDE) * att_ref[...].astype(WIDE)
            per = [jnp.sum(x[:, HD * i : HD * i + HD], axis=1, keepdims=True) for i in range(heads)]
            per = jnp.concatenate(per + [jnp.zeros((size, 128 - heads), WIDE)], axis=1)
            dd_ref[:, rows] = jnp.transpose(per)[0:8]
            lse_ref[:, rows] = l_ref[...]
            at += size
        for kv_ref, d_ref, base in ((kvo_ref, dkvo_ref, half), (kvm_ref, dkvm_ref, 0)):
            for at in range(0, half, block):
                keys = slice(at, at + block)
                bias = jnp.where(idc_ref[base + at : base + at + block, 0:1] == idr_ref[0:1, :half], 0.0, MASKED)
                dks, dvs = [], []
                for head in range(heads):
                    cols = slice(head * HD, head * HD + HD)
                    late = slice(width + head * HD, width + head * HD + HD)
                    q = q_ref[:, cols]
                    ga = ga_ref[:, cols]
                    v = kv_ref[keys, late]
                    scaled = kv_ref[keys, cols] * jnp.asarray(HD**-0.5, NARROW)
                    p = jnp.exp(dot(scaled, q, NT) + bias - lse_ref[head : head + 1, :])
                    dvs.append(dot(p.astype(NARROW), ga))
                    ds = (p * (dot(v, ga, NT) - dd_ref[head : head + 1, :])).astype(NARROW)
                    dks.append(dot(ds, q) * HD**-0.5)
                    y = dot(scaled, ds, TN)
                    if base and not at:
                        dqt_ref[cols, :] = y
                    else:
                        dqt_ref[cols, :] += y
                d_ref[keys, :] = jnp.concatenate(dks + dvs, axis=1).astype(NARROW)
        dq_ref[...] = jnp.transpose(dqt_ref[...]).astype(NARROW)

    return kernel


def make_attn_join(number, i):
    def kernel(dqa_ref, dkva_ref, ra_ref, atta_ref, dqb_ref, dkvb_ref, rb_ref, attb_ref,
               wqa_ref, wkva_ref, wqb_ref, wkvb_ref, dq_ref, dkv_ref, att_ref, part_ref):
        size = part_ref.shape[0]
        rows = slice(number * size, number * size + size)
        y = None
        for slot, j, dq1_ref, own_ref, got_ref, a_ref, wq_ref, wkv_ref in (
            (0, i, dqa_ref, dkva_ref, ra_ref, atta_ref, wqa_ref, wkva_ref),
            (1, 0, dqb_ref, dkvb_ref, rb_ref, attb_ref, wqb_ref, wkvb_ref),
        ):
            dq = dq1_ref[rows, :]
            dq_ref[slot] = dq
            att_ref[slot] = a_ref[...]
            dkv = (own_ref[rows, :].astype(WIDE) + got_ref[rows, :].astype(WIDE)).astype(NARROW)
            dkv_ref[slot] = dkv
            z = dot(dq, wq_ref[j], NT) + dot(dkv, wkv_ref[j], NT)
            y = z if y is None else y + z
        part_ref[...] = y.astype(NARROW)

    return kernel


def attn_grad_kernel(core_ref, *refs):
    *refs, keep_ref, send_ref = refs
    dq, dkv, att, n, g = (refs[2 * i : 2 * i + 2] for i in range(5))
    width = dq[0].shape[2]
    for out_ref, slot in ((send_ref, 1 - core_ref[1]), (keep_ref, core_ref[1])):
        many = lambda x, y: sum(dot(a[slot], b[...], TN) for a, b in zip(x, y)).astype(NARROW)
        out_ref[0:width, :] = many(dq, n)
        out_ref[width : 3 * width, :] = many(dkv, n)
        out_ref[3 * width : 4 * width, :] = many(att, g)
        put_rows(
            out_ref,
            4 * width,
            [sum(row_sum(x[slot]) for x in dq), sum(row_sum(x[slot]) for x in dkv)[:, width:]],
        )


def vector_kernel(at_ref, *refs):
    *refs, last_ref, out_ref = refs
    once = jnp.where(at_ref[3] == 0, 1.0, 0.0)
    rows = [refs[0][2:3, :] + refs[1][2:3, :]]
    for a_ref, b_ref in zip(refs[2::2], refs[3::2]):
        rows.append(a_ref[0:3, :] + b_ref[0:3, :])
    rows = jnp.concatenate(rows, axis=0) * once
    last = last_ref[0:3, :]
    count = rows.shape[0] + last.shape[0]
    out_ref[...] = jnp.concatenate([rows, last, jnp.zeros((16 - count, rows.shape[1]), WIDE)], axis=0)


def pack_kernel(at_ref, *refs):
    *refs, out_ref = refs
    at = 0
    for ref in refs:
        width = ref.shape[2]
        out_ref[:, at : at + width] = ref[0]
        at += width


def pair_bits(pairs, core):
    count = pairs.bit_length() - 1
    return [(i + core) % count for i in range(count)]


def by_steps(number, pairs, core):
    return sum(((number >> i) & 1) << bit for i, bit in enumerate(pair_bits(pairs, core)))


def block_of(at_ref, pairs, number, other=0):
    core = at_ref[1] if not other else 1 - at_ref[1]
    return at_ref[0] ^ jnp.where(core == 0, by_steps(number, pairs, 0), by_steps(number, pairs, 1))


def stack_kernel(*refs):
    *refs, out_ref = refs
    at = 0
    for ref in refs:
        count = ref.shape[0]
        out_ref[at : at + count] = ref[...]
        at += count


def place_kernel(at_ref, own_ref, other_ref, *outs):
    pairs, size, _ = own_ref.shape
    for p in range(pairs):
        for ref, which in ((own_ref, 0), (other_ref, 1)):
            core = at_ref[1] if not which else 1 - at_ref[1]
            row = pl.multiple_of((2 * block_of(at_ref, pairs, p, which) + core) * size, size)
            at = 0
            for out_ref in outs:
                width = out_ref.shape[2]
                out_ref[0, pl.ds(row, size), :] = ref[p, :, at : at + width]
                at += width


def make_cut(pairs):
    def kernel(at_ref, keep_ref, got_ref, kept_ref, sent_ref):
        count, size, _ = kept_ref.shape
        for p in range(count):
            number = sum(((p >> (count.bit_length() - 2 - i)) & 1) << (i + 1) for i in range(count.bit_length() - 1))
            for ref, last in ((kept_ref, 0), (sent_ref, 1)):
                rows = pl.ds(pl.multiple_of(block_of(at_ref, pairs, number + last) * size, size), size)
                ref[p] = (keep_ref[rows, :].astype(WIDE) + got_ref[rows, :].astype(WIDE)).astype(NARROW)

    return kernel


def split_kernel(kept_ref, got_ref, out_ref, sent_ref):
    count = out_ref.shape[0]
    for p in range(count):
        out_ref[p] = (kept_ref[p].astype(WIDE) + got_ref[p].astype(WIDE)).astype(NARROW)
        sent_ref[p] = (kept_ref[count + p].astype(WIDE) + got_ref[count + p].astype(WIDE)).astype(NARROW)


def sum_kernel(*refs):
    *refs, out_ref = refs
    out_ref[...] = sum(r[...].astype(WIDE) for r in refs).astype(out_ref.dtype)


def choose_kernel(at_ref, own_ref, got_ref, out_ref):
    out_ref[...] = jnp.where(at_ref[1] == 0, own_ref[...].astype(WIDE), got_ref[...].astype(WIDE)).astype(NARROW)


def order_kernel(at_ref, own_ref, got_ref, out_ref):
    count = own_ref.shape[0]
    for p in range(count):
        out_ref[block_of(at_ref, 2 * count, p)] = own_ref[p]
        out_ref[block_of(at_ref, 2 * count, count + p)] = got_ref[p]


def pair_kernel(at_ref, own_ref, got_ref, out_ref):
    out_ref[at_ref[1]] = own_ref[...]
    out_ref[1 - at_ref[1]] = got_ref[...]


def rows_kernel(at_ref, near_ref, near_got_ref, far_ref, far_got_ref, out_ref):
    near, lower = at_ref[4] == 1, at_ref[3]
    size = near_ref.shape[1]
    pick = lambda a, b: jnp.where(near, a[0].astype(WIDE), b[0].astype(WIDE))
    out_ref[pl.ds(pl.multiple_of(lower * size, size), size), :] = pick(near_ref, far_ref)
    out_ref[pl.ds(pl.multiple_of((1 - lower) * size, size), size), :] = pick(near_got_ref, far_got_ref)


class Layout:
    def __init__(self, mesh):
        self.pairs = mesh.shape["dp"] // 2
        self.tensor = mesh.shape["tensor"]
        self.lowers = self.tensor // 2
        self.everyone = [
            (k, c, h, l)
            for k in range(self.pairs)
            for c in range(2)
            for h in range(2)
            for l in range(self.lowers)
        ]
        self.same = [a for a in self.everyone if a[1] == a[2]]
        self.cross = [a for a in self.everyone if a[1] != a[2]]
        self.core0 = [a for a in self.everyone if a[1] == 0]
        self.core1 = [a for a in self.everyone if a[1] == 1]

    def place(self, k, c, h, l):
        return (2 * k + c) * self.tensor + self.lowers * h + l

    def send(self, value, among, where):
        perm = [(self.place(*a), self.place(*where(*a))) for a in among]
        return lax.ppermute(value, AXES, perm)

    def to_core(self, value, among=None):
        return self.send(value, among or self.everyone, lambda k, c, h, l: (k, 1 - c, h, l))

    def to_lower(self, value, among=None):
        return self.send(value, among or self.everyone, lambda k, c, h, l: (k, c, h, 1 - l))

    def to_upper(self, value):
        return self.send(value, self.everyone, lambda k, c, h, l: (k, c, 1 - h, l))

    def exchange(self, value, step):
        return self.send(
            value, self.everyone, lambda k, c, h, l: (k ^ (1 << pair_bits(self.pairs, c)[step]), c, h, l)
        )


def tie(value, *others):
    return lax.optimization_barrier((value, *others))[0]


def block(value, number, count):
    size = value.shape[0] // count
    return lax.dynamic_slice_in_dim(value, number * size, size, 0)


def pack(run, lay, at, weights, i):
    size = weights[0].shape[1] // (2 * lay.pairs)
    widths = [w.shape[2] for w in weights]
    if size % 16:
        part = 2 * at[0] + at[1]
        return jnp.concatenate([block(w[i], part, 2 * lay.pairs) for w in weights], axis=1)
    spec = lambda w: pl.BlockSpec((1, size, w), lambda _, at: (i, 2 * at[0] + at[1], 0))
    run.last = pl.pallas_call(
        pack_kernel,
        grid_spec=pltpu.PrefetchScalarGridSpec(
            num_scalar_prefetch=1,
            grid=(1,),
            in_specs=[spec(w) for w in widths],
            out_specs=pl.BlockSpec((size, sum(widths)), lambda *_: (0, 0)),
        ),
        out_shape=shape((size, sum(widths))),
        compiler_params=pltpu.CompilerParams(vmem_limit_bytes=VMEM_LIMIT),
        cost_estimate=pl.CostEstimate(flops=int(run.scale * COST), bytes_accessed=int(run.scale * COST // 300), transcendentals=0),
    )(run.after(at), *weights)
    return run.last


class Gather:
    def __init__(self, run, lay, piece):
        self.run, self.lay, self.step = run, lay, 0
        self.value = piece[None]
        self.got = lay.exchange(self.value, 0)

    def next(self):
        self.step += 1
        n, *rest = self.value.shape
        (self.value,) = self.run(0.7, stack_kernel, [shape((2 * n, *rest))], self.value, self.got)
        if 1 << self.step < self.lay.pairs:
            self.got = self.lay.exchange(self.value, self.step)

    def all(self):
        while self.value.shape[0] < self.lay.pairs:
            self.next()
        return self.value

    def ordered(self, at):
        while 2 * self.value.shape[0] < self.lay.pairs:
            self.next()
        _, rows, d = self.value.shape
        (out,) = self.run(0.8, order_kernel, [shape((self.lay.pairs, rows, d))], at, self.value, self.got)
        return out.reshape(-1, d)


def unpack(run, lay, at, own, other, widths):
    size = own.shape[1]
    rows = 2 * lay.pairs * size
    if size % 16 == 0:
        return run(2.0, place_kernel, [shape((1, rows, w)) for w in widths], at, own, other)
    places = [
        (2 * block_of(at, lay.pairs, p, e) + (at[1] ^ e), x[p]) for p in range(lay.pairs) for e, x in ((0, own), (1, other))
    ]
    whole = jnp.zeros((rows, own.shape[2]), own.dtype)
    for place, part in places:
        whole = lax.dynamic_update_slice_in_dim(whole, part, place * size, 0)
    out, start = [], 0
    for w in widths:
        out.append(whole[None, :, start : start + w])
        start += w
    return out


class Scatter:
    def __init__(self, run, lay, at, keep, got):
        self.run, self.lay, self.step = run, lay, 0
        size, d = keep.shape
        parts = [shape((lay.pairs // 2, size // lay.pairs, d))] * 2
        self.kept, sent = run(1.2, make_cut(lay.pairs), parts, at, keep, got)
        self.got = lay.exchange(sent, 0)

    def next(self):
        self.step += 1
        n, *rest = self.kept.shape
        self.kept, sent = self.run(0.7, split_kernel, [shape((n // 2, *rest))] * 2, self.kept, self.got)
        self.got = self.lay.exchange(sent, self.step)

    def across(self):
        while self.kept.shape[0] > 1:
            self.next()
        self.mine = total(self.run, self.kept, self.got)
        self.got = self.lay.send(self.mine, self.lay.core1, lambda k, c, h, l: (k, 0, 1 - h, l))

    def to_core(self):
        self.mine = total(self.run, self.mine, self.got)
        self.got = self.lay.to_core(self.mine, self.lay.core0)

    def gather(self, at):
        (piece,) = self.run(0.4, choose_kernel, [shape(self.mine.shape)], at, self.mine, self.got)
        return Gather(self.run, self.lay, piece[0])


def total(run, *parts):
    return run(0.4, sum_kernel, [shape(parts[0].shape, parts[0].dtype)], *parts)[0]


def both_halves(run, at, piece, got):
    return run(0.5, pair_kernel, [shape((2, *piece.shape))], at, piece, got)[0]


def to_holders(lay, both):
    near = lay.to_lower(both, lay.same)
    far = lay.send(both, lay.same, lambda k, c, h, l: (k, c, 1 - h, l))
    return near, far


def whole_rows(run, at, near, near_got, far, far_got):
    _, size, d = near.shape
    spec = lambda: pl.BlockSpec((1, size, d), lambda i, *_: (i, 0, 0))
    run.last = pl.pallas_call(
        rows_kernel,
        grid_spec=pltpu.PrefetchScalarGridSpec(
            num_scalar_prefetch=1,
            grid=(2,),
            in_specs=[spec() for _ in range(4)],
            out_specs=pl.BlockSpec((2 * size, d), lambda i, *_: (i, 0)),
        ),
        out_shape=shape((4 * size, d), WIDE),
        compiler_params=pltpu.CompilerParams(vmem_limit_bytes=VMEM_LIMIT),
        cost_estimate=pl.CostEstimate(flops=int(2 * COST), bytes_accessed=int(2 * COST // 300), transcendentals=0),
    )(run.after(at), near, near_got, far, far_got)
    return run.last


def body(
    lay,
    tokens_in,
    patch_mask,
    image_ids,
    mask_token,
    norm1_gain,
    norm1_bias,
    qkv_weight,
    qv_bias,
    out_weight,
    out_bias,
    norm2_gain,
    norm2_bias,
    up_weight,
    up_bias,
    down_weight,
    down_bias,
    out_grad,
):
    dp, tensor = lax.axis_index("dp"), lax.axis_index("tensor")
    c, h = dp % 2, tensor // lay.lowers
    at = jnp.stack([dp // 2, c, h, tensor % lay.lowers, c == h]).astype(jnp.int32)
    layers, d, _, width = qkv_weight.shape
    units = up_weight.shape[2]
    half = tokens_in.shape[0] // 2
    chunk = half // 2
    both = range(2)
    by_half = lambda x: x.reshape(2, half, d)

    part_f = shape((chunk, d), WIDE)
    part_b = shape((chunk, d))
    part_q = shape((chunk, width))
    part_l = shape((8, chunk), WIDE)
    part_u = shape((2, chunk, units))
    sums_f = shape((8, d), WIDE)
    rows_q = shape((half, width))
    rows_kv = shape((half, 2 * width))

    run = Clock()
    run.scale = EARLY
    tok_got = lay.to_core(tokens_in, lay.same)
    ids = jnp.stack([image_ids, patch_mask])
    ids_got = lay.to_core(ids, lay.same)
    native = (
        qkv_weight[:, :, 0],
        qkv_weight[:, :, 1:].reshape(layers, d, 2 * width),
        jnp.swapaxes(out_weight, 1, 2),
        up_weight,
        down_weight,
    )
    widths = [w.shape[2] for w in native]
    qv = qv_bias.reshape(2 * layers, width)
    b_qv = [qv, lay.to_upper(qv)]
    b_up = [up_bias, lay.to_upper(up_bias)]
    late = pack(run, lay, at, native[3:], 0)
    first = lay.to_upper(pack(run, lay, at, native[:3], 0))
    following = pack(run, lay, at, native, 1)
    at = tie(at, b_qv[1], b_up[1])
    *rows, idr, idc, mask = run(
        2.5,
        first_kernel,
        [part_f, part_f, part_b, part_b, shape((2, 2 * half), WIDE), shape((2 * half, 8), WIDE), shape((half, 8), WIDE)],
        at,
        by_half(tokens_in),
        by_half(tok_got),
        ids,
        ids_got,
        mask_token[None],
        norm1_gain,
        norm1_bias,
    )
    h_rows, n1 = rows[:2], rows[2:]

    def project(i, s, w, j):
        q, kv = run(0.8, make_qkv(i, j), [rows_q, rows_kv], *n1, w[0], w[1], b_qv[s])
        return q, kv, lay.to_core(kv)

    def attend(s, chunks):
        return run(
            2.0 * len(chunks),
            make_attn(width, chunk, chunks),
            [part_q, part_l] * len(chunks),
            q[s],
            kvm[s],
            kvo[s],
            idc,
            idr,
        )

    fetched = [None] * layers
    kept = []
    for i in range(layers):
        f_w = fetched[i]
        q, kvm, kvo, mine, got = ([None] * 2 for _ in range(5))
        att, lse = ([[None] * 2 for _ in both] for _ in range(2))
        q[0], kvm[0], kvo[0] = project(i, 0, native, i)
        if i:
            f_w = fetched[i] = unpack(run, lay, at, own, other, widths)
            q[1], kvm[1], kvo[1] = project(i, 1, f_w, 0)
        att[0][0], lse[0][0], att[0][1], lse[0][1] = attend(0, (0, 1))
        if i == layers - 1:
            g_got = lay.to_core(tie(out_grad, att[0][0]), lay.same)
        if i == 0:
            late = lay.to_upper(tie(late, first))
            first = Gather(run, lay, tie(first, att[0][0]))
            first.next()
            first.got = tie(first.got, late)
            own = first.all()
            other = lay.to_core(own)
            late = Gather(run, lay, tie(late, own))
            following = lay.to_upper(tie(following, late.value))
            f_w = unpack(run, lay, at, own, other, widths[:3])
            q[1], kvm[1], kvo[1] = project(i, 1, f_w, 0)
            run.scale = 1.0
        for a in both:
            att[1][a], lse[1][a] = attend(1, (a,))
            (mine[a],) = run(0.9, make_out(i), [part_b], att[0][a], att[1][a], native[2], f_w[2])
            got[a] = lay.to_lower(mine[a])
            if i == 0 and a == 0:
                late.next()
        middle, n2, hid, slope, part, got2 = ([None] * 2 for _ in range(6))

        def norm_middle(a):
            middle[a], n2[a] = run(
                0.8, make_norm(i, i), [part_f, part_b], h_rows[a], mine[a], got[a], out_bias, norm2_gain, norm2_bias
            )

        if i == 0:
            norm_middle(0)
            own = late.all()
            other = lay.to_core(own)
            norm_middle(1)
            f_w = fetched[0] = [*f_w, *unpack(run, lay, at, own, other, widths[3:])]
        for a in both:
            if i:
                norm_middle(a)
            hid[a], slope[a], part[a] = run(
                2.9,
                make_mlp(i),
                [part_u, part_u, part_b],
                n2[a],
                native[3],
                f_w[3],
                b_up[0],
                b_up[1],
                native[4],
                f_w[4],
            )
            if i + 1 < layers:
                got2[a] = lay.to_lower(part[a])
                if a == 0:
                    following = Gather(run, lay, tie(following, part[0]))
        kept.append((h_rows, n1, q, kvm, kvo, att, lse, middle, n2, hid, slope))
        if i + 1 < layers:
            following.next()
            h_rows, n1 = [None] * 2, [None] * 2
            for a in both:
                h_rows[a], n1[a] = run(
                    0.8,
                    make_norm(i, i + 1),
                    [part_f, part_b],
                    middle[a],
                    part[a],
                    got2[a],
                    down_bias,
                    norm1_gain,
                    norm1_bias,
                )
            own = following.all()
            other = lay.to_core(own)
    *g, = run(1.5, grad_kernel, [part_f] * 2 + [part_b] * 2 + [sums_f] * 2, at, by_half(out_grad), by_half(g_got))
    g, low, sums = g[:2], g[2:4], g[4:]

    extra = 16 * max(lay.pairs, 4)
    done = {}

    def back_mlp(i):
        for a in both:
            gb[a], mine[a] = run(
                2.0, make_mlp_back(i), [part_u, part_b], low[a], native[4], f_w[4], slope[a], native[3], f_w[3]
            )
            got[a] = lay.to_lower(mine[a])

    def mlp_grads():
        size = units + d + extra
        keep, sent = run(4.2, mlp_grad_kernel, [shape((size, d))] * 2, at, *hid, *low, *n2, *gb)
        return keep, lay.to_core(sent)

    def back_norm(i, a, x, gain):
        return run(1.4, make_norm_back(i), [part_f, part_b, sums_f], g[a], mine[a], got[a], x[a], gain)

    def back_attn(i, s):
        w, j = (native, i) if s == 0 else (f_w, 0)
        dq[s], dkvm[s], dkvo[s] = run(
            SHORT,
            make_attn_back(width, half, j),
            [rows_q, rows_kv, rows_kv],
            *gml,
            w[2],
            q[s],
            kvm[s],
            kvo[s],
            *att[s],
            *lse[s],
            idc,
            idr,
            scratch=[
                pltpu.VMEM((half, width), NARROW),
                pltpu.VMEM((width, half), WIDE),
                pltpu.VMEM((8, half), WIDE),
                pltpu.VMEM((8, half), WIDE),
            ],
        )
        dkvr[s] = lay.to_core(dkvo[s])

    def join(i, a):
        dqs[a], dkvs[a], atts[a], mine[a] = run(
            1.7,
            make_attn_join(a, i),
            [shape((2, chunk, width)), shape((2, chunk, 2 * width)), shape((2, chunk, width)), part_b],
            dq[0],
            dkvm[0],
            dkvr[0],
            att[0][a],
            dq[1],
            dkvm[1],
            dkvr[1],
            att[1][a],
            native[0],
            native[1],
            f_w[0],
            f_w[1],
        )

    def attn_grads():
        size = 4 * width + extra
        keep, sent = run(2.5, attn_grad_kernel, [shape((size, d))] * 2, at, *dqs, *dkvs, *atts, *n1, *gml)
        return keep, lay.to_core(sent)

    i = layers - 1
    h_rows, n1, q, kvm, kvo, att, lse, middle, n2, hid, slope = kept[i]
    f_w = fetched[i]
    gb, mine, got, gm, gml, dq, dkvm, dkvo, dkvr, dqs, dkvs, atts = ([None] * 2 for _ in range(12))
    back_mlp(i)
    mlp1 = mlp_grads()
    vectors = [*sums]
    for a in both:
        gm[a], gml[a], sums[a] = back_norm(i, a, middle, norm2_gain)
        if a == 0:
            (sent,) = run(0.4, pick_kernel, [part_b], at, *part)
            last_got = lay.to_lower(sent)
    vectors += sums
    back_attn(i, 0)
    (rows,) = run(0.5, make_last_rows(i), [part_b], at, *middle, *part, last_got, down_bias)
    rows_got = lay.to_core(rows)
    mlp1 = Scatter(run, lay, at, *mlp1)
    back_attn(i, 1)
    act = both_halves(run, at, rows, rows_got)
    for a in both:
        join(i, a)
        got[a] = lay.to_lower(mine[a])
    attn1 = attn_grads()
    g, new_g, low, sums = gm, [None] * 2, [None] * 2, [None] * 2
    for a in both:
        new_g[a], low[a], sums[a] = back_norm(i, a, h_rows, norm1_gain)
        if a == 0:
            mlp1.next()
    g = new_g
    vectors += sums

    i = 0
    h_rows, n1, q, kvm, kvo, att, lse, middle, n2, hid, slope = kept[i]
    f_w = fetched[i]
    gb, mine, got, gm, gml, dq, dkvm, dkvo, dkvr, dqs, dkvs, atts = ([None] * 2 for _ in range(12))
    back_mlp(i)
    mlp1.across()
    attn1 = Scatter(run, lay, at, *attn1)
    mlp0 = mlp_grads()
    sums = [None] * 2
    for a in both:
        gm[a], gml[a], sums[a] = back_norm(i, a, middle, norm2_gain)
    vectors += sums
    act_near, act_far = to_holders(lay, tie(act, gml[1]))
    mlp0 = Scatter(run, lay, at, *mlp0)
    attn1.next()
    mlp1.to_core()
    back_attn(i, 0)
    attn1.across()
    mlp1 = mlp1.gather(at)
    back_attn(i, 1)
    attn1.to_core()
    mlp0.next()
    mlp1.next()
    act_far_got = lay.to_lower(tie(act_far, mlp1.value), lay.cross)
    for a in both:
        join(i, a)
    (sent,) = run(0.4, pick_kernel, [part_b], at, *mine)
    got = lay.to_lower(sent)
    attn1 = attn1.gather(at)
    attn0 = attn_grads()
    attn1.next()
    mlp0.across()
    tok, last = run(1.4, last_back_kernel, [part_b, sums_f], at, *gm, *mine, got, *h_rows, mask, norm1_gain)
    tok_got = lay.to_core(tok)
    (last,) = run(0.4, vector_kernel, [shape((16, d), WIDE)], at, *vectors, last)
    small = lay.to_core(last)
    attn0 = Scatter(run, lay, at, *attn0)
    activations = whole_rows(run, at, act, act_near, act_far, act_far_got)
    tok = both_halves(run, at, tok, tok_got)
    tok_near, tok_far = to_holders(lay, tok)
    last = total(run, last, small)

    def flip(step):
        return lay.send(last, lay.everyone, lambda k, c, h, l: (k ^ (1 << step), c, h, l))

    small = flip(0)
    mlp0.to_core()
    mlp1 = mlp1.ordered(at)
    last = total(run, last, small)
    small = flip(1)
    attn0.next()
    mlp0 = mlp0.gather(at)
    last = total(run, last, small)
    for step in range(2, lay.pairs.bit_length() - 1):
        last = total(run, last, flip(step))
    small = lay.to_upper(last)
    attn0.across()
    mlp0.next()
    last = total(run, last, small)
    small = lay.to_lower(last)
    attn0.to_core()
    tok_far_got = lay.to_lower(tok_far, lay.cross)
    attn0 = attn0.gather(at)
    mlp0 = mlp0.ordered(at)
    last = total(run, last, small)
    attn1 = attn1.ordered(at)
    mlp = [mlp0, mlp1]
    d_mlp = [jnp.stack([x[a:b] for x in mlp]).astype(WIDE) for a, b in ((0, units), (units, units + d))]
    attn0.got = tie(attn0.got, *d_mlp)
    attn0.next()
    tokens_grad = whole_rows(run, at, tok, tok_near, tok_far, tok_far_got)
    attn0 = attn0.ordered(at)

    attn = [attn0, attn1]
    stack = lambda packs, a, b: jnp.stack([x[a:b] for x in packs]).astype(WIDE)
    d_qkv = jnp.stack([jnp.transpose(x[: 3 * width]) for x in attn]).astype(WIDE)
    def by_layer(row1, row0):
        return jnp.concatenate([last[row0 : row0 + 1], last[row1 : row1 + 1]], axis=0)

    return (
        activations,
        tokens_grad,
        last[12],
        by_layer(4, 10),
        by_layer(5, 11),
        d_qkv.reshape(layers, d, 3, width),
        stack(attn, 4 * width, 4 * width + 2)[:, :, :width],
        stack(attn, 3 * width, 4 * width),
        by_layer(3, 9),
        by_layer(1, 7),
        by_layer(2, 8),
        d_mlp[1],
        stack(mlp, units + d, units + d + 1)[:, 0, :units],
        d_mlp[0],
        by_layer(0, 6),
    )


def solution(mesh):
    lay = Layout(mesh)
    placed = (
        P("dp", None),
        P("dp"),
        P("dp"),
        P(),
        P(),
        P(),
        P(None, None, None, "tensor"),
        P(None, None, "tensor"),
        P(None, "tensor", None),
        P(),
        P(),
        P(),
        P(None, None, "tensor"),
        P(None, "tensor"),
        P(None, "tensor", None),
        P(),
        P("dp", None),
    )
    return jax.shard_map(
        partial(body, lay),
        mesh=mesh,
        in_specs=placed,
        out_specs=(
            P("dp", None),
            P("dp", None),
            P(),
            P(),
            P(),
            P(None, None, None, "tensor"),
            P(None, None, "tensor"),
            P(None, "tensor", None),
            P(),
            P(),
            P(),
            P(None, None, "tensor"),
            P(None, "tensor"),
            P(None, "tensor", None),
            P(),
        ),
        check_vma=False,
    )
```

```python
from functools import partial

import jax
import jax.numpy as jnp
from jax import lax
from jax.experimental import pallas as pl
from jax.experimental.pallas import tpu as pltpu
from jax.sharding import PartitionSpec as P

AXES = ("dp", "tensor")
VMEM_LIMIT = 16 * 2**20
COST = 1.0e10
EARLY = 0.001
SHORT = 0.001
HD = 64
WIDE = jnp.float32
NARROW = jnp.bfloat16
EPSILON = 1e-06
MASKED = -1e30
NN = ((1,), (0,))
NT = ((1,), (1,))
TN = ((0,), (0,))


def dot(a, b, dims=NN):
    return lax.dot_general(a, b, (dims, ((), ())), preferred_element_type=WIDE)


class Clock:
    def __init__(self):
        self.last = None
        self.scale = 1.0

    def __call__(self, us, kernel, outs, *args, scratch=()):
        outs = call(us * self.scale, kernel, outs, self.after(args[0]), *args[1:], scratch=scratch)
        self.last = outs[-1]
        return outs

    def after(self, value):
        return value if self.last is None else lax.optimization_barrier((value, self.last))[0]


def call(us, kernel, outs, *args, scratch=()):
    return pl.pallas_call(
        kernel,
        out_shape=outs,
        in_specs=[pl.BlockSpec(memory_space=pltpu.SMEM if x.ndim == 1 else pltpu.VMEM) for x in args],
        out_specs=[pl.BlockSpec(memory_space=pltpu.VMEM)] * len(outs),
        scratch_shapes=list(scratch),
        compiler_params=pltpu.CompilerParams(vmem_limit_bytes=VMEM_LIMIT),
        cost_estimate=pl.CostEstimate(flops=int(us * COST), bytes_accessed=int(us * COST // 300), transcendentals=0),
    )(*args)


def shape(s, kind=NARROW):
    return jax.ShapeDtypeStruct(s, kind)


def first_kernel(at_ref, own_ref, got_ref, ids_ref, ids_got_ref, fill_ref, gain_ref, shift_ref,
                 ha_ref, hb_ref, na_ref, nb_ref, idr_ref, idc_ref, mask_ref):
    core, near = at_ref[1], at_ref[4] == 1
    half = own_ref.shape[1]
    both = jnp.where(near, ids_ref[...], ids_got_ref[...]).astype(WIDE)
    swapped = jnp.concatenate([both[:, half:], both[:, :half]], axis=1)
    both = jnp.where(core == 0, both, swapped)
    idr_ref[...] = both
    column = jnp.transpose(jnp.concatenate([both, jnp.zeros((6, 2 * half), WIDE)], axis=0))
    idc_ref[...] = column
    mask_ref[...] = column[:half, 1:2] + jnp.zeros((half, 8), WIDE)
    chunk = ha_ref.shape[0]
    for h_ref, n_ref, at in ((ha_ref, na_ref, 0), (hb_ref, nb_ref, chunk)):
        for r in range(0, chunk, 128):
            rows = slice(at + r, at + r + 128)
            x = jnp.where(near, own_ref[core, rows, :].astype(WIDE), got_ref[core, rows, :].astype(WIDE))
            h = jnp.where(mask_ref[rows, 0:1] == 1.0, fill_ref[...], x)
            h_ref[r : r + 128, :] = h
            centre, inv = stats(h)
            n_ref[r : r + 128, :] = (centre * inv * gain_ref[0:1, :] + shift_ref[0:1, :]).astype(NARROW)


def grad_kernel(at_ref, own_ref, got_ref, ga_ref, gb_ref, la_ref, lb_ref, sa_ref, sb_ref):
    core, near = at_ref[1], at_ref[4] == 1
    chunk, d = ga_ref.shape
    zero = jnp.zeros((1, d), WIDE)
    for g_ref, l_ref, s_ref, at in ((ga_ref, la_ref, sa_ref, 0), (gb_ref, lb_ref, sb_ref, chunk)):
        total = jnp.zeros((8, d), WIDE)
        for r in range(0, chunk, 64):
            rows = slice(at + r, at + r + 64)
            g = jnp.where(near, own_ref[core, rows, :], got_ref[core, rows, :])
            g_ref[r : r + 64, :] = g
            l_ref[r : r + 64, :] = g.astype(NARROW)
            total += fold(g)
        total = jnp.sum(total, axis=0, keepdims=True)
        s_ref[...] = jnp.concatenate([zero, zero, total, jnp.zeros((5, d), WIDE)], axis=0)


def stats(x):
    mean = jnp.mean(x, axis=-1, keepdims=True)
    centre = x - mean
    spread = jnp.mean(centre * centre, axis=-1, keepdims=True)
    return centre, lax.rsqrt(spread + EPSILON)


def fold(x):
    return jnp.sum(x.reshape(x.shape[0] // 8, 8, x.shape[1]), axis=0)


def make_norm(i, j):
    def kernel(x_ref, a_ref, b_ref, bias_ref, gain_ref, shift_ref, h_ref, n_ref):
        for r in range(0, x_ref.shape[0], 128):
            rows = slice(r, r + 128)
            h = x_ref[rows, :] + (a_ref[rows, :].astype(WIDE) + b_ref[rows, :].astype(WIDE)) + bias_ref[i : i + 1, :]
            h_ref[rows, :] = h
            centre, inv = stats(h)
            n_ref[rows, :] = (centre * inv * gain_ref[j : j + 1, :] + shift_ref[j : j + 1, :]).astype(NARROW)

    return kernel


def make_last_rows(i):
    def kernel(at_ref, xa_ref, xb_ref, pa_ref, pb_ref, got_ref, bias_ref, out_ref):
        lower = at_ref[3] == 0
        x = jnp.where(lower, xa_ref[...], xb_ref[...])
        p = jnp.where(lower, pa_ref[...].astype(WIDE), pb_ref[...].astype(WIDE))
        out_ref[...] = (x + (p + got_ref[...].astype(WIDE)) + bias_ref[i : i + 1, :]).astype(NARROW)

    return kernel


def pick_kernel(at_ref, a_ref, b_ref, out_ref):
    out_ref[...] = jnp.where(at_ref[3] == 0, b_ref[...].astype(WIDE), a_ref[...].astype(WIDE)).astype(NARROW)


def norm_back(rows, gn, x, g, gain):
    centre, inv = stats(x)
    xhat = centre * inv
    e = gn * gain
    mean_e = jnp.mean(e, axis=-1, keepdims=True)
    mean_ex = jnp.mean(e * xhat, axis=-1, keepdims=True)
    return g + inv * (e - mean_e - xhat * mean_ex), gn * xhat


def put_sums(sums_ref, sums):
    d = sums_ref.shape[1]
    sums = [jnp.sum(x, axis=0, keepdims=True) for x in sums]
    sums_ref[...] = jnp.concatenate(sums + [jnp.zeros((8 - len(sums), d), WIDE)], axis=0)


def make_norm_back(i):
    def kernel(g_ref, a_ref, b_ref, x_ref, gain_ref, out_ref, low_ref, sums_ref):
        chunk, d = x_ref.shape
        sums = [jnp.zeros((8, d), WIDE)] * 3
        for r in range(0, chunk, 64):
            rows = slice(r, r + 64)
            gn = a_ref[rows, :].astype(WIDE) + b_ref[rows, :].astype(WIDE)
            out, scaled = norm_back(rows, gn, x_ref[rows, :], g_ref[rows, :], gain_ref[i : i + 1, :])
            out_ref[rows, :] = out
            low_ref[rows, :] = out.astype(NARROW)
            sums = [s + fold(y) for s, y in zip(sums, (scaled, gn, out))]
        put_sums(sums_ref, sums)

    return kernel


def last_back_kernel(at_ref, ga_ref, gb_ref, pa_ref, pb_ref, got_ref, xa_ref, xb_ref, mask_ref, gain_ref, low_ref, sums_ref):
    lower = at_ref[3]
    first = lower == 0
    chunk, d = xa_ref.shape
    sums = [jnp.zeros((8, d), WIDE)] * 3
    pick = lambda a, b, rows: jnp.where(first, a[rows, :].astype(WIDE), b[rows, :].astype(WIDE))
    for r in range(0, chunk, 64):
        rows = slice(r, r + 64)
        gn = pick(pa_ref, pb_ref, rows) + got_ref[rows, :].astype(WIDE)
        out, scaled = norm_back(
            rows, gn, pick(xa_ref, xb_ref, rows), pick(ga_ref, gb_ref, rows), gain_ref[0:1, :]
        )
        masked = mask_ref[pl.ds(pl.multiple_of(lower * chunk, chunk) + r, 64), 0:1] == 1.0
        low_ref[rows, :] = jnp.where(masked, 0.0, out).astype(NARROW)
        sums = [s + fold(y) for s, y in zip(sums, (scaled, gn, jnp.where(masked, out, 0.0)))]
    put_sums(sums_ref, sums)


def make_qkv(i, j):
    def kernel(na_ref, nb_ref, wq_ref, wkv_ref, b_ref, q_ref, kv_ref):
        chunk = na_ref.shape[0]
        width = wq_ref.shape[2]
        zero = jnp.zeros((1, width), WIDE)
        for n_ref, at in ((na_ref, 0), (nb_ref, chunk)):
            rows = slice(at, at + chunk)
            n = n_ref[...]
            q_ref[rows, :] = (dot(n, wq_ref[j]) + b_ref[2 * i : 2 * i + 1, :]).astype(NARROW)
            bias = jnp.concatenate([zero, b_ref[2 * i + 1 : 2 * i + 2, :]], axis=1)
            kv_ref[rows, :] = (dot(n, wkv_ref[j]) + bias).astype(NARROW)

    return kernel


def make_attn(width, chunk, chunks):
    heads = width // HD

    def kernel(q_ref, kvm_ref, kvo_ref, idc_ref, idr_ref, *refs):
        half = q_ref.shape[0]
        for n, number in enumerate(chunks):
            att_ref, lse_ref = refs[2 * n : 2 * n + 2]
            rows = slice(number * chunk, number * chunk + chunk)
            idr = idr_ref[0:1, rows]
            bias = [jnp.where(idc_ref[x : x + half, 0:1] == idr, 0.0, MASKED) for x in (0, half)]
            outs, lses = [], []
            for head in range(heads):
                cols = slice(head * HD, head * HD + HD)
                late = slice(width + head * HD, width + head * HD + HD)
                q = q_ref[rows, cols] * jnp.asarray(HD**-0.5, NARROW)
                s = [dot(ref[:, cols], q, NT) + b for ref, b in zip((kvm_ref, kvo_ref), bias)]
                top = jnp.max(jnp.maximum(s[0], s[1]), axis=0, keepdims=True)
                e = [jnp.exp(x - top) for x in s]
                total = jnp.sum(e[0] + e[1], axis=0, keepdims=True)
                o = dot(kvm_ref[:, late], e[0].astype(NARROW), TN)
                o = o + dot(kvo_ref[:, late], e[1].astype(NARROW), TN)
                outs.append(o * (1.0 / total))
                lses.append(top + jnp.log(total))
            att_ref[...] = jnp.transpose(jnp.concatenate(outs, axis=0)).astype(NARROW)
            lse_ref[0:heads, :] = jnp.concatenate(lses, axis=0)

    return kernel


def make_out(i):
    def kernel(a_ref, b_ref, wa_ref, wb_ref, part_ref):
        part_ref[...] = (dot(a_ref[...], wa_ref[i], NT) + dot(b_ref[...], wb_ref[0], NT)).astype(NARROW)

    return kernel


ERF = (0.254829592, -0.284496736, 1.421413741, -1.453152027, 1.061405429)


def gelu_and_slope(x):
    bell = jnp.exp(x * x * -0.5)
    t = 1.0 / (1.0 + (0.3275911 * 0.7071067811865476) * jnp.abs(x))
    tail = t * (ERF[0] + t * (ERF[1] + t * (ERF[2] + t * (ERF[3] + t * ERF[4]))))
    tail = 0.5 * (tail * bell)
    phi = jnp.where(x < 0.0, tail, 1.0 - tail)
    return x * phi, phi + x * (0.3989422804014327 * bell)


def make_mlp(i):
    def kernel(n_ref, up_a_ref, up_b_ref, bias_a_ref, bias_b_ref, down_a_ref, down_b_ref, hid_ref, slope_ref, part_ref):
        y = None
        for slot, j, up_ref, bias_ref, down_ref in (
            (0, i, up_a_ref, bias_a_ref, down_a_ref),
            (1, 0, up_b_ref, bias_b_ref, down_b_ref),
        ):
            for f in range(0, up_ref.shape[2], 256):
                cols = slice(f, f + 256)
                x = dot(n_ref[...], up_ref[j, :, cols]) + bias_ref[i : i + 1, cols]
                hid, slope = gelu_and_slope(x)
                hid_ref[slot, :, cols] = hid.astype(NARROW)
                slope_ref[slot, :, cols] = slope.astype(NARROW)
            z = dot(hid_ref[slot], down_ref[j])
            y = z if y is None else y + z
        part_ref[...] = y.astype(NARROW)

    return kernel


def make_mlp_back(i):
    def kernel(g_ref, down_a_ref, down_b_ref, slope_ref, up_a_ref, up_b_ref, gb_ref, part_ref):
        y = None
        for slot, j, down_ref, up_ref in ((0, i, down_a_ref, up_a_ref), (1, 0, down_b_ref, up_b_ref)):
            dh = dot(g_ref[...], down_ref[j], NT)
            gb = (dh * slope_ref[slot].astype(WIDE)).astype(NARROW)
            gb_ref[slot] = gb
            z = dot(gb, up_ref[j], NT)
            y = z if y is None else y + z
        part_ref[...] = y.astype(NARROW)

    return kernel


def row_sum(x):
    return jnp.sum(fold(x.astype(WIDE)), axis=0, keepdims=True)


def wide_row(x, d):
    return x if x.shape[1] == d else jnp.concatenate([x, jnp.zeros((1, d - x.shape[1]), WIDE)], axis=1)


def put_rows(out_ref, at, rows):
    d = out_ref.shape[1]
    rows = [wide_row(r, d) for r in rows]
    out_ref[at : at + 16, :] = jnp.concatenate(rows + [jnp.zeros((16 - len(rows), d), WIDE)], axis=0).astype(NARROW)
    if out_ref.shape[0] > at + 16:
        out_ref[at + 16 :, :] = jnp.zeros((out_ref.shape[0] - at - 16, d), NARROW)


def mlp_grad_kernel(core_ref, *refs):
    *refs, keep_ref, send_ref = refs
    hid, gl, n, gb = (refs[2 * i : 2 * i + 2] for i in range(4))
    units = hid[0].shape[2]
    d = n[0].shape[1]
    for out_ref, slot in ((send_ref, 1 - core_ref[1]), (keep_ref, core_ref[1])):
        for f in range(0, units, 256):
            y = sum(dot(x[slot, :, f : f + 256], y[...], TN) for x, y in zip(hid, gl))
            out_ref[f : f + 256, :] = y.astype(NARROW)
        for f in range(0, d, 256):
            y = sum(dot(x[:, f : f + 256], y[slot], TN) for x, y in zip(n, gb))
            out_ref[units + f : units + f + 256, :] = y.astype(NARROW)
        put_rows(out_ref, units + d, [sum(row_sum(x[slot]) for x in gb)])


def make_attn_back(width, block, i):
    heads = width // HD

    def kernel(ga_in, gb_in, w_ref, q_ref, kvm_ref, kvo_ref, atta_ref, attb_ref, lsea_ref, lseb_ref, idc_ref, idr_ref,
               dq_ref, dkvm_ref, dkvo_ref, ga_ref, dqt_ref, dd_ref, lse_ref):
        half = q_ref.shape[0]
        at = 0
        for g_in, att_ref, l_ref in ((ga_in, atta_ref, lsea_ref), (gb_in, attb_ref, lseb_ref)):
            size = g_in.shape[0]
            rows = slice(at, at + size)
            ga = dot(g_in[...], w_ref[i]).astype(NARROW)
            ga_ref[rows, :] = ga
            x = ga.astype(WIDE) * att_ref[...].astype(WIDE)
            per = [jnp.sum(x[:, HD * i : HD * i + HD], axis=1, keepdims=True) for i in range(heads)]
            per = jnp.concatenate(per + [jnp.zeros((size, 128 - heads), WIDE)], axis=1)
            dd_ref[:, rows] = jnp.transpose(per)[0:8]
            lse_ref[:, rows] = l_ref[...]
            at += size
        for kv_ref, d_ref, base in ((kvo_ref, dkvo_ref, half), (kvm_ref, dkvm_ref, 0)):
            for at in range(0, half, block):
                keys = slice(at, at + block)
                bias = jnp.where(idc_ref[base + at : base + at + block, 0:1] == idr_ref[0:1, :half], 0.0, MASKED)
                dks, dvs = [], []
                for head in range(heads):
                    cols = slice(head * HD, head * HD + HD)
                    late = slice(width + head * HD, width + head * HD + HD)
                    q = q_ref[:, cols]
                    ga = ga_ref[:, cols]
                    v = kv_ref[keys, late]
                    scaled = kv_ref[keys, cols] * jnp.asarray(HD**-0.5, NARROW)
                    p = jnp.exp(dot(scaled, q, NT) + bias - lse_ref[head : head + 1, :])
                    dvs.append(dot(p.astype(NARROW), ga))
                    ds = (p * (dot(v, ga, NT) - dd_ref[head : head + 1, :])).astype(NARROW)
                    dks.append(dot(ds, q) * HD**-0.5)
                    y = dot(scaled, ds, TN)
                    if base and not at:
                        dqt_ref[cols, :] = y
                    else:
                        dqt_ref[cols, :] += y
                d_ref[keys, :] = jnp.concatenate(dks + dvs, axis=1).astype(NARROW)
        dq_ref[...] = jnp.transpose(dqt_ref[...]).astype(NARROW)

    return kernel


def make_attn_join(number, i):
    def kernel(dqa_ref, dkva_ref, ra_ref, atta_ref, dqb_ref, dkvb_ref, rb_ref, attb_ref,
               wqa_ref, wkva_ref, wqb_ref, wkvb_ref, dq_ref, dkv_ref, att_ref, part_ref):
        size = part_ref.shape[0]
        rows = slice(number * size, number * size + size)
        y = None
        for slot, j, dq1_ref, own_ref, got_ref, a_ref, wq_ref, wkv_ref in (
            (0, i, dqa_ref, dkva_ref, ra_ref, atta_ref, wqa_ref, wkva_ref),
            (1, 0, dqb_ref, dkvb_ref, rb_ref, attb_ref, wqb_ref, wkvb_ref),
        ):
            dq = dq1_ref[rows, :]
            dq_ref[slot] = dq
            att_ref[slot] = a_ref[...]
            dkv = (own_ref[rows, :].astype(WIDE) + got_ref[rows, :].astype(WIDE)).astype(NARROW)
            dkv_ref[slot] = dkv
            z = dot(dq, wq_ref[j], NT) + dot(dkv, wkv_ref[j], NT)
            y = z if y is None else y + z
        part_ref[...] = y.astype(NARROW)

    return kernel


def attn_grad_kernel(core_ref, *refs):
    *refs, keep_ref, send_ref = refs
    dq, dkv, att, n, g = (refs[2 * i : 2 * i + 2] for i in range(5))
    width = dq[0].shape[2]
    for out_ref, slot in ((send_ref, 1 - core_ref[1]), (keep_ref, core_ref[1])):
        many = lambda x, y: sum(dot(a[slot], b[...], TN) for a, b in zip(x, y)).astype(NARROW)
        out_ref[0:width, :] = many(dq, n)
        out_ref[width : 3 * width, :] = many(dkv, n)
        out_ref[3 * width : 4 * width, :] = many(att, g)
        put_rows(
            out_ref,
            4 * width,
            [sum(row_sum(x[slot]) for x in dq), sum(row_sum(x[slot]) for x in dkv)[:, width:]],
        )


def vector_kernel(at_ref, *refs):
    *refs, last_ref, out_ref = refs
    once = jnp.where(at_ref[3] == 0, 1.0, 0.0)
    rows = [refs[0][2:3, :] + refs[1][2:3, :]]
    for a_ref, b_ref in zip(refs[2::2], refs[3::2]):
        rows.append(a_ref[0:3, :] + b_ref[0:3, :])
    rows = jnp.concatenate(rows, axis=0) * once
    last = last_ref[0:3, :]
    count = rows.shape[0] + last.shape[0]
    out_ref[...] = jnp.concatenate([rows, last, jnp.zeros((16 - count, rows.shape[1]), WIDE)], axis=0)


def pack_kernel(at_ref, *refs):
    *refs, out_ref = refs
    at = 0
    for ref in refs:
        width = ref.shape[2]
        out_ref[:, at : at + width] = ref[0]
        at += width


def pair_bits(pairs, core):
    count = pairs.bit_length() - 1
    return [(i + core) % count for i in range(count)]


def by_steps(number, pairs, core):
    return sum(((number >> i) & 1) << bit for i, bit in enumerate(pair_bits(pairs, core)))


def block_of(at_ref, pairs, number, other=0):
    core = at_ref[1] if not other else 1 - at_ref[1]
    return at_ref[0] ^ jnp.where(core == 0, by_steps(number, pairs, 0), by_steps(number, pairs, 1))


def stack_kernel(*refs):
    *refs, out_ref = refs
    at = 0
    for ref in refs:
        count = ref.shape[0]
        out_ref[at : at + count] = ref[...]
        at += count


def place_kernel(at_ref, own_ref, other_ref, *outs):
    pairs, size, _ = own_ref.shape
    for p in range(pairs):
        for ref, which in ((own_ref, 0), (other_ref, 1)):
            core = at_ref[1] if not which else 1 - at_ref[1]
            row = pl.multiple_of((2 * block_of(at_ref, pairs, p, which) + core) * size, size)
            at = 0
            for out_ref in outs:
                width = out_ref.shape[2]
                out_ref[0, pl.ds(row, size), :] = ref[p, :, at : at + width]
                at += width


def make_cut(pairs):
    def kernel(at_ref, keep_ref, got_ref, kept_ref, sent_ref):
        count, size, _ = kept_ref.shape
        for p in range(count):
            number = sum(((p >> (count.bit_length() - 2 - i)) & 1) << (i + 1) for i in range(count.bit_length() - 1))
            for ref, last in ((kept_ref, 0), (sent_ref, 1)):
                rows = pl.ds(pl.multiple_of(block_of(at_ref, pairs, number + last) * size, size), size)
                ref[p] = (keep_ref[rows, :].astype(WIDE) + got_ref[rows, :].astype(WIDE)).astype(NARROW)

    return kernel


def split_kernel(kept_ref, got_ref, out_ref, sent_ref):
    count = out_ref.shape[0]
    for p in range(count):
        out_ref[p] = (kept_ref[p].astype(WIDE) + got_ref[p].astype(WIDE)).astype(NARROW)
        sent_ref[p] = (kept_ref[count + p].astype(WIDE) + got_ref[count + p].astype(WIDE)).astype(NARROW)


def sum_kernel(*refs):
    *refs, out_ref = refs
    out_ref[...] = sum(r[...].astype(WIDE) for r in refs).astype(out_ref.dtype)


def choose_kernel(at_ref, own_ref, got_ref, out_ref):
    out_ref[...] = jnp.where(at_ref[1] == 0, own_ref[...].astype(WIDE), got_ref[...].astype(WIDE)).astype(NARROW)


def order_kernel(at_ref, own_ref, got_ref, out_ref):
    count = own_ref.shape[0]
    for p in range(count):
        out_ref[block_of(at_ref, 2 * count, p)] = own_ref[p]
        out_ref[block_of(at_ref, 2 * count, count + p)] = got_ref[p]


def pair_kernel(at_ref, own_ref, got_ref, out_ref):
    out_ref[at_ref[1]] = own_ref[...]
    out_ref[1 - at_ref[1]] = got_ref[...]


def rows_kernel(at_ref, near_ref, near_got_ref, far_ref, far_got_ref, out_ref):
    near, lower = at_ref[4] == 1, at_ref[3]
    size = near_ref.shape[1]
    pick = lambda a, b: jnp.where(near, a[0].astype(WIDE), b[0].astype(WIDE))
    out_ref[pl.ds(pl.multiple_of(lower * size, size), size), :] = pick(near_ref, far_ref)
    out_ref[pl.ds(pl.multiple_of((1 - lower) * size, size), size), :] = pick(near_got_ref, far_got_ref)


class Layout:
    def __init__(self, mesh):
        self.pairs = mesh.shape["dp"] // 2
        self.tensor = mesh.shape["tensor"]
        self.lowers = self.tensor // 2
        self.everyone = [
            (k, c, h, l)
            for k in range(self.pairs)
            for c in range(2)
            for h in range(2)
            for l in range(self.lowers)
        ]
        self.same = [a for a in self.everyone if a[1] == a[2]]
        self.cross = [a for a in self.everyone if a[1] != a[2]]
        self.core0 = [a for a in self.everyone if a[1] == 0]
        self.core1 = [a for a in self.everyone if a[1] == 1]

    def place(self, k, c, h, l):
        return (2 * k + c) * self.tensor + self.lowers * h + l

    def send(self, value, among, where):
        perm = [(self.place(*a), self.place(*where(*a))) for a in among]
        return lax.ppermute(value, AXES, perm)

    def to_core(self, value, among=None):
        return self.send(value, among or self.everyone, lambda k, c, h, l: (k, 1 - c, h, l))

    def to_lower(self, value, among=None):
        return self.send(value, among or self.everyone, lambda k, c, h, l: (k, c, h, 1 - l))

    def to_upper(self, value):
        return self.send(value, self.everyone, lambda k, c, h, l: (k, c, 1 - h, l))

    def exchange(self, value, step):
        return self.send(
            value, self.everyone, lambda k, c, h, l: (k ^ (1 << pair_bits(self.pairs, c)[step]), c, h, l)
        )


def tie(value, *others):
    return lax.optimization_barrier((value, *others))[0]


def block(value, number, count):
    size = value.shape[0] // count
    return lax.dynamic_slice_in_dim(value, number * size, size, 0)


def pack(run, lay, at, weights, i):
    size = weights[0].shape[1] // (2 * lay.pairs)
    widths = [w.shape[2] for w in weights]
    if size % 16:
        part = 2 * at[0] + at[1]
        return jnp.concatenate([block(w[i], part, 2 * lay.pairs) for w in weights], axis=1)
    spec = lambda w: pl.BlockSpec((1, size, w), lambda _, at: (i, 2 * at[0] + at[1], 0))
    run.last = pl.pallas_call(
        pack_kernel,
        grid_spec=pltpu.PrefetchScalarGridSpec(
            num_scalar_prefetch=1,
            grid=(1,),
            in_specs=[spec(w) for w in widths],
            out_specs=pl.BlockSpec((size, sum(widths)), lambda *_: (0, 0)),
        ),
        out_shape=shape((size, sum(widths))),
        compiler_params=pltpu.CompilerParams(vmem_limit_bytes=VMEM_LIMIT),
        cost_estimate=pl.CostEstimate(flops=int(run.scale * COST), bytes_accessed=int(run.scale * COST // 300), transcendentals=0),
    )(run.after(at), *weights)
    return run.last


class Gather:
    def __init__(self, run, lay, piece):
        self.run, self.lay, self.step = run, lay, 0
        self.value = piece[None]
        self.got = lay.exchange(self.value, 0)

    def next(self):
        self.step += 1
        n, *rest = self.value.shape
        (self.value,) = self.run(0.7, stack_kernel, [shape((2 * n, *rest))], self.value, self.got)
        if 1 << self.step < self.lay.pairs:
            self.got = self.lay.exchange(self.value, self.step)

    def all(self):
        while self.value.shape[0] < self.lay.pairs:
            self.next()
        return self.value

    def ordered(self, at):
        while 2 * self.value.shape[0] < self.lay.pairs:
            self.next()
        _, rows, d = self.value.shape
        (out,) = self.run(0.8, order_kernel, [shape((self.lay.pairs, rows, d))], at, self.value, self.got)
        return out.reshape(-1, d)


def unpack(run, lay, at, own, other, widths):
    size = own.shape[1]
    rows = 2 * lay.pairs * size
    if size % 16 == 0:
        return run(2.0, place_kernel, [shape((1, rows, w)) for w in widths], at, own, other)
    places = [
        (2 * block_of(at, lay.pairs, p, e) + (at[1] ^ e), x[p]) for p in range(lay.pairs) for e, x in ((0, own), (1, other))
    ]
    whole = jnp.zeros((rows, own.shape[2]), own.dtype)
    for place, part in places:
        whole = lax.dynamic_update_slice_in_dim(whole, part, place * size, 0)
    out, start = [], 0
    for w in widths:
        out.append(whole[None, :, start : start + w])
        start += w
    return out


class Scatter:
    def __init__(self, run, lay, at, keep, got):
        self.run, self.lay, self.step = run, lay, 0
        size, d = keep.shape
        parts = [shape((lay.pairs // 2, size // lay.pairs, d))] * 2
        self.kept, sent = run(1.2, make_cut(lay.pairs), parts, at, keep, got)
        self.got = lay.exchange(sent, 0)

    def next(self):
        self.step += 1
        n, *rest = self.kept.shape
        self.kept, sent = self.run(0.7, split_kernel, [shape((n // 2, *rest))] * 2, self.kept, self.got)
        self.got = self.lay.exchange(sent, self.step)

    def across(self):
        while self.kept.shape[0] > 1:
            self.next()
        self.mine = total(self.run, self.kept, self.got)
        self.got = self.lay.send(self.mine, self.lay.core1, lambda k, c, h, l: (k, 0, 1 - h, l))

    def to_core(self):
        self.mine = total(self.run, self.mine, self.got)
        self.got = self.lay.to_core(self.mine, self.lay.core0)

    def gather(self, at):
        (piece,) = self.run(0.4, choose_kernel, [shape(self.mine.shape)], at, self.mine, self.got)
        return Gather(self.run, self.lay, piece[0])


def total(run, *parts):
    return run(0.4, sum_kernel, [shape(parts[0].shape, parts[0].dtype)], *parts)[0]


def both_halves(run, at, piece, got):
    return run(0.5, pair_kernel, [shape((2, *piece.shape))], at, piece, got)[0]


def to_holders(lay, both):
    near = lay.to_lower(both, lay.same)
    far = lay.send(both, lay.same, lambda k, c, h, l: (k, c, 1 - h, l))
    return near, far


def whole_rows(run, at, near, near_got, far, far_got):
    _, size, d = near.shape
    spec = lambda: pl.BlockSpec((1, size, d), lambda i, *_: (i, 0, 0))
    run.last = pl.pallas_call(
        rows_kernel,
        grid_spec=pltpu.PrefetchScalarGridSpec(
            num_scalar_prefetch=1,
            grid=(2,),
            in_specs=[spec() for _ in range(4)],
            out_specs=pl.BlockSpec((2 * size, d), lambda i, *_: (i, 0)),
        ),
        out_shape=shape((4 * size, d), WIDE),
        compiler_params=pltpu.CompilerParams(vmem_limit_bytes=VMEM_LIMIT),
        cost_estimate=pl.CostEstimate(flops=int(2 * COST), bytes_accessed=int(2 * COST // 300), transcendentals=0),
    )(run.after(at), near, near_got, far, far_got)
    return run.last


def body(
    lay,
    tokens_in,
    patch_mask,
    image_ids,
    mask_token,
    norm1_gain,
    norm1_bias,
    qkv_weight,
    qv_bias,
    out_weight,
    out_bias,
    norm2_gain,
    norm2_bias,
    up_weight,
    up_bias,
    down_weight,
    down_bias,
    out_grad,
):
    dp, tensor = lax.axis_index("dp"), lax.axis_index("tensor")
    c, h = dp % 2, tensor // lay.lowers
    at = jnp.stack([dp // 2, c, h, tensor % lay.lowers, c == h]).astype(jnp.int32)
    layers, d, _, width = qkv_weight.shape
    units = up_weight.shape[2]
    half = tokens_in.shape[0] // 2
    chunk = half // 2
    both = range(2)
    by_half = lambda x: x.reshape(2, half, d)

    part_f = shape((chunk, d), WIDE)
    part_b = shape((chunk, d))
    part_q = shape((chunk, width))
    part_l = shape((8, chunk), WIDE)
    part_u = shape((2, chunk, units))
    sums_f = shape((8, d), WIDE)
    rows_q = shape((half, width))
    rows_kv = shape((half, 2 * width))

    run = Clock()
    run.scale = EARLY
    tok_got = lay.to_core(tokens_in, lay.same)
    ids = jnp.stack([image_ids, patch_mask])
    ids_got = lay.to_core(ids, lay.same)
    native = (
        qkv_weight[:, :, 0],
        qkv_weight[:, :, 1:].reshape(layers, d, 2 * width),
        jnp.swapaxes(out_weight, 1, 2),
        up_weight,
        down_weight,
    )
    widths = [w.shape[2] for w in native]
    qv = qv_bias.reshape(2 * layers, width)
    b_qv = [qv, lay.to_upper(qv)]
    b_up = [up_bias, lay.to_upper(up_bias)]
    late = pack(run, lay, at, native[3:], 0)
    first = lay.to_upper(pack(run, lay, at, native[:3], 0))
    following = pack(run, lay, at, native, 1)
    at = tie(at, b_qv[1], b_up[1])
    *rows, idr, idc, mask = run(
        2.5,
        first_kernel,
        [part_f, part_f, part_b, part_b, shape((2, 2 * half), WIDE), shape((2 * half, 8), WIDE), shape((half, 8), WIDE)],
        at,
        by_half(tokens_in),
        by_half(tok_got),
        ids,
        ids_got,
        mask_token[None],
        norm1_gain,
        norm1_bias,
    )
    h_rows, n1 = rows[:2], rows[2:]

    def project(i, s, w, j):
        q, kv = run(0.8, make_qkv(i, j), [rows_q, rows_kv], *n1, w[0], w[1], b_qv[s])
        return q, kv, lay.to_core(kv)

    def attend(s, chunks):
        return run(
            2.0 * len(chunks),
            make_attn(width, chunk, chunks),
            [part_q, part_l] * len(chunks),
            q[s],
            kvm[s],
            kvo[s],
            idc,
            idr,
        )

    fetched = [None] * layers
    kept = []
    for i in range(layers):
        f_w = fetched[i]
        q, kvm, kvo, mine, got = ([None] * 2 for _ in range(5))
        att, lse = ([[None] * 2 for _ in both] for _ in range(2))
        q[0], kvm[0], kvo[0] = project(i, 0, native, i)
        if i:
            f_w = fetched[i] = unpack(run, lay, at, own, other, widths)
            q[1], kvm[1], kvo[1] = project(i, 1, f_w, 0)
        att[0][0], lse[0][0], att[0][1], lse[0][1] = attend(0, (0, 1))
        if i == layers - 1:
            g_got = lay.to_core(tie(out_grad, att[0][0]), lay.same)
        if i == 0:
            late = lay.to_upper(tie(late, first))
            first = Gather(run, lay, tie(first, att[0][0]))
            first.next()
            first.got = tie(first.got, late)
            own = first.all()
            other = lay.to_core(own)
            late = Gather(run, lay, tie(late, own))
            following = lay.to_upper(tie(following, late.value))
            f_w = unpack(run, lay, at, own, other, widths[:3])
            q[1], kvm[1], kvo[1] = project(i, 1, f_w, 0)
            run.scale = 1.0
        for a in both:
            att[1][a], lse[1][a] = attend(1, (a,))
            (mine[a],) = run(0.9, make_out(i), [part_b], att[0][a], att[1][a], native[2], f_w[2])
            got[a] = lay.to_lower(mine[a])
            if i == 0 and a == 0:
                late.next()
        middle, n2, hid, slope, part, got2 = ([None] * 2 for _ in range(6))

        def norm_middle(a):
            middle[a], n2[a] = run(
                0.8, make_norm(i, i), [part_f, part_b], h_rows[a], mine[a], got[a], out_bias, norm2_gain, norm2_bias
            )

        if i == 0:
            norm_middle(0)
            own = late.all()
            other = lay.to_core(own)
            norm_middle(1)
            f_w = fetched[0] = [*f_w, *unpack(run, lay, at, own, other, widths[3:])]
        for a in both:
            if i:
                norm_middle(a)
            hid[a], slope[a], part[a] = run(
                2.9,
                make_mlp(i),
                [part_u, part_u, part_b],
                n2[a],
                native[3],
                f_w[3],
                b_up[0],
                b_up[1],
                native[4],
                f_w[4],
            )
            if i + 1 < layers:
                got2[a] = lay.to_lower(part[a])
                if a == 0:
                    following = Gather(run, lay, tie(following, part[0]))
        kept.append((h_rows, n1, q, kvm, kvo, att, lse, middle, n2, hid, slope))
        if i + 1 < layers:
            following.next()
            h_rows, n1 = [None] * 2, [None] * 2
            for a in both:
                h_rows[a], n1[a] = run(
                    0.8,
                    make_norm(i, i + 1),
                    [part_f, part_b],
                    middle[a],
                    part[a],
                    got2[a],
                    down_bias,
                    norm1_gain,
                    norm1_bias,
                )
            own = following.all()
            other = lay.to_core(own)
    *g, = run(1.5, grad_kernel, [part_f] * 2 + [part_b] * 2 + [sums_f] * 2, at, by_half(out_grad), by_half(g_got))
    g, low, sums = g[:2], g[2:4], g[4:]

    extra = 16 * max(lay.pairs, 4)
    done = {}

    def back_mlp(i):
        for a in both:
            gb[a], mine[a] = run(
                2.0, make_mlp_back(i), [part_u, part_b], low[a], native[4], f_w[4], slope[a], native[3], f_w[3]
            )
            got[a] = lay.to_lower(mine[a])

    def mlp_grads():
        size = units + d + extra
        keep, sent = run(4.2, mlp_grad_kernel, [shape((size, d))] * 2, at, *hid, *low, *n2, *gb)
        return keep, lay.to_core(sent)

    def back_norm(i, a, x, gain):
        return run(1.4, make_norm_back(i), [part_f, part_b, sums_f], g[a], mine[a], got[a], x[a], gain)

    def back_attn(i, s):
        w, j = (native, i) if s == 0 else (f_w, 0)
        dq[s], dkvm[s], dkvo[s] = run(
            SHORT,
            make_attn_back(width, half, j),
            [rows_q, rows_kv, rows_kv],
            *gml,
            w[2],
            q[s],
            kvm[s],
            kvo[s],
            *att[s],
            *lse[s],
            idc,
            idr,
            scratch=[
                pltpu.VMEM((half, width), NARROW),
                pltpu.VMEM((width, half), WIDE),
                pltpu.VMEM((8, half), WIDE),
                pltpu.VMEM((8, half), WIDE),
            ],
        )
        dkvr[s] = lay.to_core(dkvo[s])

    def join(i, a):
        dqs[a], dkvs[a], atts[a], mine[a] = run(
            1.7,
            make_attn_join(a, i),
            [shape((2, chunk, width)), shape((2, chunk, 2 * width)), shape((2, chunk, width)), part_b],
            dq[0],
            dkvm[0],
            dkvr[0],
            att[0][a],
            dq[1],
            dkvm[1],
            dkvr[1],
            att[1][a],
            native[0],
            native[1],
            f_w[0],
            f_w[1],
        )

    def attn_grads():
        size = 4 * width + extra
        keep, sent = run(2.5, attn_grad_kernel, [shape((size, d))] * 2, at, *dqs, *dkvs, *atts, *n1, *gml)
        return keep, lay.to_core(sent)

    i = layers - 1
    h_rows, n1, q, kvm, kvo, att, lse, middle, n2, hid, slope = kept[i]
    f_w = fetched[i]
    gb, mine, got, gm, gml, dq, dkvm, dkvo, dkvr, dqs, dkvs, atts = ([None] * 2 for _ in range(12))
    back_mlp(i)
    mlp1 = mlp_grads()
    vectors = [*sums]
    for a in both:
        gm[a], gml[a], sums[a] = back_norm(i, a, middle, norm2_gain)
        if a == 0:
            (sent,) = run(0.4, pick_kernel, [part_b], at, *part)
            last_got = lay.to_lower(sent)
    vectors += sums
    back_attn(i, 0)
    (rows,) = run(0.5, make_last_rows(i), [part_b], at, *middle, *part, last_got, down_bias)
    rows_got = lay.to_core(rows)
    mlp1 = Scatter(run, lay, at, *mlp1)
    back_attn(i, 1)
    act = both_halves(run, at, rows, rows_got)
    for a in both:
        join(i, a)
        got[a] = lay.to_lower(mine[a])
    attn1 = attn_grads()
    g, new_g, low, sums = gm, [None] * 2, [None] * 2, [None] * 2
    for a in both:
        new_g[a], low[a], sums[a] = back_norm(i, a, h_rows, norm1_gain)
        if a == 0:
            mlp1.next()
    g = new_g
    vectors += sums

    i = 0
    h_rows, n1, q, kvm, kvo, att, lse, middle, n2, hid, slope = kept[i]
    f_w = fetched[i]
    gb, mine, got, gm, gml, dq, dkvm, dkvo, dkvr, dqs, dkvs, atts = ([None] * 2 for _ in range(12))
    back_mlp(i)
    mlp1.across()
    attn1 = Scatter(run, lay, at, *attn1)
    mlp0 = mlp_grads()
    sums = [None] * 2
    for a in both:
        gm[a], gml[a], sums[a] = back_norm(i, a, middle, norm2_gain)
    vectors += sums
    act_near, act_far = to_holders(lay, tie(act, gml[1]))
    mlp0 = Scatter(run, lay, at, *mlp0)
    attn1.next()
    mlp1.to_core()
    back_attn(i, 0)
    attn1.across()
    mlp1 = mlp1.gather(at)
    back_attn(i, 1)
    attn1.to_core()
    mlp0.next()
    mlp1.next()
    act_far_got = lay.to_lower(tie(act_far, mlp1.value), lay.cross)
    for a in both:
        join(i, a)
    (sent,) = run(0.4, pick_kernel, [part_b], at, *mine)
    got = lay.to_lower(sent)
    attn1 = attn1.gather(at)
    attn0 = attn_grads()
    attn1.next()
    mlp0.across()
    tok, last = run(1.4, last_back_kernel, [part_b, sums_f], at, *gm, *mine, got, *h_rows, mask, norm1_gain)
    tok_got = lay.to_core(tok)
    (last,) = run(0.4, vector_kernel, [shape((16, d), WIDE)], at, *vectors, last)
    small = lay.to_core(last)
    attn0 = Scatter(run, lay, at, *attn0)
    activations = whole_rows(run, at, act, act_near, act_far, act_far_got)
    tok = both_halves(run, at, tok, tok_got)
    tok_near, tok_far = to_holders(lay, tok)
    last = total(run, last, small)

    def flip(step):
        return lay.send(last, lay.everyone, lambda k, c, h, l: (k ^ (1 << step), c, h, l))

    small = flip(0)
    mlp0.to_core()
    mlp1 = mlp1.ordered(at)
    last = total(run, last, small)
    small = flip(1)
    attn0.next()
    mlp0 = mlp0.gather(at)
    last = total(run, last, small)
    for step in range(2, lay.pairs.bit_length() - 1):
        last = total(run, last, flip(step))
    small = lay.to_upper(last)
    attn0.across()
    mlp0.next()
    last = total(run, last, small)
    small = lay.to_lower(last)
    attn0.to_core()
    tok_far_got = lay.to_lower(tok_far, lay.cross)
    attn0 = attn0.gather(at)
    mlp0 = mlp0.ordered(at)
    attn1 = attn1.ordered(at)
    mlp = [mlp0, mlp1]
    d_mlp = [jnp.stack([x[a:b] for x in mlp]).astype(WIDE) for a, b in ((0, units), (units, units + d))]
    attn0.got = tie(attn0.got, *d_mlp)
    attn0.next()
    tokens_grad = whole_rows(run, at, tok, tok_near, tok_far, tok_far_got)
    last = total(run, last, small)
    attn0 = attn0.ordered(at)

    attn = [attn0, attn1]
    stack = lambda packs, a, b: jnp.stack([x[a:b] for x in packs]).astype(WIDE)
    d_qkv = jnp.stack([jnp.transpose(x[: 3 * width]) for x in attn]).astype(WIDE)
    def by_layer(row1, row0):
        return jnp.concatenate([last[row0 : row0 + 1], last[row1 : row1 + 1]], axis=0)

    return (
        activations,
        tokens_grad,
        last[12],
        by_layer(4, 10),
        by_layer(5, 11),
        d_qkv.reshape(layers, d, 3, width),
        stack(attn, 4 * width, 4 * width + 2)[:, :, :width],
        stack(attn, 3 * width, 4 * width),
        by_layer(3, 9),
        by_layer(1, 7),
        by_layer(2, 8),
        d_mlp[1],
        stack(mlp, units + d, units + d + 1)[:, 0, :units],
        d_mlp[0],
        by_layer(0, 6),
    )


def solution(mesh):
    lay = Layout(mesh)
    placed = (
        P("dp", None),
        P("dp"),
        P("dp"),
        P(),
        P(),
        P(),
        P(None, None, None, "tensor"),
        P(None, None, "tensor"),
        P(None, "tensor", None),
        P(),
        P(),
        P(),
        P(None, None, "tensor"),
        P(None, "tensor"),
        P(None, "tensor", None),
        P(),
        P("dp", None),
    )
    return jax.shard_map(
        partial(body, lay),
        mesh=mesh,
        in_specs=placed,
        out_specs=(
            P("dp", None),
            P("dp", None),
            P(),
            P(),
            P(),
            P(None, None, None, "tensor"),
            P(None, None, "tensor"),
            P(None, "tensor", None),
            P(),
            P(),
            P(),
            P(None, None, "tensor"),
            P(None, "tensor"),
            P(None, "tensor", None),
            P(),
        ),
        check_vma=False,
    )
```

```python
from functools import partial

import jax
import jax.numpy as jnp
from jax import lax
from jax.experimental import pallas as pl
from jax.experimental.pallas import tpu as pltpu
from jax.sharding import PartitionSpec as P

AXES = ("dp", "tensor")
VMEM_LIMIT = 12 * 2**20
COST = 1.0e10
EARLY = 0.001
SHORT = 0.001
HD = 64
WIDE = jnp.float32
NARROW = jnp.bfloat16
EPSILON = 1e-06
MASKED = -1e30
NN = ((1,), (0,))
NT = ((1,), (1,))
TN = ((0,), (0,))


def dot(a, b, dims=NN):
    return lax.dot_general(a, b, (dims, ((), ())), preferred_element_type=WIDE)


class Clock:
    def __init__(self):
        self.last = None
        self.scale = 1.0

    def __call__(self, us, kernel, outs, *args, scratch=()):
        outs = call(us * self.scale, kernel, outs, self.after(args[0]), *args[1:], scratch=scratch)
        self.last = outs[-1]
        return outs

    def after(self, value):
        return value if self.last is None else lax.optimization_barrier((value, self.last))[0]


def call(us, kernel, outs, *args, scratch=()):
    return pl.pallas_call(
        kernel,
        out_shape=outs,
        in_specs=[pl.BlockSpec(memory_space=pltpu.SMEM if x.ndim == 1 else pltpu.VMEM) for x in args],
        out_specs=[pl.BlockSpec(memory_space=pltpu.VMEM)] * len(outs),
        scratch_shapes=list(scratch),
        compiler_params=pltpu.CompilerParams(vmem_limit_bytes=VMEM_LIMIT),
        cost_estimate=pl.CostEstimate(flops=int(us * COST), bytes_accessed=int(us * COST // 300), transcendentals=0),
    )(*args)


def shape(s, kind=NARROW):
    return jax.ShapeDtypeStruct(s, kind)


def first_kernel(at_ref, own_ref, got_ref, ids_ref, ids_got_ref, fill_ref, gain_ref, shift_ref,
                 ha_ref, hb_ref, na_ref, nb_ref, idr_ref, idc_ref, mask_ref):
    core, near = at_ref[1], at_ref[4] == 1
    half = own_ref.shape[1]
    both = jnp.where(near, ids_ref[...], ids_got_ref[...]).astype(WIDE)
    swapped = jnp.concatenate([both[:, half:], both[:, :half]], axis=1)
    both = jnp.where(core == 0, both, swapped)
    idr_ref[...] = both
    column = jnp.transpose(jnp.concatenate([both, jnp.zeros((6, 2 * half), WIDE)], axis=0))
    idc_ref[...] = column
    mask_ref[...] = column[:half, 1:2] + jnp.zeros((half, 8), WIDE)
    chunk = ha_ref.shape[0]
    for h_ref, n_ref, at in ((ha_ref, na_ref, 0), (hb_ref, nb_ref, chunk)):
        for r in range(0, chunk, 128):
            rows = slice(at + r, at + r + 128)
            x = jnp.where(near, own_ref[core, rows, :].astype(WIDE), got_ref[core, rows, :].astype(WIDE))
            h = jnp.where(mask_ref[rows, 0:1] == 1.0, fill_ref[...], x)
            h_ref[r : r + 128, :] = h
            centre, inv = stats(h)
            n_ref[r : r + 128, :] = (centre * inv * gain_ref[0:1, :] + shift_ref[0:1, :]).astype(NARROW)


def grad_kernel(at_ref, own_ref, got_ref, ga_ref, gb_ref, la_ref, lb_ref, sa_ref, sb_ref):
    core, near = at_ref[1], at_ref[4] == 1
    chunk, d = ga_ref.shape
    zero = jnp.zeros((1, d), WIDE)
    for g_ref, l_ref, s_ref, at in ((ga_ref, la_ref, sa_ref, 0), (gb_ref, lb_ref, sb_ref, chunk)):
        total = jnp.zeros((8, d), WIDE)
        for r in range(0, chunk, 64):
            rows = slice(at + r, at + r + 64)
            g = jnp.where(near, own_ref[core, rows, :], got_ref[core, rows, :])
            g_ref[r : r + 64, :] = g
            l_ref[r : r + 64, :] = g.astype(NARROW)
            total += fold(g)
        total = jnp.sum(total, axis=0, keepdims=True)
        s_ref[...] = jnp.concatenate([zero, zero, total, jnp.zeros((5, d), WIDE)], axis=0)


def stats(x):
    mean = jnp.mean(x, axis=-1, keepdims=True)
    centre = x - mean
    spread = jnp.mean(centre * centre, axis=-1, keepdims=True)
    return centre, lax.rsqrt(spread + EPSILON)


def fold(x):
    return jnp.sum(x.reshape(x.shape[0] // 8, 8, x.shape[1]), axis=0)


def make_norm(i, j):
    def kernel(x_ref, a_ref, b_ref, bias_ref, gain_ref, shift_ref, h_ref, n_ref):
        for r in range(0, x_ref.shape[0], 128):
            rows = slice(r, r + 128)
            h = x_ref[rows, :] + (a_ref[rows, :].astype(WIDE) + b_ref[rows, :].astype(WIDE)) + bias_ref[i : i + 1, :]
            h_ref[rows, :] = h
            centre, inv = stats(h)
            n_ref[rows, :] = (centre * inv * gain_ref[j : j + 1, :] + shift_ref[j : j + 1, :]).astype(NARROW)

    return kernel


def make_last_rows(i):
    def kernel(at_ref, xa_ref, xb_ref, pa_ref, pb_ref, got_ref, bias_ref, out_ref):
        lower = at_ref[3] == 0
        x = jnp.where(lower, xa_ref[...], xb_ref[...])
        p = jnp.where(lower, pa_ref[...].astype(WIDE), pb_ref[...].astype(WIDE))
        out_ref[...] = (x + (p + got_ref[...].astype(WIDE)) + bias_ref[i : i + 1, :]).astype(NARROW)

    return kernel


def pick_kernel(at_ref, a_ref, b_ref, out_ref):
    out_ref[...] = jnp.where(at_ref[3] == 0, b_ref[...].astype(WIDE), a_ref[...].astype(WIDE)).astype(NARROW)


def norm_back(rows, gn, x, g, gain):
    centre, inv = stats(x)
    xhat = centre * inv
    e = gn * gain
    mean_e = jnp.mean(e, axis=-1, keepdims=True)
    mean_ex = jnp.mean(e * xhat, axis=-1, keepdims=True)
    return g + inv * (e - mean_e - xhat * mean_ex), gn * xhat


def put_sums(sums_ref, sums):
    d = sums_ref.shape[1]
    sums = [jnp.sum(x, axis=0, keepdims=True) for x in sums]
    sums_ref[...] = jnp.concatenate(sums + [jnp.zeros((8 - len(sums), d), WIDE)], axis=0)


def make_norm_back(i):
    def kernel(g_ref, a_ref, b_ref, x_ref, gain_ref, out_ref, low_ref, sums_ref):
        chunk, d = x_ref.shape
        sums = [jnp.zeros((8, d), WIDE)] * 3
        for r in range(0, chunk, 64):
            rows = slice(r, r + 64)
            gn = a_ref[rows, :].astype(WIDE) + b_ref[rows, :].astype(WIDE)
            out, scaled = norm_back(rows, gn, x_ref[rows, :], g_ref[rows, :], gain_ref[i : i + 1, :])
            out_ref[rows, :] = out
            low_ref[rows, :] = out.astype(NARROW)
            sums = [s + fold(y) for s, y in zip(sums, (scaled, gn, out))]
        put_sums(sums_ref, sums)

    return kernel


def last_back_kernel(at_ref, ga_ref, gb_ref, pa_ref, pb_ref, got_ref, xa_ref, xb_ref, mask_ref, gain_ref, low_ref, sums_ref):
    lower = at_ref[3]
    first = lower == 0
    chunk, d = xa_ref.shape
    sums = [jnp.zeros((8, d), WIDE)] * 3
    pick = lambda a, b, rows: jnp.where(first, a[rows, :].astype(WIDE), b[rows, :].astype(WIDE))
    for r in range(0, chunk, 64):
        rows = slice(r, r + 64)
        gn = pick(pa_ref, pb_ref, rows) + got_ref[rows, :].astype(WIDE)
        out, scaled = norm_back(
            rows, gn, pick(xa_ref, xb_ref, rows), pick(ga_ref, gb_ref, rows), gain_ref[0:1, :]
        )
        masked = mask_ref[pl.ds(pl.multiple_of(lower * chunk, chunk) + r, 64), 0:1] == 1.0
        low_ref[rows, :] = jnp.where(masked, 0.0, out).astype(NARROW)
        sums = [s + fold(y) for s, y in zip(sums, (scaled, gn, jnp.where(masked, out, 0.0)))]
    put_sums(sums_ref, sums)


def make_qkv(i, j):
    def kernel(na_ref, nb_ref, wq_ref, wkv_ref, b_ref, q_ref, kv_ref):
        chunk = na_ref.shape[0]
        width = wq_ref.shape[2]
        zero = jnp.zeros((1, width), WIDE)
        for n_ref, at in ((na_ref, 0), (nb_ref, chunk)):
            rows = slice(at, at + chunk)
            n = n_ref[...]
            q_ref[rows, :] = (dot(n, wq_ref[j]) + b_ref[2 * i : 2 * i + 1, :]).astype(NARROW)
            bias = jnp.concatenate([zero, b_ref[2 * i + 1 : 2 * i + 2, :]], axis=1)
            kv_ref[rows, :] = (dot(n, wkv_ref[j]) + bias).astype(NARROW)

    return kernel


def make_attn(width, chunk, chunks):
    heads = width // HD

    def kernel(q_ref, kvm_ref, kvo_ref, idc_ref, idr_ref, *refs):
        half = q_ref.shape[0]
        for n, number in enumerate(chunks):
            att_ref, lse_ref = refs[2 * n : 2 * n + 2]
            rows = slice(number * chunk, number * chunk + chunk)
            idr = idr_ref[0:1, rows]
            bias = [jnp.where(idc_ref[x : x + half, 0:1] == idr, 0.0, MASKED) for x in (0, half)]
            outs, lses = [], []
            for head in range(heads):
                cols = slice(head * HD, head * HD + HD)
                late = slice(width + head * HD, width + head * HD + HD)
                q = q_ref[rows, cols] * jnp.asarray(HD**-0.5, NARROW)
                s = [dot(ref[:, cols], q, NT) + b for ref, b in zip((kvm_ref, kvo_ref), bias)]
                top = jnp.max(jnp.maximum(s[0], s[1]), axis=0, keepdims=True)
                e = [jnp.exp(x - top) for x in s]
                total = jnp.sum(e[0] + e[1], axis=0, keepdims=True)
                o = dot(kvm_ref[:, late], e[0].astype(NARROW), TN)
                o = o + dot(kvo_ref[:, late], e[1].astype(NARROW), TN)
                outs.append(o * (1.0 / total))
                lses.append(top + jnp.log(total))
            att_ref[...] = jnp.transpose(jnp.concatenate(outs, axis=0)).astype(NARROW)
            lse_ref[0:heads, :] = jnp.concatenate(lses, axis=0)

    return kernel


def make_out(i):
    def kernel(a_ref, b_ref, wa_ref, wb_ref, part_ref):
        part_ref[...] = (dot(a_ref[...], wa_ref[i], NT) + dot(b_ref[...], wb_ref[0], NT)).astype(NARROW)

    return kernel


ERF = (0.254829592, -0.284496736, 1.421413741, -1.453152027, 1.061405429)


def gelu_and_slope(x):
    bell = jnp.exp(x * x * -0.5)
    t = 1.0 / (1.0 + (0.3275911 * 0.7071067811865476) * jnp.abs(x))
    tail = t * (ERF[0] + t * (ERF[1] + t * (ERF[2] + t * (ERF[3] + t * ERF[4]))))
    tail = 0.5 * (tail * bell)
    phi = jnp.where(x < 0.0, tail, 1.0 - tail)
    return x * phi, phi + x * (0.3989422804014327 * bell)


def make_mlp(i):
    def kernel(n_ref, up_a_ref, up_b_ref, bias_a_ref, bias_b_ref, down_a_ref, down_b_ref, hid_ref, slope_ref, part_ref):
        y = None
        for slot, j, up_ref, bias_ref, down_ref in (
            (0, i, up_a_ref, bias_a_ref, down_a_ref),
            (1, 0, up_b_ref, bias_b_ref, down_b_ref),
        ):
            for f in range(0, up_ref.shape[2], 256):
                cols = slice(f, f + 256)
                x = dot(n_ref[...], up_ref[j, :, cols]) + bias_ref[i : i + 1, cols]
                hid, slope = gelu_and_slope(x)
                hid_ref[slot, :, cols] = hid.astype(NARROW)
                slope_ref[slot, :, cols] = slope.astype(NARROW)
            z = dot(hid_ref[slot], down_ref[j])
            y = z if y is None else y + z
        part_ref[...] = y.astype(NARROW)

    return kernel


def make_mlp_back(i):
    def kernel(g_ref, down_a_ref, down_b_ref, slope_ref, up_a_ref, up_b_ref, gb_ref, part_ref):
        y = None
        for slot, j, down_ref, up_ref in ((0, i, down_a_ref, up_a_ref), (1, 0, down_b_ref, up_b_ref)):
            dh = dot(g_ref[...], down_ref[j], NT)
            gb = (dh * slope_ref[slot].astype(WIDE)).astype(NARROW)
            gb_ref[slot] = gb
            z = dot(gb, up_ref[j], NT)
            y = z if y is None else y + z
        part_ref[...] = y.astype(NARROW)

    return kernel


def row_sum(x):
    return jnp.sum(fold(x.astype(WIDE)), axis=0, keepdims=True)


def wide_row(x, d):
    return x if x.shape[1] == d else jnp.concatenate([x, jnp.zeros((1, d - x.shape[1]), WIDE)], axis=1)


def put_rows(out_ref, at, rows):
    d = out_ref.shape[1]
    rows = [wide_row(r, d) for r in rows]
    out_ref[at : at + 16, :] = jnp.concatenate(rows + [jnp.zeros((16 - len(rows), d), WIDE)], axis=0).astype(NARROW)
    if out_ref.shape[0] > at + 16:
        out_ref[at + 16 :, :] = jnp.zeros((out_ref.shape[0] - at - 16, d), NARROW)


def mlp_grad_kernel(core_ref, *refs):
    *refs, keep_ref, send_ref = refs
    hid, gl, n, gb = (refs[2 * i : 2 * i + 2] for i in range(4))
    units = hid[0].shape[2]
    d = n[0].shape[1]
    for out_ref, slot in ((send_ref, 1 - core_ref[1]), (keep_ref, core_ref[1])):
        for f in range(0, units, 256):
            y = sum(dot(x[slot, :, f : f + 256], y[...], TN) for x, y in zip(hid, gl))
            out_ref[f : f + 256, :] = y.astype(NARROW)
        for f in range(0, d, 256):
            y = sum(dot(x[:, f : f + 256], y[slot], TN) for x, y in zip(n, gb))
            out_ref[units + f : units + f + 256, :] = y.astype(NARROW)
        put_rows(out_ref, units + d, [sum(row_sum(x[slot]) for x in gb)])


def make_attn_back(width, block, i):
    heads = width // HD

    def kernel(ga_in, gb_in, w_ref, q_ref, kvm_ref, kvo_ref, atta_ref, attb_ref, lsea_ref, lseb_ref, idc_ref, idr_ref,
               dq_ref, dkvm_ref, dkvo_ref, ga_ref, dqt_ref, dd_ref, lse_ref):
        half = q_ref.shape[0]
        at = 0
        for g_in, att_ref, l_ref in ((ga_in, atta_ref, lsea_ref), (gb_in, attb_ref, lseb_ref)):
            size = g_in.shape[0]
            rows = slice(at, at + size)
            ga = dot(g_in[...], w_ref[i]).astype(NARROW)
            ga_ref[rows, :] = ga
            x = ga.astype(WIDE) * att_ref[...].astype(WIDE)
            per = [jnp.sum(x[:, HD * i : HD * i + HD], axis=1, keepdims=True) for i in range(heads)]
            per = jnp.concatenate(per + [jnp.zeros((size, 128 - heads), WIDE)], axis=1)
            dd_ref[:, rows] = jnp.transpose(per)[0:8]
            lse_ref[:, rows] = l_ref[...]
            at += size
        for kv_ref, d_ref, base in ((kvo_ref, dkvo_ref, half), (kvm_ref, dkvm_ref, 0)):
            for at in range(0, half, block):
                keys = slice(at, at + block)
                bias = jnp.where(idc_ref[base + at : base + at + block, 0:1] == idr_ref[0:1, :half], 0.0, MASKED)
                dks, dvs = [], []
                for head in range(heads):
                    cols = slice(head * HD, head * HD + HD)
                    late = slice(width + head * HD, width + head * HD + HD)
                    q = q_ref[:, cols]
                    ga = ga_ref[:, cols]
                    v = kv_ref[keys, late]
                    scaled = kv_ref[keys, cols] * jnp.asarray(HD**-0.5, NARROW)
                    p = jnp.exp(dot(scaled, q, NT) + bias - lse_ref[head : head + 1, :])
                    dvs.append(dot(p.astype(NARROW), ga))
                    ds = (p * (dot(v, ga, NT) - dd_ref[head : head + 1, :])).astype(NARROW)
                    dks.append(dot(ds, q) * HD**-0.5)
                    y = dot(scaled, ds, TN)
                    if base and not at:
                        dqt_ref[cols, :] = y
                    else:
                        dqt_ref[cols, :] += y
                d_ref[keys, :] = jnp.concatenate(dks + dvs, axis=1).astype(NARROW)
        dq_ref[...] = jnp.transpose(dqt_ref[...]).astype(NARROW)

    return kernel


def make_attn_join(number, i):
    def kernel(dqa_ref, dkva_ref, ra_ref, atta_ref, dqb_ref, dkvb_ref, rb_ref, attb_ref,
               wqa_ref, wkva_ref, wqb_ref, wkvb_ref, dq_ref, dkv_ref, att_ref, part_ref):
        size = part_ref.shape[0]
        rows = slice(number * size, number * size + size)
        y = None
        for slot, j, dq1_ref, own_ref, got_ref, a_ref, wq_ref, wkv_ref in (
            (0, i, dqa_ref, dkva_ref, ra_ref, atta_ref, wqa_ref, wkva_ref),
            (1, 0, dqb_ref, dkvb_ref, rb_ref, attb_ref, wqb_ref, wkvb_ref),
        ):
            dq = dq1_ref[rows, :]
            dq_ref[slot] = dq
            att_ref[slot] = a_ref[...]
            dkv = (own_ref[rows, :].astype(WIDE) + got_ref[rows, :].astype(WIDE)).astype(NARROW)
            dkv_ref[slot] = dkv
            z = dot(dq, wq_ref[j], NT) + dot(dkv, wkv_ref[j], NT)
            y = z if y is None else y + z
        part_ref[...] = y.astype(NARROW)

    return kernel


def attn_grad_kernel(core_ref, *refs):
    *refs, keep_ref, send_ref = refs
    dq, dkv, att, n, g = (refs[2 * i : 2 * i + 2] for i in range(5))
    width = dq[0].shape[2]
    for out_ref, slot in ((send_ref, 1 - core_ref[1]), (keep_ref, core_ref[1])):
        many = lambda x, y: sum(dot(a[slot], b[...], TN) for a, b in zip(x, y)).astype(NARROW)
        out_ref[0:width, :] = many(dq, n)
        out_ref[width : 3 * width, :] = many(dkv, n)
        out_ref[3 * width : 4 * width, :] = many(att, g)
        put_rows(
            out_ref,
            4 * width,
            [sum(row_sum(x[slot]) for x in dq), sum(row_sum(x[slot]) for x in dkv)[:, width:]],
        )


def vector_kernel(at_ref, *refs):
    *refs, last_ref, out_ref = refs
    once = jnp.where(at_ref[3] == 0, 1.0, 0.0)
    rows = [refs[0][2:3, :] + refs[1][2:3, :]]
    for a_ref, b_ref in zip(refs[2::2], refs[3::2]):
        rows.append(a_ref[0:3, :] + b_ref[0:3, :])
    rows = jnp.concatenate(rows, axis=0) * once
    last = last_ref[0:3, :]
    count = rows.shape[0] + last.shape[0]
    out_ref[...] = jnp.concatenate([rows, last, jnp.zeros((16 - count, rows.shape[1]), WIDE)], axis=0)


def pack_kernel(at_ref, *refs):
    *refs, out_ref = refs
    at = 0
    for ref in refs:
        width = ref.shape[2]
        out_ref[:, at : at + width] = ref[0]
        at += width


def pair_bits(pairs, core):
    count = pairs.bit_length() - 1
    return [(i + core) % count for i in range(count)]


def by_steps(number, pairs, core):
    return sum(((number >> i) & 1) << bit for i, bit in enumerate(pair_bits(pairs, core)))


def block_of(at_ref, pairs, number, other=0):
    core = at_ref[1] if not other else 1 - at_ref[1]
    return at_ref[0] ^ jnp.where(core == 0, by_steps(number, pairs, 0), by_steps(number, pairs, 1))


def stack_kernel(*refs):
    *refs, out_ref = refs
    at = 0
    for ref in refs:
        count = ref.shape[0]
        out_ref[at : at + count] = ref[...]
        at += count


def place_kernel(at_ref, own_ref, other_ref, *outs):
    pairs, size, _ = own_ref.shape
    for p in range(pairs):
        for ref, which in ((own_ref, 0), (other_ref, 1)):
            core = at_ref[1] if not which else 1 - at_ref[1]
            row = pl.multiple_of((2 * block_of(at_ref, pairs, p, which) + core) * size, size)
            at = 0
            for out_ref in outs:
                width = out_ref.shape[2]
                out_ref[0, pl.ds(row, size), :] = ref[p, :, at : at + width]
                at += width


def make_cut(pairs):
    def kernel(at_ref, keep_ref, got_ref, kept_ref, sent_ref):
        count, size, _ = kept_ref.shape
        for p in range(count):
            number = sum(((p >> (count.bit_length() - 2 - i)) & 1) << (i + 1) for i in range(count.bit_length() - 1))
            for ref, last in ((kept_ref, 0), (sent_ref, 1)):
                rows = pl.ds(pl.multiple_of(block_of(at_ref, pairs, number + last) * size, size), size)
                ref[p] = (keep_ref[rows, :].astype(WIDE) + got_ref[rows, :].astype(WIDE)).astype(NARROW)

    return kernel


def split_kernel(kept_ref, got_ref, out_ref, sent_ref):
    count = out_ref.shape[0]
    for p in range(count):
        out_ref[p] = (kept_ref[p].astype(WIDE) + got_ref[p].astype(WIDE)).astype(NARROW)
        sent_ref[p] = (kept_ref[count + p].astype(WIDE) + got_ref[count + p].astype(WIDE)).astype(NARROW)


def sum_kernel(*refs):
    *refs, out_ref = refs
    out_ref[...] = sum(r[...].astype(WIDE) for r in refs).astype(out_ref.dtype)


def choose_kernel(at_ref, own_ref, got_ref, out_ref):
    out_ref[...] = jnp.where(at_ref[1] == 0, own_ref[...].astype(WIDE), got_ref[...].astype(WIDE)).astype(NARROW)


def order_kernel(at_ref, own_ref, got_ref, out_ref):
    count = own_ref.shape[0]
    for p in range(count):
        out_ref[block_of(at_ref, 2 * count, p)] = own_ref[p]
        out_ref[block_of(at_ref, 2 * count, count + p)] = got_ref[p]


def pair_kernel(at_ref, own_ref, got_ref, out_ref):
    out_ref[at_ref[1]] = own_ref[...]
    out_ref[1 - at_ref[1]] = got_ref[...]


def rows_kernel(at_ref, near_ref, near_got_ref, far_ref, far_got_ref, out_ref):
    near, lower = at_ref[4] == 1, at_ref[3]
    size = near_ref.shape[1]
    pick = lambda a, b: jnp.where(near, a[0].astype(WIDE), b[0].astype(WIDE))
    out_ref[pl.ds(pl.multiple_of(lower * size, size), size), :] = pick(near_ref, far_ref)
    out_ref[pl.ds(pl.multiple_of((1 - lower) * size, size), size), :] = pick(near_got_ref, far_got_ref)


class Layout:
    def __init__(self, mesh):
        self.pairs = mesh.shape["dp"] // 2
        self.tensor = mesh.shape["tensor"]
        self.lowers = self.tensor // 2
        self.everyone = [
            (k, c, h, l)
            for k in range(self.pairs)
            for c in range(2)
            for h in range(2)
            for l in range(self.lowers)
        ]
        self.same = [a for a in self.everyone if a[1] == a[2]]
        self.cross = [a for a in self.everyone if a[1] != a[2]]
        self.core0 = [a for a in self.everyone if a[1] == 0]
        self.core1 = [a for a in self.everyone if a[1] == 1]

    def place(self, k, c, h, l):
        return (2 * k + c) * self.tensor + self.lowers * h + l

    def send(self, value, among, where):
        perm = [(self.place(*a), self.place(*where(*a))) for a in among]
        return lax.ppermute(value, AXES, perm)

    def to_core(self, value, among=None):
        return self.send(value, among or self.everyone, lambda k, c, h, l: (k, 1 - c, h, l))

    def to_lower(self, value, among=None):
        return self.send(value, among or self.everyone, lambda k, c, h, l: (k, c, h, 1 - l))

    def to_upper(self, value):
        return self.send(value, self.everyone, lambda k, c, h, l: (k, c, 1 - h, l))

    def exchange(self, value, step):
        return self.send(
            value, self.everyone, lambda k, c, h, l: (k ^ (1 << pair_bits(self.pairs, c)[step]), c, h, l)
        )


def tie(value, *others):
    return lax.optimization_barrier((value, *others))[0]


def block(value, number, count):
    size = value.shape[0] // count
    return lax.dynamic_slice_in_dim(value, number * size, size, 0)


def pack(run, lay, at, weights, i):
    size = weights[0].shape[1] // (2 * lay.pairs)
    widths = [w.shape[2] for w in weights]
    if size % 16:
        part = 2 * at[0] + at[1]
        return jnp.concatenate([block(w[i], part, 2 * lay.pairs) for w in weights], axis=1)
    spec = lambda w: pl.BlockSpec((1, size, w), lambda _, at: (i, 2 * at[0] + at[1], 0))
    run.last = pl.pallas_call(
        pack_kernel,
        grid_spec=pltpu.PrefetchScalarGridSpec(
            num_scalar_prefetch=1,
            grid=(1,),
            in_specs=[spec(w) for w in widths],
            out_specs=pl.BlockSpec((size, sum(widths)), lambda *_: (0, 0)),
        ),
        out_shape=shape((size, sum(widths))),
        compiler_params=pltpu.CompilerParams(vmem_limit_bytes=VMEM_LIMIT),
        cost_estimate=pl.CostEstimate(flops=int(run.scale * COST), bytes_accessed=int(run.scale * COST // 300), transcendentals=0),
    )(run.after(at), *weights)
    return run.last


class Gather:
    def __init__(self, run, lay, piece):
        self.run, self.lay, self.step = run, lay, 0
        self.value = piece[None]
        self.got = lay.exchange(self.value, 0)

    def next(self):
        self.step += 1
        n, *rest = self.value.shape
        (self.value,) = self.run(0.7, stack_kernel, [shape((2 * n, *rest))], self.value, self.got)
        if 1 << self.step < self.lay.pairs:
            self.got = self.lay.exchange(self.value, self.step)

    def all(self):
        while self.value.shape[0] < self.lay.pairs:
            self.next()
        return self.value

    def ordered(self, at):
        while 2 * self.value.shape[0] < self.lay.pairs:
            self.next()
        _, rows, d = self.value.shape
        (out,) = self.run(0.8, order_kernel, [shape((self.lay.pairs, rows, d))], at, self.value, self.got)
        return out.reshape(-1, d)


def unpack(run, lay, at, own, other, widths):
    size = own.shape[1]
    rows = 2 * lay.pairs * size
    if size % 16 == 0:
        return run(2.0, place_kernel, [shape((1, rows, w)) for w in widths], at, own, other)
    places = [
        (2 * block_of(at, lay.pairs, p, e) + (at[1] ^ e), x[p]) for p in range(lay.pairs) for e, x in ((0, own), (1, other))
    ]
    whole = jnp.zeros((rows, own.shape[2]), own.dtype)
    for place, part in places:
        whole = lax.dynamic_update_slice_in_dim(whole, part, place * size, 0)
    out, start = [], 0
    for w in widths:
        out.append(whole[None, :, start : start + w])
        start += w
    return out


class Scatter:
    def __init__(self, run, lay, at, keep, got):
        self.run, self.lay, self.step = run, lay, 0
        size, d = keep.shape
        parts = [shape((lay.pairs // 2, size // lay.pairs, d))] * 2
        self.kept, sent = run(1.2, make_cut(lay.pairs), parts, at, keep, got)
        self.got = lay.exchange(sent, 0)

    def next(self):
        self.step += 1
        n, *rest = self.kept.shape
        self.kept, sent = self.run(0.7, split_kernel, [shape((n // 2, *rest))] * 2, self.kept, self.got)
        self.got = self.lay.exchange(sent, self.step)

    def across(self):
        while self.kept.shape[0] > 1:
            self.next()
        self.mine = total(self.run, self.kept, self.got)
        self.got = self.lay.send(self.mine, self.lay.core1, lambda k, c, h, l: (k, 0, 1 - h, l))

    def to_core(self):
        self.mine = total(self.run, self.mine, self.got)
        self.got = self.lay.to_core(self.mine, self.lay.core0)

    def gather(self, at):
        (piece,) = self.run(0.4, choose_kernel, [shape(self.mine.shape)], at, self.mine, self.got)
        return Gather(self.run, self.lay, piece[0])


def total(run, *parts):
    return run(0.4, sum_kernel, [shape(parts[0].shape, parts[0].dtype)], *parts)[0]


def both_halves(run, at, piece, got):
    return run(0.5, pair_kernel, [shape((2, *piece.shape))], at, piece, got)[0]


def to_holders(lay, both):
    near = lay.to_lower(both, lay.same)
    far = lay.send(both, lay.same, lambda k, c, h, l: (k, c, 1 - h, l))
    return near, far


def whole_rows(run, at, near, near_got, far, far_got):
    _, size, d = near.shape
    spec = lambda: pl.BlockSpec((1, size, d), lambda i, *_: (i, 0, 0))
    run.last = pl.pallas_call(
        rows_kernel,
        grid_spec=pltpu.PrefetchScalarGridSpec(
            num_scalar_prefetch=1,
            grid=(2,),
            in_specs=[spec() for _ in range(4)],
            out_specs=pl.BlockSpec((2 * size, d), lambda i, *_: (i, 0)),
        ),
        out_shape=shape((4 * size, d), WIDE),
        compiler_params=pltpu.CompilerParams(vmem_limit_bytes=VMEM_LIMIT),
        cost_estimate=pl.CostEstimate(flops=int(2 * COST), bytes_accessed=int(2 * COST // 300), transcendentals=0),
    )(run.after(at), near, near_got, far, far_got)
    return run.last


def body(
    lay,
    tokens_in,
    patch_mask,
    image_ids,
    mask_token,
    norm1_gain,
    norm1_bias,
    qkv_weight,
    qv_bias,
    out_weight,
    out_bias,
    norm2_gain,
    norm2_bias,
    up_weight,
    up_bias,
    down_weight,
    down_bias,
    out_grad,
):
    dp, tensor = lax.axis_index("dp"), lax.axis_index("tensor")
    c, h = dp % 2, tensor // lay.lowers
    at = jnp.stack([dp // 2, c, h, tensor % lay.lowers, c == h]).astype(jnp.int32)
    layers, d, _, width = qkv_weight.shape
    units = up_weight.shape[2]
    half = tokens_in.shape[0] // 2
    chunk = half // 2
    both = range(2)
    by_half = lambda x: x.reshape(2, half, d)

    part_f = shape((chunk, d), WIDE)
    part_b = shape((chunk, d))
    part_q = shape((chunk, width))
    part_l = shape((8, chunk), WIDE)
    part_u = shape((2, chunk, units))
    sums_f = shape((8, d), WIDE)
    rows_q = shape((half, width))
    rows_kv = shape((half, 2 * width))

    run = Clock()
    run.scale = EARLY
    tok_got = lay.to_core(tokens_in, lay.same)
    ids = jnp.stack([image_ids, patch_mask])
    ids_got = lay.to_core(ids, lay.same)
    native = (
        qkv_weight[:, :, 0],
        qkv_weight[:, :, 1:].reshape(layers, d, 2 * width),
        jnp.swapaxes(out_weight, 1, 2),
        up_weight,
        down_weight,
    )
    widths = [w.shape[2] for w in native]
    qv = qv_bias.reshape(2 * layers, width)
    b_qv = [qv, lay.to_upper(qv)]
    b_up = [up_bias, lay.to_upper(up_bias)]
    late = pack(run, lay, at, native[3:], 0)
    first = lay.to_upper(pack(run, lay, at, native[:3], 0))
    following = pack(run, lay, at, native, 1)
    at = tie(at, b_qv[1], b_up[1])
    *rows, idr, idc, mask = run(
        2.5,
        first_kernel,
        [part_f, part_f, part_b, part_b, shape((2, 2 * half), WIDE), shape((2 * half, 8), WIDE), shape((half, 8), WIDE)],
        at,
        by_half(tokens_in),
        by_half(tok_got),
        ids,
        ids_got,
        mask_token[None],
        norm1_gain,
        norm1_bias,
    )
    h_rows, n1 = rows[:2], rows[2:]

    def project(i, s, w, j):
        q, kv = run(0.8, make_qkv(i, j), [rows_q, rows_kv], *n1, w[0], w[1], b_qv[s])
        return q, kv, lay.to_core(kv)

    def attend(s, chunks):
        return run(
            2.0 * len(chunks),
            make_attn(width, chunk, chunks),
            [part_q, part_l] * len(chunks),
            q[s],
            kvm[s],
            kvo[s],
            idc,
            idr,
        )

    fetched = [None] * layers
    kept = []
    for i in range(layers):
        f_w = fetched[i]
        q, kvm, kvo, mine, got = ([None] * 2 for _ in range(5))
        att, lse = ([[None] * 2 for _ in both] for _ in range(2))
        q[0], kvm[0], kvo[0] = project(i, 0, native, i)
        if i:
            f_w = fetched[i] = unpack(run, lay, at, own, other, widths)
            q[1], kvm[1], kvo[1] = project(i, 1, f_w, 0)
        att[0][0], lse[0][0], att[0][1], lse[0][1] = attend(0, (0, 1))
        if i == layers - 1:
            g_got = lay.to_core(tie(out_grad, att[0][0]), lay.same)
        if i == 0:
            late = lay.to_upper(tie(late, first))
            first = Gather(run, lay, tie(first, att[0][0]))
            first.next()
            first.got = tie(first.got, late)
            own = first.all()
            other = lay.to_core(own)
            late = Gather(run, lay, tie(late, own))
            following = lay.to_upper(tie(following, late.value))
            f_w = unpack(run, lay, at, own, other, widths[:3])
            q[1], kvm[1], kvo[1] = project(i, 1, f_w, 0)
            run.scale = 1.0
        for a in both:
            att[1][a], lse[1][a] = attend(1, (a,))
            (mine[a],) = run(0.9, make_out(i), [part_b], att[0][a], att[1][a], native[2], f_w[2])
            got[a] = lay.to_lower(mine[a])
            if i == 0 and a == 0:
                late.next()
        middle, n2, hid, slope, part, got2 = ([None] * 2 for _ in range(6))

        def norm_middle(a):
            middle[a], n2[a] = run(
                0.8, make_norm(i, i), [part_f, part_b], h_rows[a], mine[a], got[a], out_bias, norm2_gain, norm2_bias
            )

        if i == 0:
            norm_middle(0)
            own = late.all()
            other = lay.to_core(own)
            norm_middle(1)
            f_w = fetched[0] = [*f_w, *unpack(run, lay, at, own, other, widths[3:])]
        for a in both:
            if i:
                norm_middle(a)
            hid[a], slope[a], part[a] = run(
                2.9,
                make_mlp(i),
                [part_u, part_u, part_b],
                n2[a],
                native[3],
                f_w[3],
                b_up[0],
                b_up[1],
                native[4],
                f_w[4],
            )
            if i + 1 < layers:
                got2[a] = lay.to_lower(part[a])
                if a == 0:
                    following = Gather(run, lay, tie(following, part[0]))
        kept.append((h_rows, n1, q, kvm, kvo, att, lse, middle, n2, hid, slope))
        if i + 1 < layers:
            following.next()
            h_rows, n1 = [None] * 2, [None] * 2
            for a in both:
                h_rows[a], n1[a] = run(
                    0.8,
                    make_norm(i, i + 1),
                    [part_f, part_b],
                    middle[a],
                    part[a],
                    got2[a],
                    down_bias,
                    norm1_gain,
                    norm1_bias,
                )
            own = following.all()
            other = lay.to_core(own)
    *g, = run(1.5, grad_kernel, [part_f] * 2 + [part_b] * 2 + [sums_f] * 2, at, by_half(out_grad), by_half(g_got))
    g, low, sums = g[:2], g[2:4], g[4:]

    extra = 16 * max(lay.pairs, 4)
    done = {}

    def back_mlp(i):
        for a in both:
            gb[a], mine[a] = run(
                2.0, make_mlp_back(i), [part_u, part_b], low[a], native[4], f_w[4], slope[a], native[3], f_w[3]
            )
            got[a] = lay.to_lower(mine[a])

    def mlp_grads():
        size = units + d + extra
        keep, sent = run(4.2, mlp_grad_kernel, [shape((size, d))] * 2, at, *hid, *low, *n2, *gb)
        return keep, lay.to_core(sent)

    def back_norm(i, a, x, gain):
        return run(1.4, make_norm_back(i), [part_f, part_b, sums_f], g[a], mine[a], got[a], x[a], gain)

    def back_attn(i, s):
        w, j = (native, i) if s == 0 else (f_w, 0)
        dq[s], dkvm[s], dkvo[s] = run(
            SHORT,
            make_attn_back(width, half, j),
            [rows_q, rows_kv, rows_kv],
            *gml,
            w[2],
            q[s],
            kvm[s],
            kvo[s],
            *att[s],
            *lse[s],
            idc,
            idr,
            scratch=[
                pltpu.VMEM((half, width), NARROW),
                pltpu.VMEM((width, half), WIDE),
                pltpu.VMEM((8, half), WIDE),
                pltpu.VMEM((8, half), WIDE),
            ],
        )
        dkvr[s] = lay.to_core(dkvo[s])

    def join(i, a):
        dqs[a], dkvs[a], atts[a], mine[a] = run(
            1.7,
            make_attn_join(a, i),
            [shape((2, chunk, width)), shape((2, chunk, 2 * width)), shape((2, chunk, width)), part_b],
            dq[0],
            dkvm[0],
            dkvr[0],
            att[0][a],
            dq[1],
            dkvm[1],
            dkvr[1],
            att[1][a],
            native[0],
            native[1],
            f_w[0],
            f_w[1],
        )

    def attn_grads():
        size = 4 * width + extra
        keep, sent = run(2.5, attn_grad_kernel, [shape((size, d))] * 2, at, *dqs, *dkvs, *atts, *n1, *gml)
        return keep, lay.to_core(sent)

    i = layers - 1
    h_rows, n1, q, kvm, kvo, att, lse, middle, n2, hid, slope = kept[i]
    f_w = fetched[i]
    gb, mine, got, gm, gml, dq, dkvm, dkvo, dkvr, dqs, dkvs, atts = ([None] * 2 for _ in range(12))
    back_mlp(i)
    mlp1 = mlp_grads()
    vectors = [*sums]
    for a in both:
        gm[a], gml[a], sums[a] = back_norm(i, a, middle, norm2_gain)
        if a == 0:
            (sent,) = run(0.4, pick_kernel, [part_b], at, *part)
            last_got = lay.to_lower(sent)
    vectors += sums
    back_attn(i, 0)
    (rows,) = run(0.5, make_last_rows(i), [part_b], at, *middle, *part, last_got, down_bias)
    rows_got = lay.to_core(rows)
    mlp1 = Scatter(run, lay, at, *mlp1)
    back_attn(i, 1)
    act = both_halves(run, at, rows, rows_got)
    for a in both:
        join(i, a)
        got[a] = lay.to_lower(mine[a])
    attn1 = attn_grads()
    g, new_g, low, sums = gm, [None] * 2, [None] * 2, [None] * 2
    for a in both:
        new_g[a], low[a], sums[a] = back_norm(i, a, h_rows, norm1_gain)
        if a == 0:
            mlp1.next()
    g = new_g
    vectors += sums

    i = 0
    h_rows, n1, q, kvm, kvo, att, lse, middle, n2, hid, slope = kept[i]
    f_w = fetched[i]
    gb, mine, got, gm, gml, dq, dkvm, dkvo, dkvr, dqs, dkvs, atts = ([None] * 2 for _ in range(12))
    back_mlp(i)
    mlp1.across()
    attn1 = Scatter(run, lay, at, *attn1)
    mlp0 = mlp_grads()
    sums = [None] * 2
    for a in both:
        gm[a], gml[a], sums[a] = back_norm(i, a, middle, norm2_gain)
    vectors += sums
    act_near, act_far = to_holders(lay, tie(act, gml[1]))
    mlp0 = Scatter(run, lay, at, *mlp0)
    attn1.next()
    mlp1.to_core()
    back_attn(i, 0)
    attn1.across()
    mlp1 = mlp1.gather(at)
    back_attn(i, 1)
    attn1.to_core()
    mlp0.next()
    mlp1.next()
    act_far_got = lay.to_lower(tie(act_far, mlp1.value), lay.cross)
    for a in both:
        join(i, a)
    (sent,) = run(0.4, pick_kernel, [part_b], at, *mine)
    got = lay.to_lower(sent)
    attn1 = attn1.gather(at)
    attn0 = attn_grads()
    attn1.next()
    mlp0.across()
    tok, last = run(1.4, last_back_kernel, [part_b, sums_f], at, *gm, *mine, got, *h_rows, mask, norm1_gain)
    tok_got = lay.to_core(tok)
    (last,) = run(0.4, vector_kernel, [shape((16, d), WIDE)], at, *vectors, last)
    small = lay.to_core(last)
    attn0 = Scatter(run, lay, at, *attn0)
    activations = whole_rows(run, at, act, act_near, act_far, act_far_got)
    tok = both_halves(run, at, tok, tok_got)
    tok_near, tok_far = to_holders(lay, tok)
    last = total(run, last, small)

    def flip(step):
        return lay.send(last, lay.everyone, lambda k, c, h, l: (k ^ (1 << step), c, h, l))

    small = flip(0)
    mlp0.to_core()
    mlp1 = mlp1.ordered(at)
    last = total(run, last, small)
    small = flip(1)
    attn0.next()
    mlp0 = mlp0.gather(at)
    last = total(run, last, small)
    for step in range(2, lay.pairs.bit_length() - 1):
        last = total(run, last, flip(step))
    small = lay.to_upper(last)
    attn0.across()
    mlp0.next()
    last = total(run, last, small)
    small = lay.to_lower(last)
    attn0.to_core()
    tok_far_got = lay.to_lower(tok_far, lay.cross)
    attn0 = attn0.gather(at)
    mlp0 = mlp0.ordered(at)
    attn1 = attn1.ordered(at)
    mlp = [mlp0, mlp1]
    d_mlp = [jnp.stack([x[a:b] for x in mlp]).astype(WIDE) for a, b in ((0, units), (units, units + d))]
    attn0.got = tie(attn0.got, *d_mlp)
    attn0.next()
    tokens_grad = whole_rows(run, at, tok, tok_near, tok_far, tok_far_got)
    last = total(run, last, small)
    attn0 = attn0.ordered(at)

    attn = [attn0, attn1]
    stack = lambda packs, a, b: jnp.stack([x[a:b] for x in packs]).astype(WIDE)
    d_qkv = jnp.stack([jnp.transpose(x[: 3 * width]) for x in attn]).astype(WIDE)
    def by_layer(row1, row0):
        return jnp.concatenate([last[row0 : row0 + 1], last[row1 : row1 + 1]], axis=0)

    return (
        activations,
        tokens_grad,
        last[12],
        by_layer(4, 10),
        by_layer(5, 11),
        d_qkv.reshape(layers, d, 3, width),
        stack(attn, 4 * width, 4 * width + 2)[:, :, :width],
        stack(attn, 3 * width, 4 * width),
        by_layer(3, 9),
        by_layer(1, 7),
        by_layer(2, 8),
        d_mlp[1],
        stack(mlp, units + d, units + d + 1)[:, 0, :units],
        d_mlp[0],
        by_layer(0, 6),
    )


def solution(mesh):
    lay = Layout(mesh)
    placed = (
        P("dp", None),
        P("dp"),
        P("dp"),
        P(),
        P(),
        P(),
        P(None, None, None, "tensor"),
        P(None, None, "tensor"),
        P(None, "tensor", None),
        P(),
        P(),
        P(),
        P(None, None, "tensor"),
        P(None, "tensor"),
        P(None, "tensor", None),
        P(),
        P("dp", None),
    )
    return jax.shard_map(
        partial(body, lay),
        mesh=mesh,
        in_specs=placed,
        out_specs=(
            P("dp", None),
            P("dp", None),
            P(),
            P(),
            P(),
            P(None, None, None, "tensor"),
            P(None, None, "tensor"),
            P(None, "tensor", None),
            P(),
            P(),
            P(),
            P(None, None, "tensor"),
            P(None, "tensor"),
            P(None, "tensor", None),
            P(),
        ),
        check_vma=False,
    )
```
